32 devices in a mesh: rows: 8 (over z, y), feat: 4 (over x, core).
Axes of the slice: x: 2, y: 2, z: 4, core: 2. Of those that a mesh axis runs over, the one named last changes fastest.
Arguments:
- gradients: bfloat16 [4096, 128], P('rows'), may hold values from -6 to 6
- hessians: bfloat16 [4096], P('rows'), may hold values from 0.25 to 2
- bin_words: int32 [128, 4096], P('feat', 'rows'), may hold values from 0 to 4095, as said below
- children: int32 [3, 4096], P(None, 'rows'), may hold values from 0 to 1, as said below
- split_feature: int32 [14], replicated, may hold values from 0 to 255
- split_bin: int32 [14], replicated, may hold values from 0 to 62
Outputs:
- split_gain_one: float32 [128, 256], P('rows', 'feat')
- split_gain_two: float32 [256, 256], P('rows', 'feat')
- split_gain_three: float32 [512, 256], P('rows', 'feat')
- child_scores: float32 [3, 8, 2, 128], P(None, 'rows')
The draws below stay inside these ranges and needn't reach their ends.
Inputs may be any that keep to these rules, and one draw needn't show every extreme that they name: `children`: of the 512 rows of one device, at most 3 / 4, 1 / 2 and 1 / 4 of 512 lie in one node at depths 1, 2 and 3; every device reaches each of these bounds in some node. `bin_words`: word w of panel p, six bits a feature with the lowest bits first, holds the bins of the panel's features 2 w and 2 w + 1, numbered within the panel of 64 features; slots past the panel's last feature are zero. Every bin is below 64.
All inputs are finite; a program needn't handle non-finite values.
Results may differ from the reference program's by a relative error of at most 0.0003.
Values may be sent and summed in bfloat16 or wider, within the bound.
No kernel may reach another device: no remote copies, remote signals or barrier semaphores. Data moves between devices by JAX's collectives and lax.ppermute only.
A program may use at most 64 MiB of HBM per device.

```python
import math
import jax
import jax.numpy as jnp
from jax import lax

FEATURES = 256
BINS = 64
OUT = 128
LEVELS = 3
ROW_DEV = 512
ROWS_TOTAL = 4096
SPLITS = 14
N_ROWS = 8
N_FEAT = 4


def draw_bin_words(key, part):
    feat_dev = FEATURES // N_FEAT
    words_dev = (feat_dev + 1) // 2
    bin_codes = jax.random.randint(key, (N_FEAT, words_dev * 2, ROWS_TOTAL), 0, BINS, dtype=jnp.int32)
    in_panel = (jnp.arange(words_dev * 2) < feat_dev).astype(jnp.int32)
    bin_codes = bin_codes * in_panel[None, :, None]
    shifts = 6 * jnp.arange(2, dtype=jnp.int32)
    packed = jnp.sum(jnp.left_shift(bin_codes.reshape(N_FEAT, words_dev, 2, ROWS_TOTAL), shifts[None, None, :, None]), axis=2)
    return packed.reshape(N_FEAT * words_dev, ROWS_TOTAL).astype(jnp.int32)


def draw_children(key, part):
    flip_key = jax.random.fold_in(key, 11)
    order_key = jax.random.fold_in(key, 23)
    flip_bits = jax.random.randint(flip_key, (N_ROWS, 7), 0, 2, dtype=jnp.int32)
    unit_rows = ROW_DEV // 64
    leaf_table = jnp.array([1, 3, 4, 8, 4, 12, 16, 16], jnp.int32) * unit_rows
    leaf_bounds = jnp.cumsum(leaf_table)[:7]
    positions = jnp.arange(ROW_DEV, dtype=jnp.int32)
    leaf_sorted = jnp.sum((positions[:, None] >= leaf_bounds[None, :]).astype(jnp.int32), axis=1)
    row_orders = jax.vmap(lambda sub_key: jax.random.permutation(sub_key, ROW_DEV))(jax.random.split(order_key, N_ROWS))
    leaf_rows = leaf_sorted[row_orders]
    heavy_top = jnp.bitwise_and(jnp.right_shift(leaf_rows, 2), 1)
    heavy_mid = jnp.bitwise_and(jnp.right_shift(leaf_rows, 1), 1)
    heavy_low = jnp.bitwise_and(leaf_rows, 1)
    child_top = jnp.bitwise_xor(heavy_top, flip_bits[:, 0:1])
    child_mid = jnp.bitwise_xor(heavy_mid, jnp.take_along_axis(flip_bits[:, 1:3], child_top, axis=1))
    node_mid = child_top * 2 + child_mid
    child_low = jnp.bitwise_xor(heavy_low, jnp.take_along_axis(flip_bits[:, 3:7], node_mid, axis=1))
    return jnp.stack([child_top, child_mid, child_low], 0).reshape(3, N_ROWS * ROW_DEV).astype(jnp.int32)


def touch_ends(entries, stream_key, low, high):
    longest = entries.shape.index(max(entries.shape))
    spots = []
    for shift in (0, 1):
        where = [jax.random.randint(jax.random.fold_in(stream_key, axis), (), 0, length) for axis, length in enumerate(entries.shape)]
        where[longest] = (where[longest] + shift) % entries.shape[longest]
        spots.append(tuple(where))
    return entries.at[spots[0]].set(low).at[spots[1]].set(high)


def block_levels(rng, shape, cuts, smallest, top_value):
    gain, own = 1.0, jax.random.fold_in(rng, 6)
    for dim, parts in cuts:
        steps = jnp.exp(jax.random.uniform(jax.random.fold_in(own, dim), (parts,), jnp.float32, smallest / len(cuts), top_value / len(cuts)))
        gain = gain * jnp.repeat(steps, shape[dim] // parts).reshape([-1 if axis == dim else 1 for axis in range(len(shape))])
    return gain


def centred(own_key, dims, width, most, shards=(), kind=jnp.bfloat16):
    result = width * jax.random.normal(own_key, dims, jnp.float32)
    if shards:
        result = result * block_levels(own_key, dims, shards, -0.22, 0.18)
    return jnp.clip(result, -most, most).astype(kind)


def setup_inputs(seed: int = 0) -> dict:
    key_of = jax.random.split(jax.random.key(seed), 7)
    return {
        "gradients": centred(key_of[0], (ROWS_TOTAL, OUT), 1.0, 6.0, ((0, 8),)),
        "hessians": jnp.clip(jnp.exp(math.log(2.0) - 2.0794415 * jax.random.uniform(key_of[1], (ROWS_TOTAL,), jnp.float32) ** block_levels(key_of[1], (ROWS_TOTAL,), ((0, 8),), -0.2, 0.2)), 0.25, 2.0).astype(jnp.bfloat16),
        "bin_words": draw_bin_words(jax.random.fold_in(key_of[6], 71), 0),
        "children": draw_children(jax.random.fold_in(key_of[6], 71), 0),
        "split_feature": touch_ends(jax.random.randint(key_of[4], (SPLITS,), 0, FEATURES), jax.random.fold_in(key_of[4], 1), 0, FEATURES - 1).astype(jnp.int32),
        "split_bin": touch_ends(jax.random.randint(key_of[5], (SPLITS,), 0, BINS - 1), jax.random.fold_in(key_of[5], 1), 0, (BINS - 1) - 1).astype(jnp.int32),
    }


penalty = 1.0

def unpack_codes(packed, feat_count):
    shifts = 6 * jnp.arange(2, dtype=jnp.int32)
    pieces = jnp.bitwise_and(jnp.right_shift(packed[:, None, :], shifts[None, :, None]), 63)
    return pieces.reshape(-1, packed.shape[-1])[:feat_count]

def split_terms(cumulative, hess_cum):
    total_sum = cumulative[..., -1:, :]
    hess_total = hess_cum[..., -1:]
    right_sum = total_sum - cumulative
    hess_right = hess_total - hess_cum
    split_score = (lax.optimization_barrier(jnp.sum(cumulative * cumulative, -1)) / (hess_cum + penalty) + lax.optimization_barrier(jnp.sum(right_sum * right_sum, -1)) / (hess_right + penalty) - lax.optimization_barrier(jnp.sum(total_sum * total_sum, -1)) / (hess_total + penalty)) / OUT
    return (split_score, right_sum, hess_right)

def reference(gradients, hessians, bin_words, children, split_feature, split_bin):
    feat_dev = FEATURES // N_FEAT
    words_dev = bin_words.shape[0] // N_FEAT
    bin_codes = jnp.concatenate([unpack_codes(bin_words[panel_index * words_dev:(panel_index + 1) * words_dev], feat_dev) for panel_index in range(N_FEAT)], 0)
    grad_wide = gradients.astype(jnp.float32)
    hess_wide = hessians.astype(jnp.float32)
    node_ids = jnp.zeros((gradients.shape[0],), jnp.int32)
    gain_list = []
    score_list = []
    for level_index in range(LEVELS):
        node_ids = node_ids * 2 + children[level_index].astype(jnp.int32)
        node_count = 2 ** (level_index + 1)

        def one_feature(code_row):
            segment = node_ids * BINS + code_row
            return (jax.ops.segment_sum(grad_wide, segment, node_count * BINS), jax.ops.segment_sum(hess_wide, segment, node_count * BINS))
        hist_grad, hist_hess = lax.map(one_feature, bin_codes)
        hist_grad = hist_grad.reshape(FEATURES, node_count, BINS, OUT)
        hist_hess = hist_hess.reshape(FEATURES, node_count, BINS)
        cumulative = jnp.cumsum(hist_grad, axis=2)
        hess_cum = jnp.cumsum(hist_hess, axis=2)
        split_score, right_sum, hess_right = split_terms(cumulative, hess_cum)
        gain_list.append(split_score.reshape(N_FEAT, feat_dev, node_count, BINS).transpose(2, 1, 0, 3).reshape(node_count * feat_dev, N_FEAT * BINS))
        first_slot = node_count - 2
        feature_ids = split_feature[first_slot:first_slot + node_count]
        bin_ids = split_bin[first_slot:first_slot + node_count]
        node_range = jnp.arange(node_count, dtype=jnp.int32)
        left_grad = cumulative[feature_ids, node_range, bin_ids]
        left_hess = hess_cum[feature_ids, node_range, bin_ids]
        right_grad = right_sum[feature_ids, node_range, bin_ids]
        right_hess = hess_right[feature_ids, node_range, bin_ids]
        child_pair = jnp.stack([-left_grad / jnp.sqrt(left_hess + penalty)[:, None], -right_grad / jnp.sqrt(right_hess + penalty)[:, None]], 1)
        score_list.append(jnp.repeat(child_pair, N_ROWS // node_count, axis=0))
    return (gain_list[0], gain_list[1], gain_list[2], jnp.stack(score_list, 0))
```

```python
import functools

import jax
import jax.numpy as jnp
from jax import lax
from jax.experimental import pallas as pl
from jax.experimental.pallas import tpu as pltpu
from jax.sharding import PartitionSpec as P

BINS = 64
LANES = 128
TILE = 16
OUT_SPLIT = 2
penalty = 1.0
VMEM_BYTES = 32 * 2**20

bf16 = jnp.bfloat16
f32 = jnp.float32
NT = (((1,), (1,)), ((), ()))


def round_up(value, unit):
    return -(-value // unit) * unit


def whole(*_):
    return pl.BlockSpec(memory_space=pltpu.VMEM)


class Plan:
    def __init__(self, rows_axis, feat_axis, gradients, bin_words, children):
        self.devices = rows_axis
        self.row_dev, self.outs = gradients.shape
        self.words = bin_words.shape[0]
        self.feats = 2 * self.words
        self.levels = children.shape[0]
        self.leaves = 2**self.levels
        self.shares = rows_axis // OUT_SPLIT
        self.share = self.feats // self.shares
        self.outs_dev = self.outs // OUT_SPLIT
        self.pair = 2 if feat_axis % 2 == 0 else 1
        self.outs_sent = self.outs_dev // self.pair
        self.code_at = self.outs_sent
        self.misc_at = self.outs_sent + self.share
        self.sent_rows = round_up(self.misc_at + 2, 8)
        self.groups = self.share // 2
        self.gain_rows = self.levels * self.groups
        self.score_at = round_up(self.gain_rows, 8)
        self.message = self.score_at + 8
        self.top_bit = rows_axis.bit_length() - 1

    def leaf_of(self, device):
        return device >> (self.top_bit - self.levels)

    def code_row(self, feature):
        return self.code_at + feature // 2 + (feature % 2) * (self.share // 2)


def prep_kernel(plan, place, feature_ref, bin_ref, grad_ref, hess_ref, word_ref, child_ref, send_ref, score_ref, masks, turned):
    rows = plan.row_dev
    grads = grad_ref[...]
    hess = hess_ref[...].astype(f32)
    words = word_ref[...]
    low = jnp.bitwise_and(words, 63)
    high = jnp.bitwise_and(jnp.right_shift(words, 6), 63)
    codes = (low.astype(f32), high.astype(f32))
    nodes = [child_ref[0:1, :]]
    for level in range(1, plan.levels):
        nodes.append(nodes[-1] * 2 + child_ref[level : level + 1, :])

    unit = jnp.where(
        lax.broadcasted_iota(jnp.int32, (plan.outs, plan.outs), 0)
        == lax.broadcasted_iota(jnp.int32, (plan.outs, plan.outs), 1),
        1.0,
        0.0,
    ).astype(bf16)
    turned[...] = lax.dot_general(unit, grads, NT, preferred_element_type=f32)

    half = lax.rem(place[1], plan.pair)
    word_share = plan.share // 2
    misc_rows = plan.sent_rows - plan.misc_at
    at = lax.broadcasted_iota(jnp.int32, (misc_rows, rows), 0)
    misc = jnp.where(at == 0, hess, jnp.where(at == 1, nodes[-1].astype(f32), 0.0))
    for split in range(OUT_SPLIT):
        start = pl.multiple_of(split * plan.outs_dev + half * plan.outs_sent, plan.outs_sent)
        part = turned[pl.ds(start, plan.outs_sent), :]
        for share in range(plan.shares):
            span = slice(share * word_share, (share + 1) * word_share)
            send_ref[share * OUT_SPLIT + split] = jnp.concatenate(
                [part, codes[0][span], codes[1][span], misc], axis=0
            ).astype(bf16)

    masks[...] = jnp.zeros_like(masks)
    panel = place[1]
    for level in range(plan.levels):
        for node in range(2 ** (level + 1)):
            slot = 2 ** (level + 1) - 2 + node
            feature = feature_ref[slot]
            inner = feature - panel * plan.feats
            owned = jnp.logical_and(inner >= 0, inner < plan.feats)
            inner = jnp.clip(inner, 0, plan.feats - 1)
            word = word_ref[pl.ds(inner // 2, 1), :]
            code = jnp.bitwise_and(jnp.right_shift(word, 6 * lax.rem(inner, 2)), 63)
            here = jnp.where(nodes[level] == node, jnp.where(owned, 1.0, 0.0), 0.0)
            left = jnp.where(code <= bin_ref[slot], here, 0.0)
            right = here - left
            under = 2 ** (plan.levels - level - 1)
            for leaf in range(node * under, (node + 1) * under):
                masks[leaf * 8 + level : leaf * 8 + level + 1, :] = left
                at_right = leaf * 8 + plan.levels + level
                masks[at_right : at_right + 1, :] = right
    mask = masks[...]
    sums = jnp.dot(mask.astype(bf16), grads, preferred_element_type=f32)
    curv = jnp.sum(mask * hess, axis=1, keepdims=True)
    shape = (plan.leaves * 8, plan.outs)
    line = jnp.bitwise_and(lax.broadcasted_iota(jnp.int32, shape, 0), 7)
    lane = lax.broadcasted_iota(jnp.int32, shape, 1)
    spread = jnp.where(lane == line, curv, 0.0).reshape(plan.leaves, 8, plan.outs)
    spread = jnp.broadcast_to(jnp.sum(spread, axis=1, keepdims=True), spread.shape)
    score_ref[...] = jnp.where(line == 2 * plan.levels, spread.reshape(shape), sums)


def main_kernel(plan, chunk, got_ref, *refs):
    others, (score_ref, out_ref, weighted, marks, left_sums) = refs[:-5], refs[-5:]
    rows = plan.row_dev
    leaves, outs_dev = plan.leaves, plan.outs_dev
    hess_at = leaves * outs_dev
    step = min(4, plan.share)
    order = [feature for k in range(plan.groups) for feature in (k, k + plan.groups)]
    level_bins = lax.broadcasted_iota(jnp.int32, (BINS, rows), 0).astype(f32).astype(bf16)
    leaf_ids = lax.broadcasted_iota(jnp.int32, (TILE, rows), 0).astype(f32)
    zero = jnp.zeros((), bf16)
    one = jnp.ones((), bf16)

    def add_chunk(first, fresh):
        for k in range(chunk):
            source = first + k
            columns = slice(k * rows, (k + 1) * rows)
            misc = got_ref[source, plan.misc_at : plan.misc_at + 2, :].astype(f32)
            hess, node = misc[0:1], misc[1:2]
            weighted[hess_at : hess_at + TILE, columns] = jnp.where(leaf_ids == node, hess, 0.0).astype(bf16)
            node_wide = jnp.broadcast_to(node, (plan.outs_sent, rows)).astype(bf16)
            for place, ref in enumerate((got_ref, *others)):
                grads = ref[source, 0 : plan.outs_sent, :]
                for leaf in range(leaves):
                    at = leaf * outs_dev + place * plan.outs_sent
                    weighted[at : at + plan.outs_sent, columns] = jnp.where(
                        node_wide == jnp.asarray(leaf, bf16), grads, zero
                    )
        for group in range(plan.share // step):
            for k in range(chunk):
                for place, feature in enumerate(order[group * step : (group + 1) * step]):
                    row = plan.code_row(feature)
                    code = got_ref[first + k, row : row + 1, :]
                    marks[place * BINS : (place + 1) * BINS, k * rows : (k + 1) * rows] = jnp.where(
                        jnp.broadcast_to(code, (BINS, rows)) <= level_bins, one, zero
                    )
            part = lax.dot_general(weighted[...], marks[...], NT, preferred_element_type=f32)
            span = slice(group * step * BINS, (group + 1) * step * BINS)
            if fresh:
                left_sums[:, span] = part
            else:
                left_sums[:, span] += part

    add_chunk(0, True)
    count = plan.devices // chunk
    if count > 1:
        lax.fori_loop(1, count, lambda c, _: (add_chunk(c * chunk, False), 0)[1], 0)

    for group in range(plan.share // step):
        span = slice(group * step * BINS, (group + 1) * step * BINS)
        left = [left_sums[leaf * outs_dev : (leaf + 1) * outs_dev, span] for leaf in range(leaves)]
        hess = [left_sums[hess_at + leaf : hess_at + leaf + 1, span] for leaf in range(leaves)]
        for level in reversed(range(plan.levels)):
            nodes = 2 ** (level + 1)
            if level < plan.levels - 1:
                left = [left[2 * n] + left[2 * n + 1] for n in range(nodes)]
                hess = [hess[2 * n] + hess[2 * n + 1] for n in range(nodes)]
            for n in range(nodes):
                total = left[n][:, BINS - 1 : BINS]
                hess_total = hess[n][:, BINS - 1 : BINS]
                right = total - left[n]
                gain = (
                    jnp.sum(left[n] * left[n], axis=0, keepdims=True) / (hess[n] + penalty)
                    + jnp.sum(right * right, axis=0, keepdims=True) / (hess_total - hess[n] + penalty)
                    - jnp.sum(total * total, axis=0, keepdims=True) / (hess_total + penalty)
                ) / plan.outs
                under = plan.devices // nodes
                for tile in range(step // 2):
                    piece = gain[:, tile * LANES : (tile + 1) * LANES]
                    row = level * plan.groups + group * (step // 2) + tile
                    for device in range(n * under, (n + 1) * under):
                        out_ref[device, row : row + 1, :] = piece
    if plan.score_at > plan.gain_rows:
        filler = jnp.zeros((plan.score_at - plan.gain_rows, LANES), f32)
        for device in range(plan.devices):
            out_ref[device, plan.gain_rows : plan.score_at, :] = filler
    for device in range(plan.devices):
        leaf = plan.leaf_of(device)
        out_ref[device, plan.score_at : plan.score_at + 8, :] = score_ref[leaf * 8 : leaf * 8 + 8, :]


def final_kernel(plan, place, got_ref, *outs):
    *gain_refs, child_ref = outs
    half = plan.groups
    for level, gain_ref in enumerate(gain_refs):
        size = plan.devices >> (level + 1)
        position = lax.rem(place[0], size)
        count = plan.feats // size // plan.share
        for t in range(count):
            share = position * count + t
            rows = slice(level * half, (level + 1) * half)
            total = got_ref[share * OUT_SPLIT, rows, :]
            for split in range(1, OUT_SPLIT):
                total = total + got_ref[share * OUT_SPLIT + split, rows, :]
            for side in range(2):
                at = t * plan.share + side * half
                gain_ref[at : at + half, :] = total[:, side * BINS : (side + 1) * BINS]
    sums = got_ref[0, plan.score_at : plan.score_at + 8, :]
    for device in range(1, plan.devices):
        sums = sums + got_ref[device, plan.score_at : plan.score_at + 8, :]
    curv = sums[2 * plan.levels : 2 * plan.levels + 1, :]
    for level in range(plan.levels):
        for side in range(2):
            line = side * plan.levels + level
            scale = jnp.sqrt(curv[:, line : line + 1] + penalty)
            child_ref[level, 0, side : side + 1, :] = -sums[line : line + 1, :] / scale


def on_device(gradients, hessians, bin_words, children, split_feature, split_bin):
    plan = Plan(lax.axis_size("rows"), lax.axis_size("feat"), gradients, bin_words, children)
    rows = plan.row_dev
    place = jnp.stack([lax.axis_index("rows"), lax.axis_index("feat")]).astype(jnp.int32)
    params = pltpu.CompilerParams(vmem_limit_bytes=VMEM_BYTES)
    smem = pl.BlockSpec(memory_space=pltpu.SMEM)

    send, scores = pl.pallas_call(
        functools.partial(prep_kernel, plan),
        out_shape=(
            jax.ShapeDtypeStruct((plan.devices, plan.sent_rows, rows), bf16),
            jax.ShapeDtypeStruct((plan.leaves * 8, plan.outs), f32),
        ),
        in_specs=[smem, smem, smem] + [whole()] * 4,
        out_specs=(whole(), whole()),
        scratch_shapes=[
            pltpu.VMEM((plan.leaves * 8, rows), f32),
            pltpu.VMEM((plan.outs, rows), f32),
        ],
        compiler_params=params,
        name="prep",
    )(place, split_feature, split_bin, gradients, hessians.reshape(1, rows), bin_words, children)

    scores = lax.psum(scores, "feat")
    got = lax.all_to_all(send, "rows", 0, 0)
    arrays = [got]
    if plan.pair > 1:
        route = [(p, p ^ 1) for p in range(lax.axis_size("feat"))]
        arrays.append(lax.ppermute(got, "feat", route))

    chunk = max(1, min(plan.devices, 4096 // rows))
    while plan.devices % chunk:
        chunk -= 1
    sums_rows = plan.leaves * plan.outs_dev + TILE
    message = pl.pallas_call(
        functools.partial(main_kernel, plan, chunk),
        out_shape=jax.ShapeDtypeStruct((plan.devices, plan.message, LANES), f32),
        in_specs=[whole()] * (len(arrays) + 1),
        out_specs=whole(),
        scratch_shapes=[
            pltpu.VMEM((sums_rows, chunk * rows), bf16),
            pltpu.VMEM((min(4, plan.share) * BINS, chunk * rows), bf16),
            pltpu.VMEM((sums_rows, plan.share * BINS), f32),
        ],
        compiler_params=params,
        name="gains",
    )(*arrays, scores)

    answer = lax.all_to_all(message, "rows", 0, 0)
    shapes = [
        jax.ShapeDtypeStruct((plan.feats // (plan.devices >> (level + 1)), BINS), f32)
        for level in range(plan.levels)
    ]
    shapes.append(jax.ShapeDtypeStruct((plan.levels, 1, 2, plan.outs), f32))
    return pl.pallas_call(
        functools.partial(final_kernel, plan),
        out_shape=tuple(shapes),
        in_specs=[smem, whole()],
        out_specs=tuple(whole() for _ in shapes),
        compiler_params=params,
        name="finish",
    )(place, answer)


def solution(mesh):
    placed = (P("rows", None), P("rows"), P("feat", "rows"), P(None, "rows"), P(), P())
    return jax.shard_map(
        on_device,
        mesh=mesh,
        in_specs=placed,
        out_specs=(
            P("rows", "feat"),
            P("rows", "feat"),
            P("rows", "feat"),
            P(None, "rows", None, None),
        ),
        check_vma=False,
    )
```

```python
import functools

import jax
import jax.numpy as jnp
from jax import lax
from jax.experimental import pallas as pl
from jax.experimental.pallas import tpu as pltpu
from jax.sharding import PartitionSpec as P

BINS = 64
LANES = 128
TILE = 16
OUT_SPLIT = 2
PIECES = 3
penalty = 1.0
VMEM_BYTES = 32 * 2**20

bf16 = jnp.bfloat16
f32 = jnp.float32
NT = (((1,), (1,)), ((), ()))


def round_up(value, unit):
    return -(-value // unit) * unit


def whole(*_):
    return pl.BlockSpec(memory_space=pltpu.VMEM)


class Plan:
    def __init__(self, rows_axis, feat_axis, gradients, bin_words, children):
        self.devices = rows_axis
        self.row_dev, self.outs = gradients.shape
        self.words = bin_words.shape[0]
        self.feats = 2 * self.words
        self.levels = children.shape[0]
        self.leaves = 2**self.levels
        self.shares = rows_axis // OUT_SPLIT
        self.share = self.feats // self.shares
        self.outs_dev = self.outs // OUT_SPLIT
        self.pair = 2 if feat_axis % 2 == 0 else 1
        self.outs_sent = self.outs_dev // self.pair
        self.code_at = self.outs_sent
        self.misc_at = self.outs_sent + self.share
        self.score_rows = 2 * self.levels + 1
        self.spans = self.row_dev // LANES
        self.misc_rows = 2 + -(-self.score_rows * PIECES // self.spans)
        self.sent_rows = round_up(self.misc_at + self.misc_rows, 8)
        self.groups = self.share // 2
        self.gain_rows = self.levels * self.groups
        self.message = round_up(self.gain_rows, 8)
        self.top_bit = rows_axis.bit_length() - 1

    def leaf_of(self, device):
        return device >> (self.top_bit - self.levels)

    def code_row(self, feature):
        return self.code_at + feature // 2 + (feature % 2) * (self.share // 2)


def prep_kernel(plan, *refs):
    inputs, send_ref, refs = refs[:6], refs[6], refs[7:]
    fetched, (masks, turned, sems) = refs[:6], refs[6:]
    copies = [
        pltpu.make_async_copy(source, target, sems.at[i])
        for i, (source, target) in enumerate(zip(inputs, fetched, strict=True))
    ]
    for copy in copies:
        copy.start()
    for copy in copies:
        copy.wait()
    grad_ref, hess_ref, word_ref, child_ref, feature_ref, bin_ref = fetched
    rows = plan.row_dev
    grads = grad_ref[...]
    hess = hess_ref[...].astype(f32).reshape(1, rows)
    panel = lax.axis_index("feat")
    words = word_ref[...]
    low = jnp.bitwise_and(words, 63)
    high = jnp.bitwise_and(jnp.right_shift(words, 6), 63)
    codes = (low.astype(f32), high.astype(f32))
    nodes = [child_ref[0:1, :]]
    for level in range(1, plan.levels):
        nodes.append(nodes[-1] * 2 + child_ref[level : level + 1, :])

    unit = jnp.where(
        lax.broadcasted_iota(jnp.int32, (plan.outs, plan.outs), 0)
        == lax.broadcasted_iota(jnp.int32, (plan.outs, plan.outs), 1),
        1.0,
        0.0,
    ).astype(bf16)
    turned[...] = lax.dot_general(unit, grads, NT, preferred_element_type=f32)

    masks[...] = jnp.zeros_like(masks)
    for level in range(plan.levels):
        for node in range(2 ** (level + 1)):
            slot = 2 ** (level + 1) - 2 + node
            feature = feature_ref[slot]
            inner = feature - panel * plan.feats
            owned = jnp.logical_and(inner >= 0, inner < plan.feats)
            inner = jnp.clip(inner, 0, plan.feats - 1)
            word = word_ref[pl.ds(inner // 2, 1), :]
            code = jnp.bitwise_and(jnp.right_shift(word, 6 * lax.rem(inner, 2)), 63)
            here = jnp.where(nodes[level] == node, jnp.where(owned, 1.0, 0.0), 0.0)
            left = jnp.where(code <= bin_ref[slot], here, 0.0)
            right = here - left
            under = 2 ** (plan.levels - level - 1)
            for leaf in range(node * under, (node + 1) * under):
                masks[leaf * 8 + level : leaf * 8 + level + 1, :] = left
                at_right = leaf * 8 + plan.levels + level
                masks[at_right : at_right + 1, :] = right
    mask = masks[...]
    sums = jnp.dot(mask.astype(bf16), grads, preferred_element_type=f32)
    curv = jnp.sum(mask * hess, axis=1, keepdims=True)
    shape = (plan.leaves * 8, plan.outs)
    line = jnp.bitwise_and(lax.broadcasted_iota(jnp.int32, shape, 0), 7)
    lane = lax.broadcasted_iota(jnp.int32, shape, 1)
    spread = jnp.where(lane == line, curv, 0.0).reshape(plan.leaves, 8, plan.outs)
    spread = jnp.broadcast_to(jnp.sum(spread, axis=1, keepdims=True), spread.shape)
    sums = jnp.where(line == 2 * plan.levels, spread.reshape(shape), sums)
    pieces = []
    for _ in range(PIECES):
        pieces.append(sums.astype(bf16).astype(f32))
        sums = sums - pieces[-1]

    half = lax.rem(panel, plan.pair)
    word_share = plan.share // 2
    own = [hess, nodes[-1].astype(f32)]
    blank = jnp.zeros((1, LANES), f32)
    filler = jnp.zeros((plan.sent_rows - plan.misc_at - plan.misc_rows, rows), f32)
    misc = []
    for leaf in range(plan.leaves):
        parts = [piece[leaf * 8 + i : leaf * 8 + i + 1] for i in range(plan.score_rows) for piece in pieces]
        parts += [blank] * (-len(parts) % plan.spans)
        lines = [jnp.concatenate(parts[i : i + plan.spans], axis=1) for i in range(0, len(parts), plan.spans)]
        lines += [filler] if filler.shape[0] else []
        misc.append(jnp.concatenate(own + lines, axis=0))
    for split in range(OUT_SPLIT):
        start = pl.multiple_of(split * plan.outs_dev + half * plan.outs_sent, plan.outs_sent)
        part = turned[pl.ds(start, plan.outs_sent), :]
        for share in range(plan.shares):
            span = slice(share * word_share, (share + 1) * word_share)
            device = share * OUT_SPLIT + split
            send_ref[device] = jnp.concatenate(
                [part, codes[0][span], codes[1][span], misc[plan.leaf_of(device)]], axis=0
            ).astype(bf16)


def main_kernel(plan, chunk, got_ref, *refs):
    others, refs = refs[: plan.pair - 1], refs[plan.pair - 1 :]
    out_ref, score_ref, weighted, marks, left_sums = refs
    rows = plan.row_dev
    leaves, outs_dev = plan.leaves, plan.outs_dev
    hess_at = leaves * outs_dev
    step = min(4, plan.share)
    order = [feature for k in range(plan.groups) for feature in (k, k + plan.groups)]
    level_bins = lax.broadcasted_iota(jnp.int32, (BINS, rows), 0).astype(f32).astype(bf16)
    leaf_ids = lax.broadcasted_iota(jnp.int32, (TILE, rows), 0).astype(f32)
    zero = jnp.zeros((), bf16)
    one = jnp.ones((), bf16)

    def add_chunk(first, fresh):
        for k in range(chunk):
            source = first + k
            columns = slice(k * rows, (k + 1) * rows)
            misc = got_ref[source, plan.misc_at : plan.misc_at + 2, :].astype(f32)
            hess, node = misc[0:1], misc[1:2]
            weighted[hess_at : hess_at + TILE, columns] = jnp.where(leaf_ids == node, hess, 0.0).astype(bf16)
            node_wide = jnp.broadcast_to(node, (plan.outs_sent, rows)).astype(bf16)
            for place, ref in enumerate((got_ref, *others)):
                grads = ref[source, 0 : plan.outs_sent, :]
                for leaf in range(leaves):
                    at = leaf * outs_dev + place * plan.outs_sent
                    weighted[at : at + plan.outs_sent, columns] = jnp.where(
                        node_wide == jnp.asarray(leaf, bf16), grads, zero
                    )
        for group in range(plan.share // step):
            for k in range(chunk):
                for place, feature in enumerate(order[group * step : (group + 1) * step]):
                    row = plan.code_row(feature)
                    code = got_ref[first + k, row : row + 1, :]
                    marks[place * BINS : (place + 1) * BINS, k * rows : (k + 1) * rows] = jnp.where(
                        jnp.broadcast_to(code, (BINS, rows)) <= level_bins, one, zero
                    )
            part = lax.dot_general(weighted[...], marks[...], NT, preferred_element_type=f32)
            span = slice(group * step * BINS, (group + 1) * step * BINS)
            if fresh:
                left_sums[:, span] = part
            else:
                left_sums[:, span] += part

    add_chunk(0, True)
    count = plan.devices // chunk
    if count > 1:
        lax.fori_loop(1, count, lambda c, _: (add_chunk(c * chunk, False), 0)[1], 0)

    for group in range(plan.share // step):
        span = slice(group * step * BINS, (group + 1) * step * BINS)
        left = [left_sums[leaf * outs_dev : (leaf + 1) * outs_dev, span] for leaf in range(leaves)]
        hess = [left_sums[hess_at + leaf : hess_at + leaf + 1, span] for leaf in range(leaves)]
        for level in reversed(range(plan.levels)):
            nodes = 2 ** (level + 1)
            if level < plan.levels - 1:
                left = [left[2 * n] + left[2 * n + 1] for n in range(nodes)]
                hess = [hess[2 * n] + hess[2 * n + 1] for n in range(nodes)]
            for n in range(nodes):
                total = left[n][:, BINS - 1 : BINS]
                hess_total = hess[n][:, BINS - 1 : BINS]
                right = total - left[n]
                gain = (
                    jnp.sum(left[n] * left[n], axis=0, keepdims=True) / (hess[n] + penalty)
                    + jnp.sum(right * right, axis=0, keepdims=True) / (hess_total - hess[n] + penalty)
                    - jnp.sum(total * total, axis=0, keepdims=True) / (hess_total + penalty)
                ) / plan.outs
                under = plan.devices // nodes
                for tile in range(step // 2):
                    piece = gain[:, tile * LANES : (tile + 1) * LANES]
                    row = level * plan.groups + group * (step // 2) + tile
                    for device in range(n * under, (n + 1) * under):
                        out_ref[device, row : row + 1, :] = piece
    if plan.message > plan.gain_rows:
        filler = jnp.zeros((plan.message - plan.gain_rows, LANES), f32)
        for device in range(plan.devices):
            out_ref[device, plan.gain_rows : plan.message, :] = filler

    def add_scores(source, total):
        for ref in (got_ref, *others):
            total = total + ref[source, plan.misc_at + 2 : plan.misc_at + plan.misc_rows, :].astype(f32)
        return total

    total = lax.fori_loop(0, plan.devices, add_scores, jnp.zeros((plan.misc_rows - 2, rows), f32))
    score_ref[...] = jnp.zeros_like(score_ref)
    for i in range(plan.score_rows):
        value = 0.0
        for piece in reversed(range(PIECES)):
            line, span = divmod(i * PIECES + piece, plan.spans)
            value = value + total[line : line + 1, span * LANES : (span + 1) * LANES]
        score_ref[i : i + 1, :] = value


def final_kernel(plan, got_ref, *refs):
    score_refs, refs = refs[: -plan.levels - 1], refs[-plan.levels - 1 :]
    *gain_refs, child_ref = refs
    half = plan.groups
    for level, gain_ref in enumerate(gain_refs):
        size = plan.devices >> (level + 1)
        position = lax.rem(lax.axis_index("rows"), size)
        count = plan.feats // size // plan.share
        for t in range(count):
            share = position * count + t
            rows = slice(level * half, (level + 1) * half)
            total = got_ref[share * OUT_SPLIT, rows, :]
            for split in range(1, OUT_SPLIT):
                total = total + got_ref[share * OUT_SPLIT + split, rows, :]
            for side in range(2):
                at = t * plan.share + side * half
                gain_ref[at : at + half, :] = total[:, side * BINS : (side + 1) * BINS]
    sums = score_refs[0][...]
    for score_ref in score_refs[1:]:
        sums = sums + score_ref[...]
    curv = sums[2 * plan.levels : 2 * plan.levels + 1, :]
    for level in range(plan.levels):
        for side in range(2):
            line = side * plan.levels + level
            scale = jnp.sqrt(curv[:, line : line + 1] + penalty)
            child_ref[level, 0, side : side + 1, :] = -sums[line : line + 1, :] / scale


def flipped(block, bit):
    count = lax.axis_size("feat")
    return lax.ppermute(block, "feat", [(p, p ^ bit) for p in range(count)])


def on_device(gradients, hessians, bin_words, children, split_feature, split_bin):
    plan = Plan(lax.axis_size("rows"), lax.axis_size("feat"), gradients, bin_words, children)
    rows = plan.row_dev
    params = pltpu.CompilerParams(vmem_limit_bytes=VMEM_BYTES)

    inputs = (gradients, hessians, bin_words, children, split_feature, split_bin)
    inputs = tuple(pltpu.with_memory_space_constraint(a, pltpu.HBM) for a in inputs)
    send = pl.pallas_call(
        functools.partial(prep_kernel, plan),
        out_shape=jax.ShapeDtypeStruct((plan.devices, plan.sent_rows, rows), bf16),
        in_specs=[pl.BlockSpec(memory_space=pltpu.HBM)] * len(inputs),
        out_specs=whole(),
        scratch_shapes=[
            *(pltpu.VMEM(a.shape, a.dtype) for a in inputs[:4]),
            *(pltpu.SMEM(a.shape, a.dtype) for a in inputs[4:]),
            pltpu.VMEM((plan.leaves * 8, rows), f32),
            pltpu.VMEM((plan.outs, rows), f32),
            pltpu.SemaphoreType.DMA((len(inputs),)),
        ],
        compiler_params=params,
        name="prep",
    )(*inputs)

    got = lax.all_to_all(send, "rows", 0, 0)
    arrays = [got] + ([flipped(got, 1)] if plan.pair > 1 else [])

    chunk = max(1, min(plan.devices, 4096 // rows))
    while plan.devices % chunk:
        chunk -= 1
    sums_rows = plan.leaves * plan.outs_dev + TILE
    message, scores = pl.pallas_call(
        functools.partial(main_kernel, plan, chunk),
        out_shape=(
            jax.ShapeDtypeStruct((plan.devices, plan.message, LANES), f32),
            jax.ShapeDtypeStruct((8, plan.outs), f32),
        ),
        in_specs=[whole()] * len(arrays),
        out_specs=(whole(), whole()),
        scratch_shapes=[
            pltpu.VMEM((sums_rows, chunk * rows), bf16),
            pltpu.VMEM((min(4, plan.share) * BINS, chunk * rows), bf16),
            pltpu.VMEM((sums_rows, plan.share * BINS), f32),
        ],
        compiler_params=params,
        name="gains",
    )(*arrays)

    score_parts = [scores]
    for away in range(1, lax.axis_size("feat") // plan.pair):
        score_parts.append(flipped(scores, away * plan.pair))
    answer = lax.all_to_all(message, "rows", 0, 0)
    shapes = [
        jax.ShapeDtypeStruct((plan.feats // (plan.devices >> (level + 1)), BINS), f32)
        for level in range(plan.levels)
    ]
    shapes.append(jax.ShapeDtypeStruct((plan.levels, 1, 2, plan.outs), f32))
    return pl.pallas_call(
        functools.partial(final_kernel, plan),
        out_shape=tuple(shapes),
        in_specs=[whole()] * (1 + len(score_parts)),
        out_specs=tuple(whole() for _ in shapes),
        compiler_params=params,
        name="finish",
    )(answer, *score_parts)


def solution(mesh):
    placed = (P("rows", None), P("rows"), P("feat", "rows"), P(None, "rows"), P(), P())
    return jax.shard_map(
        on_device,
        mesh=mesh,
        in_specs=placed,
        out_specs=(
            P("rows", "feat"),
            P("rows", "feat"),
            P("rows", "feat"),
            P(None, "rows", None, None),
        ),
        check_vma=False,
    )
```

```python
import functools

import jax
import jax.numpy as jnp
from jax import lax
from jax.experimental import pallas as pl
from jax.experimental.pallas import tpu as pltpu
from jax.sharding import PartitionSpec as P

BINS = 64
LANES = 128
TILE = 16
OUT_SPLIT = 2
PIECES = 2
penalty = 1.0
VMEM_BYTES = 32 * 2**20

bf16 = jnp.bfloat16
f32 = jnp.float32
NT = (((1,), (1,)), ((), ()))


def round_up(value, unit):
    return -(-value // unit) * unit


def whole(*_):
    return pl.BlockSpec(memory_space=pltpu.VMEM)


class Plan:
    def __init__(self, rows_axis, feat_axis, gradients, bin_words, children):
        self.devices = rows_axis
        self.half = rows_axis // 2
        self.row_dev, self.outs = gradients.shape
        self.words = bin_words.shape[0]
        self.feats = 2 * self.words
        self.levels = children.shape[0]
        self.leaves = 2 ** (self.levels - 1)
        self.slots = round_up(self.row_dev * 3 // 4, LANES)
        self.shares = self.half // OUT_SPLIT
        self.share = self.feats // self.shares
        self.outs_dev = self.outs // OUT_SPLIT
        self.pair = 2 if feat_axis % 2 == 0 else 1
        self.outs_sent = self.outs_dev // self.pair
        self.code_at = self.outs_sent
        self.misc_at = self.outs_sent + self.share
        self.score_rows = 2 * self.levels + 1
        self.spans = self.slots // LANES
        self.misc_rows = 2 + -(-self.score_rows * PIECES // self.spans)
        self.sent_rows = round_up(self.misc_at + self.misc_rows, 8)
        self.sizes = [self.devices >> (level + 1) for level in range(self.levels)]
        self.returned = [self.feats // size for size in self.sizes]
        self.needed = [min(self.share, count) for count in self.returned]
        self.block = min(self.needed)
        self.step = min(4, self.share)
        self.tiles = [
            (start + k, start + k + self.block // 2)
            for start in range(0, self.share, self.block)
            for k in range(self.block // 2)
        ]
        self.level_at = [sum(self.needed[:level]) // 2 for level in range(self.levels)]
        self.gain_rows = sum(self.needed) // 2
        self.message = round_up(self.gain_rows, 8)

    def code_row(self, feature):
        return self.code_at + feature // 2 + (feature % 2) * (self.share // 2)


def prep_kernel(plan, *refs):
    inputs, send_ref, refs = refs[:6], refs[6], refs[7:]
    fetched, (masks, table, packed, sems) = refs[:6], refs[6:]
    copies = [
        pltpu.make_async_copy(source, target, sems.at[i])
        for i, (source, target) in enumerate(zip(inputs, fetched, strict=True))
    ]
    for copy in copies:
        copy.start()
    for copy in copies:
        copy.wait()
    grad_ref, hess_ref, word_ref, child_ref, feature_ref, bin_ref = fetched
    rows = plan.row_dev
    grads = grad_ref[...]
    hess = hess_ref[...].astype(f32).reshape(1, rows)
    panel = lax.axis_index("feat")
    words = word_ref[...]
    low = jnp.bitwise_and(words, 63)
    high = jnp.bitwise_and(jnp.right_shift(words, 6), 63)
    codes = (low.astype(f32), high.astype(f32))
    nodes = [child_ref[0:1, :]]
    for level in range(1, plan.levels):
        nodes.append(nodes[-1] * 2 + child_ref[level : level + 1, :])

    unit = jnp.where(
        lax.broadcasted_iota(jnp.int32, (plan.outs, plan.outs), 0)
        == lax.broadcasted_iota(jnp.int32, (plan.outs, plan.outs), 1),
        1.0,
        0.0,
    ).astype(bf16)
    low_at, high_at, own_at = plan.outs, plan.outs + plan.words, plan.outs + plan.feats
    table[0:low_at] = lax.dot_general(unit, grads, NT, preferred_element_type=f32).astype(bf16)
    table[low_at:high_at] = low.astype(f32).astype(bf16)
    table[high_at:own_at] = high.astype(f32).astype(bf16)
    at = lax.broadcasted_iota(jnp.int32, (TILE, rows), 0)
    leaf = jnp.bitwise_and(nodes[-1], plan.leaves - 1).astype(f32)
    table[own_at:] = jnp.where(at == 0, hess, jnp.where(at == 1, leaf, 0.0)).astype(bf16)
    side = jnp.where(at == nodes[0], 1.0, 0.0)
    ahead = jnp.where(
        lax.broadcasted_iota(jnp.int32, (rows, rows), 0) <= lax.broadcasted_iota(jnp.int32, (rows, rows), 1), 1.0, 0.0
    )
    rank = jnp.dot(side.astype(bf16), ahead.astype(bf16), preferred_element_type=f32)
    slot = jnp.where(side > 0.0, rank - 1.0, -1.0)
    slot_ids = lax.broadcasted_iota(jnp.int32, (plan.slots, rows), 0).astype(f32)
    for half in range(2):
        chosen = jnp.where(slot_ids == slot[half : half + 1], 1.0, 0.0).astype(bf16)
        packed[half] = lax.dot_general(table[...], chosen, NT, preferred_element_type=f32)

    masks[...] = jnp.zeros_like(masks)
    leaf_count = 2 * plan.leaves
    for level in range(plan.levels):
        for node in range(2 ** (level + 1)):
            slot = 2 ** (level + 1) - 2 + node
            feature = feature_ref[slot]
            inner = feature - panel * plan.feats
            owned = jnp.logical_and(inner >= 0, inner < plan.feats)
            inner = jnp.clip(inner, 0, plan.feats - 1)
            word = word_ref[pl.ds(inner // 2, 1), :]
            code = jnp.bitwise_and(jnp.right_shift(word, 6 * lax.rem(inner, 2)), 63)
            here = jnp.where(nodes[level] == node, jnp.where(owned, 1.0, 0.0), 0.0)
            left = jnp.where(code <= bin_ref[slot], here, 0.0)
            right = here - left
            under = 2 ** (plan.levels - level - 1)
            for leaf in range(node * under, (node + 1) * under):
                masks[leaf * 8 + level : leaf * 8 + level + 1, :] = left
                at_right = leaf * 8 + plan.levels + level
                masks[at_right : at_right + 1, :] = right
    mask = masks[...]
    sums = jnp.dot(mask.astype(bf16), grads, preferred_element_type=f32)
    curv = jnp.sum(mask * hess, axis=1, keepdims=True)
    shape = (leaf_count * 8, plan.outs)
    line = jnp.bitwise_and(lax.broadcasted_iota(jnp.int32, shape, 0), 7)
    lane = lax.broadcasted_iota(jnp.int32, shape, 1)
    spread = jnp.where(lane == line, curv, 0.0).reshape(leaf_count, 8, plan.outs)
    spread = jnp.broadcast_to(jnp.sum(spread, axis=1, keepdims=True), spread.shape)
    sums = jnp.where(line == 2 * plan.levels, spread.reshape(shape), sums)
    pieces = []
    for _ in range(PIECES):
        pieces.append(sums.astype(bf16).astype(f32))
        sums = sums - pieces[-1]

    parity = lax.rem(panel, plan.pair)
    word_share = plan.share // 2
    blank = jnp.zeros((1, LANES), f32)
    filler = jnp.zeros((plan.sent_rows - plan.misc_at - plan.misc_rows, plan.slots), f32)
    lines = []
    for leaf in range(leaf_count):
        parts = [piece[leaf * 8 + i : leaf * 8 + i + 1] for i in range(plan.score_rows) for piece in pieces]
        parts += [blank] * (-len(parts) % plan.spans)
        parts = [jnp.concatenate(parts[i : i + plan.spans], axis=1) for i in range(0, len(parts), plan.spans)]
        lines.append(jnp.concatenate(parts + ([filler] if filler.shape[0] else []), axis=0))
    for device in range(plan.devices):
        half, place = divmod(device, plan.half)
        share, split = divmod(place, OUT_SPLIT)
        start = pl.multiple_of(split * plan.outs_dev + parity * plan.outs_sent, plan.outs_sent)
        low_from, high_from = low_at + share * word_share, high_at + share * word_share
        send_ref[device] = jnp.concatenate(
            [
                packed[half, pl.ds(start, plan.outs_sent), :],
                packed[half, low_from : low_from + word_share, :],
                packed[half, high_from : high_from + word_share, :],
                packed[half, own_at : own_at + 2, :],
                lines[device * leaf_count // plan.devices],
            ],
            axis=0,
        ).astype(bf16)


def main_kernel(plan, chunk, got_ref, *refs):
    others, refs = refs[: plan.pair - 1], refs[plan.pair - 1 :]
    out_ref, score_ref, weighted, marks, left_sums = refs
    rows = plan.slots
    leaves, outs_dev, step = plan.leaves, plan.outs_dev, plan.step
    hess_at = leaves * outs_dev
    order = [feature for tile in plan.tiles for feature in tile]
    level_bins = lax.broadcasted_iota(jnp.int32, (BINS, rows), 0).astype(f32).astype(bf16)
    leaf_ids = lax.broadcasted_iota(jnp.int32, (TILE, rows), 0).astype(f32)
    zero = jnp.zeros((), bf16)
    one = jnp.ones((), bf16)

    def add_chunk(first, fresh):
        for k in range(chunk):
            source = first + k
            columns = slice(k * rows, (k + 1) * rows)
            misc = got_ref[source, plan.misc_at : plan.misc_at + 2, :].astype(f32)
            hess, node = misc[0:1], misc[1:2]
            weighted[hess_at : hess_at + TILE, columns] = jnp.where(leaf_ids == node, hess, 0.0).astype(bf16)
            node_wide = jnp.broadcast_to(node, (plan.outs_sent, rows)).astype(bf16)
            for place, ref in enumerate((got_ref, *others)):
                grads = ref[source, 0 : plan.outs_sent, :]
                for leaf in range(leaves):
                    at = leaf * outs_dev + place * plan.outs_sent
                    weighted[at : at + plan.outs_sent, columns] = jnp.where(
                        node_wide == jnp.asarray(leaf, bf16), grads, zero
                    )
        for group in range(plan.share // step):
            for k in range(chunk):
                for place, feature in enumerate(order[group * step : (group + 1) * step]):
                    row = plan.code_row(feature)
                    code = got_ref[first + k, row : row + 1, :]
                    marks[place * BINS : (place + 1) * BINS, k * rows : (k + 1) * rows] = jnp.where(
                        jnp.broadcast_to(code, (BINS, rows)) <= level_bins, one, zero
                    )
            part = lax.dot_general(weighted[...], marks[...], NT, preferred_element_type=f32)
            span = slice(group * step * BINS, (group + 1) * step * BINS)
            if count == 1:
                add_gains(group, part)
            elif fresh:
                left_sums[:, span] = part
            else:
                left_sums[:, span] += part

    def add_gains(group, sums):
        left = [sums[leaf * outs_dev : (leaf + 1) * outs_dev] for leaf in range(leaves)]
        hess = [sums[hess_at + leaf : hess_at + leaf + 1] for leaf in range(leaves)]
        for level in reversed(range(plan.levels)):
            nodes = 2**level
            if level < plan.levels - 1:
                left = [left[2 * n] + left[2 * n + 1] for n in range(nodes)]
                hess = [hess[2 * n] + hess[2 * n + 1] for n in range(nodes)]
            for n in range(nodes):
                total = left[n][:, BINS - 1 : BINS]
                hess_total = hess[n][:, BINS - 1 : BINS]
                right = total - left[n]
                gain = (
                    jnp.sum(left[n] * left[n], axis=0, keepdims=True) / (hess[n] + penalty)
                    + jnp.sum(right * right, axis=0, keepdims=True) / (hess_total - hess[n] + penalty)
                    - jnp.sum(total * total, axis=0, keepdims=True) / (hess_total + penalty)
                ) / plan.outs
                size = plan.sizes[level]
                for tile in range(step // 2):
                    piece = gain[:, tile * LANES : (tile + 1) * LANES]
                    for place in range(size):
                        first = place * plan.returned[level] % plan.share // 2
                        line = group * (step // 2) + tile - first
                        if 0 <= line < plan.needed[level] // 2:
                            row = plan.level_at[level] + line
                            out_ref[n * size + place, row : row + 1, :] = piece

    count = plan.devices // chunk
    add_chunk(0, True)
    if count > 1:
        lax.fori_loop(1, count, lambda c, _: (add_chunk(c * chunk, False), 0)[1], 0)
        for group in range(plan.share // step):
            add_gains(group, left_sums[:, group * step * BINS : (group + 1) * step * BINS])
    if plan.message > plan.gain_rows:
        filler = jnp.zeros((plan.message - plan.gain_rows, LANES), f32)
        for device in range(plan.half):
            out_ref[device, plan.gain_rows : plan.message, :] = filler

    def add_scores(source, total):
        for ref in (got_ref, *others):
            total = total + ref[source, plan.misc_at + 2 : plan.misc_at + plan.misc_rows, :].astype(f32)
        return total

    total = lax.fori_loop(0, plan.devices, add_scores, jnp.zeros((plan.misc_rows - 2, rows), f32))
    score_ref[...] = jnp.zeros_like(score_ref)
    for i in range(plan.score_rows):
        value = 0.0
        for piece in reversed(range(PIECES)):
            line, span = divmod(i * PIECES + piece, plan.spans)
            value = value + total[line : line + 1, span * LANES : (span + 1) * LANES]
        score_ref[i : i + 1, :] = value


def final_kernel(plan, got_ref, *refs):
    score_refs, refs = refs[: -plan.levels - 1], refs[-plan.levels - 1 :]
    *gain_refs, child_ref = refs
    side = plan.block // 2
    for level, gain_ref in enumerate(gain_refs):
        position = lax.rem(lax.axis_index("rows"), plan.sizes[level])
        for t in range(plan.returned[level] // plan.needed[level]):
            share = (position * plan.returned[level] + t * plan.share) // plan.share
            rows = slice(plan.level_at[level], plan.level_at[level] + plan.needed[level] // 2)
            total = got_ref[share * OUT_SPLIT, rows, :]
            for split in range(1, OUT_SPLIT):
                total = total + got_ref[share * OUT_SPLIT + split, rows, :]
            for start in range(0, plan.needed[level], plan.block):
                part = total[start // 2 : start // 2 + side]
                at = t * plan.share + start
                gain_ref[at : at + side, :] = part[:, :BINS]
                gain_ref[at + side : at + 2 * side, :] = part[:, BINS:]
    sums = score_refs[0][...]
    for score_ref in score_refs[1:]:
        sums = sums + score_ref[...]
    curv = sums[2 * plan.levels : 2 * plan.levels + 1, :]
    for level in range(plan.levels):
        for side in range(2):
            line = side * plan.levels + level
            scale = jnp.sqrt(curv[:, line : line + 1] + penalty)
            child_ref[level, 0, side : side + 1, :] = -sums[line : line + 1, :] / scale


def flipped(block, bit):
    count = lax.axis_size("feat")
    return lax.ppermute(block, "feat", [(p, p ^ bit) for p in range(count)])


def on_device(gradients, hessians, bin_words, children, split_feature, split_bin):
    plan = Plan(lax.axis_size("rows"), lax.axis_size("feat"), gradients, bin_words, children)
    params = pltpu.CompilerParams(vmem_limit_bytes=VMEM_BYTES)

    inputs = (gradients, hessians, bin_words, children, split_feature, split_bin)
    inputs = tuple(pltpu.with_memory_space_constraint(a, pltpu.HBM) for a in inputs)
    send = pl.pallas_call(
        functools.partial(prep_kernel, plan),
        out_shape=jax.ShapeDtypeStruct((plan.devices, plan.sent_rows, plan.slots), bf16),
        in_specs=[pl.BlockSpec(memory_space=pltpu.HBM)] * len(inputs),
        out_specs=whole(),
        scratch_shapes=[
            *(pltpu.VMEM(a.shape, a.dtype) for a in inputs[:4]),
            *(pltpu.SMEM(a.shape, a.dtype) for a in inputs[4:]),
            pltpu.VMEM((2 * plan.leaves * 8, plan.row_dev), f32),
            pltpu.VMEM((plan.outs + plan.feats + TILE, plan.row_dev), bf16),
            pltpu.VMEM((2, plan.outs + plan.feats + TILE, plan.slots), f32),
            pltpu.SemaphoreType.DMA((len(inputs),)),
        ],
        compiler_params=params,
        name="prep",
    )(*inputs)

    got = lax.all_to_all(send, "rows", 0, 0)
    arrays = [got] + ([flipped(got, 1)] if plan.pair > 1 else [])

    chunk = max(1, min(plan.devices, 4096 // plan.slots))
    while plan.devices % chunk:
        chunk -= 1
    sums_rows = plan.leaves * plan.outs_dev + TILE
    message, scores = pl.pallas_call(
        functools.partial(main_kernel, plan, chunk),
        out_shape=(
            jax.ShapeDtypeStruct((plan.half, plan.message, LANES), f32),
            jax.ShapeDtypeStruct((8, plan.outs), f32),
        ),
        in_specs=[whole()] * len(arrays),
        out_specs=(whole(), whole()),
        scratch_shapes=[
            pltpu.VMEM((sums_rows, chunk * plan.slots), bf16),
            pltpu.VMEM((plan.step * BINS, chunk * plan.slots), bf16),
            pltpu.VMEM((sums_rows, plan.share * BINS), f32),
        ],
        compiler_params=params,
        name="gains",
    )(*arrays)

    score_parts = [scores]
    for away in range(1, lax.axis_size("feat") // plan.pair):
        score_parts.append(flipped(scores, away * plan.pair))
    halves = [list(range(plan.half)), list(range(plan.half, plan.devices))]
    answer = lax.all_to_all(message, "rows", 0, 0, axis_index_groups=halves)
    shapes = [
        jax.ShapeDtypeStruct((count, BINS), f32) for count in plan.returned
    ]
    shapes.append(jax.ShapeDtypeStruct((plan.levels, 1, 2, plan.outs), f32))
    return pl.pallas_call(
        functools.partial(final_kernel, plan),
        out_shape=tuple(shapes),
        in_specs=[whole()] * (1 + len(score_parts)),
        out_specs=tuple(whole() for _ in shapes),
        compiler_params=params,
        name="finish",
    )(answer, *score_parts)


def solution(mesh):
    placed = (P("rows", None), P("rows"), P("feat", "rows"), P(None, "rows"), P(), P())
    return jax.shard_map(
        on_device,
        mesh=mesh,
        in_specs=placed,
        out_specs=(
            P("rows", "feat"),
            P("rows", "feat"),
            P("rows", "feat"),
            P(None, "rows", None, None),
        ),
        check_vma=False,
    )
```

```python
import functools

import jax
import jax.numpy as jnp
from jax import lax
from jax.experimental import pallas as pl
from jax.experimental.pallas import tpu as pltpu
from jax.sharding import PartitionSpec as P

BINS = 64
LANES = 128
TILE = 16
OUT_SPLIT = 2
PIECES = 2
penalty = 1.0
VMEM_BYTES = 32 * 2**20

bf16 = jnp.bfloat16
f32 = jnp.float32
NT = (((1,), (1,)), ((), ()))


def round_up(value, unit):
    return -(-value // unit) * unit


def whole(*_):
    return pl.BlockSpec(memory_space=pltpu.VMEM)


class Plan:
    def __init__(self, rows_axis, feat_axis, gradients, bin_words, children):
        self.devices = rows_axis
        self.half = rows_axis // 2
        self.row_dev, self.outs = gradients.shape
        self.words = bin_words.shape[0]
        self.feats = 2 * self.words
        self.levels = children.shape[0]
        self.leaves = 2 ** (self.levels - 1)
        self.slots = round_up(self.row_dev * 3 // 4, LANES)
        self.shares = self.half // OUT_SPLIT
        self.share = self.feats // self.shares
        self.outs_dev = self.outs // OUT_SPLIT
        self.pair = 2 if feat_axis % 2 == 0 else 1
        self.outs_sent = self.outs_dev // self.pair
        self.code_at = self.outs_sent
        self.misc_at = self.outs_sent + self.share
        self.score_rows = 2 * self.levels + 1
        self.spans = self.slots // LANES
        self.misc_rows = 2 + -(-self.score_rows * PIECES // self.spans)
        self.sent_rows = round_up(self.misc_at + self.misc_rows, 8)
        self.sizes = [self.devices >> (level + 1) for level in range(self.levels)]
        self.returned = [self.feats // size for size in self.sizes]
        self.needed = [min(self.share, count) for count in self.returned]
        self.block = min(self.needed)
        self.step = min(8, self.share)
        self.tiles = [
            (start + k, start + k + self.block // 2)
            for start in range(0, self.share, self.block)
            for k in range(self.block // 2)
        ]
        self.level_at = [sum(self.needed[:level]) // 2 for level in range(self.levels)]
        self.gain_rows = sum(self.needed) // 2
        self.message = round_up(self.gain_rows, 8)

    def code_row(self, feature):
        return self.code_at + feature // 2 + (feature % 2) * (self.share // 2)


def prep_kernel(plan, *refs):
    inputs, send_ref, refs = refs[:6], refs[6], refs[7:]
    fetched, (masks, table, packed, sems) = refs[:6], refs[6:]
    copies = [
        pltpu.make_async_copy(source, target, sems.at[i])
        for i, (source, target) in enumerate(zip(inputs, fetched, strict=True))
    ]
    for copy in copies:
        copy.start()
    for copy in copies:
        copy.wait()
    grad_ref, hess_ref, word_ref, child_ref, feature_ref, bin_ref = fetched
    rows = plan.row_dev
    grads = grad_ref[...]
    hess = hess_ref[...].astype(f32).reshape(1, rows)
    panel = lax.axis_index("feat")
    words = word_ref[...]
    low = jnp.bitwise_and(words, 63)
    high = jnp.bitwise_and(jnp.right_shift(words, 6), 63)
    codes = (low.astype(f32), high.astype(f32))
    nodes = [child_ref[0:1, :]]
    for level in range(1, plan.levels):
        nodes.append(nodes[-1] * 2 + child_ref[level : level + 1, :])

    unit = jnp.where(
        lax.broadcasted_iota(jnp.int32, (plan.outs, plan.outs), 0)
        == lax.broadcasted_iota(jnp.int32, (plan.outs, plan.outs), 1),
        1.0,
        0.0,
    ).astype(bf16)
    low_at, high_at, own_at = plan.outs, plan.outs + plan.words, plan.outs + plan.feats
    table[0:low_at] = lax.dot_general(unit, grads, NT, preferred_element_type=f32).astype(bf16)
    table[low_at:high_at] = low.astype(f32).astype(bf16)
    table[high_at:own_at] = high.astype(f32).astype(bf16)
    at = lax.broadcasted_iota(jnp.int32, (TILE, rows), 0)
    leaf = jnp.bitwise_and(nodes[-1], plan.leaves - 1).astype(f32)
    table[own_at:] = jnp.where(at == 0, hess, jnp.where(at == 1, leaf, 0.0)).astype(bf16)
    side = jnp.where(at == nodes[0], 1.0, 0.0)
    ahead = jnp.where(
        lax.broadcasted_iota(jnp.int32, (rows, rows), 0) <= lax.broadcasted_iota(jnp.int32, (rows, rows), 1), 1.0, 0.0
    )
    rank = jnp.dot(side.astype(bf16), ahead.astype(bf16), preferred_element_type=f32)
    slot = jnp.where(side > 0.0, rank - 1.0, -1.0)
    slot_ids = lax.broadcasted_iota(jnp.int32, (plan.slots, rows), 0).astype(f32)
    for half in range(2):
        chosen = jnp.where(slot_ids == slot[half : half + 1], 1.0, 0.0).astype(bf16)
        packed[half] = lax.dot_general(table[...], chosen, NT, preferred_element_type=f32)

    masks[...] = jnp.zeros_like(masks)
    leaf_count = 2 * plan.leaves
    for level in range(plan.levels):
        for node in range(2 ** (level + 1)):
            slot = 2 ** (level + 1) - 2 + node
            feature = feature_ref[slot]
            inner = feature - panel * plan.feats
            owned = jnp.logical_and(inner >= 0, inner < plan.feats)
            inner = jnp.clip(inner, 0, plan.feats - 1)
            word = word_ref[pl.ds(inner // 2, 1), :]
            code = jnp.bitwise_and(jnp.right_shift(word, 6 * lax.rem(inner, 2)), 63)
            here = jnp.where(nodes[level] == node, jnp.where(owned, 1.0, 0.0), 0.0)
            left = jnp.where(code <= bin_ref[slot], here, 0.0)
            right = here - left
            under = 2 ** (plan.levels - level - 1)
            for leaf in range(node * under, (node + 1) * under):
                masks[leaf * 8 + level : leaf * 8 + level + 1, :] = left
                at_right = leaf * 8 + plan.levels + level
                masks[at_right : at_right + 1, :] = right
    mask = masks[...]
    sums = jnp.dot(mask.astype(bf16), grads, preferred_element_type=f32)
    curv = jnp.sum(mask * hess, axis=1, keepdims=True)
    shape = (leaf_count * 8, plan.outs)
    line = jnp.bitwise_and(lax.broadcasted_iota(jnp.int32, shape, 0), 7)
    lane = lax.broadcasted_iota(jnp.int32, shape, 1)
    spread = jnp.where(lane == line, curv, 0.0).reshape(leaf_count, 8, plan.outs)
    spread = jnp.broadcast_to(jnp.sum(spread, axis=1, keepdims=True), spread.shape)
    sums = jnp.where(line == 2 * plan.levels, spread.reshape(shape), sums)
    pieces = []
    for _ in range(PIECES):
        pieces.append(sums.astype(bf16).astype(f32))
        sums = sums - pieces[-1]

    parity = lax.rem(panel, plan.pair)
    word_share = plan.share // 2
    blank = jnp.zeros((1, LANES), f32)
    filler = jnp.zeros((plan.sent_rows - plan.misc_at - plan.misc_rows, plan.slots), f32)
    lines = []
    for leaf in range(leaf_count):
        parts = [piece[leaf * 8 + i : leaf * 8 + i + 1] for i in range(plan.score_rows) for piece in pieces]
        parts += [blank] * (-len(parts) % plan.spans)
        parts = [jnp.concatenate(parts[i : i + plan.spans], axis=1) for i in range(0, len(parts), plan.spans)]
        lines.append(jnp.concatenate(parts + ([filler] if filler.shape[0] else []), axis=0))
    for device in range(plan.devices):
        half, place = divmod(device, plan.half)
        share, split = divmod(place, OUT_SPLIT)
        start = pl.multiple_of(split * plan.outs_dev + parity * plan.outs_sent, plan.outs_sent)
        low_from, high_from = low_at + share * word_share, high_at + share * word_share
        send_ref[device] = jnp.concatenate(
            [
                packed[half, pl.ds(start, plan.outs_sent), :],
                packed[half, low_from : low_from + word_share, :],
                packed[half, high_from : high_from + word_share, :],
                packed[half, own_at : own_at + 2, :],
                lines[device * leaf_count // plan.devices],
            ],
            axis=0,
        ).astype(bf16)


def main_kernel(plan, chunk, got_ref, *refs):
    others, refs = refs[: plan.pair - 1], refs[plan.pair - 1 :]
    out_ref, weighted, left_sums = refs
    rows = plan.slots
    leaves, outs_dev, step = plan.leaves, plan.outs_dev, plan.step
    hess_at = leaves * outs_dev
    order = [feature for tile in plan.tiles for feature in tile]
    level_bins = lax.broadcasted_iota(jnp.int32, (BINS, rows), 0).astype(f32).astype(bf16)
    leaf_ids = lax.broadcasted_iota(jnp.int32, (TILE, rows), 0).astype(f32)
    zero = jnp.zeros((), bf16)
    one = jnp.ones((), bf16)

    def marked(source, feature):
        row = plan.code_row(feature)
        code = jnp.broadcast_to(got_ref[source, row : row + 1, :], (BINS, rows))
        return jnp.where(code <= level_bins, one, zero)

    def add_chunk(first, fresh):
        for k in range(chunk):
            source = first + k
            columns = slice(k * rows, (k + 1) * rows)
            misc = got_ref[source, plan.misc_at : plan.misc_at + 2, :].astype(f32)
            hess, node = misc[0:1], misc[1:2]
            weighted[hess_at : hess_at + TILE, columns] = jnp.where(leaf_ids == node, hess, 0.0).astype(bf16)
            node_wide = jnp.broadcast_to(node, (plan.outs_sent, rows)).astype(bf16)
            for place, ref in enumerate((got_ref, *others)):
                grads = ref[source, 0 : plan.outs_sent, :]
                for leaf in range(leaves):
                    at = leaf * outs_dev + place * plan.outs_sent
                    weighted[at : at + plan.outs_sent, columns] = jnp.where(
                        node_wide == jnp.asarray(leaf, bf16), grads, zero
                    )
        for group in range(plan.share // step):
            features = order[group * step : (group + 1) * step]
            marks = jnp.concatenate(
                [
                    jnp.concatenate([marked(first + k, feature) for feature in features], axis=0)
                    for k in range(chunk)
                ],
                axis=1,
            )
            part = lax.dot_general(weighted[...], marks, NT, preferred_element_type=f32)
            span = slice(group * step * BINS, (group + 1) * step * BINS)
            if count == 1:
                add_gains(group, part)
            elif fresh:
                left_sums[:, span] = part
            else:
                left_sums[:, span] += part

    known = []

    def add_gains(group, sums):
        left = [sums[leaf * outs_dev : (leaf + 1) * outs_dev] for leaf in range(leaves)]
        hess = [sums[hess_at + leaf : hess_at + leaf + 1] for leaf in range(leaves)]
        ends = [(level, n) for level in reversed(range(plan.levels)) for n in range(2**level)]
        for level in reversed(range(plan.levels - 1)):
            past = len(left) - 2 ** (level + 1)
            for n in range(past, len(left), 2):
                left.append(left[n] + left[n + 1])
                hess.append(hess[n] + hess[n + 1])
        hess = jnp.concatenate(hess, axis=0) + penalty
        if not known:
            totals = [part[:, BINS - 1 : BINS] for part in left]
            squares = jnp.concatenate([jnp.sum(t * t, axis=0, keepdims=True) for t in totals], axis=0)
            hess_total = hess[:, BINS - 1 : BINS] + penalty
            known.extend([totals, hess_total, squares / (hess_total - penalty)])
        totals, hess_total, whole_part = known
        on_left = jnp.concatenate([jnp.sum(part * part, axis=0, keepdims=True) for part in left], axis=0)
        rights = [t - part for t, part in zip(totals, left, strict=True)]
        on_right = jnp.concatenate([jnp.sum(part * part, axis=0, keepdims=True) for part in rights], axis=0)
        gains = (on_left / hess + on_right / (hess_total - hess) - whole_part) / plan.outs
        for line_at, (level, n) in enumerate(ends):
            size = plan.sizes[level]
            for tile in range(step // 2):
                piece = gains[line_at : line_at + 1, tile * LANES : (tile + 1) * LANES]
                for place in range(size):
                    first = place * plan.returned[level] % plan.share // 2
                    line = group * (step // 2) + tile - first
                    if 0 <= line < plan.needed[level] // 2:
                        row = plan.level_at[level] + line
                        out_ref[n * size + place, row : row + 1, :] = piece

    count = plan.devices // chunk
    add_chunk(0, True)
    if count > 1:
        lax.fori_loop(1, count, lambda c, _: (add_chunk(c * chunk, False), 0)[1], 0)
        for group in range(plan.share // step):
            add_gains(group, left_sums[:, group * step * BINS : (group + 1) * step * BINS])
    if plan.message > plan.gain_rows:
        filler = jnp.zeros((plan.message - plan.gain_rows, LANES), f32)
        for device in range(plan.half):
            out_ref[device, plan.gain_rows : plan.message, :] = filler


def score_kernel(plan, got_ref, score_ref):
    def add(source, total):
        return total + got_ref[source, plan.misc_at + 2 : plan.misc_at + plan.misc_rows, :].astype(f32)

    total = lax.fori_loop(0, plan.devices, add, jnp.zeros((plan.misc_rows - 2, plan.slots), f32))
    score_ref[...] = jnp.zeros_like(score_ref)
    for i in range(plan.score_rows):
        value = 0.0
        for piece in reversed(range(PIECES)):
            line, span = divmod(i * PIECES + piece, plan.spans)
            value = value + total[line : line + 1, span * LANES : (span + 1) * LANES]
        score_ref[i : i + 1, :] = value


def final_kernel(plan, got_ref, *refs):
    score_refs, refs = refs[: -plan.levels - 1], refs[-plan.levels - 1 :]
    *gain_refs, child_ref = refs
    side = plan.block // 2
    for level, gain_ref in enumerate(gain_refs):
        position = lax.rem(lax.axis_index("rows"), plan.sizes[level])
        for t in range(plan.returned[level] // plan.needed[level]):
            share = (position * plan.returned[level] + t * plan.share) // plan.share
            rows = slice(plan.level_at[level], plan.level_at[level] + plan.needed[level] // 2)
            total = got_ref[share * OUT_SPLIT, rows, :]
            for split in range(1, OUT_SPLIT):
                total = total + got_ref[share * OUT_SPLIT + split, rows, :]
            for start in range(0, plan.needed[level], plan.block):
                part = total[start // 2 : start // 2 + side]
                at = t * plan.share + start
                gain_ref[at : at + side, :] = part[:, :BINS]
                gain_ref[at + side : at + 2 * side, :] = part[:, BINS:]
    sums = score_refs[0][...]
    for score_ref in score_refs[1:]:
        sums = sums + score_ref[...]
    curv = sums[2 * plan.levels : 2 * plan.levels + 1, :]
    for level in range(plan.levels):
        for side in range(2):
            line = side * plan.levels + level
            scale = jnp.sqrt(curv[:, line : line + 1] + penalty)
            child_ref[level, 0, side : side + 1, :] = -sums[line : line + 1, :] / scale


def flipped(block, bit):
    count = lax.axis_size("feat")
    return lax.ppermute(block, "feat", [(p, p ^ bit) for p in range(count)])


def on_device(gradients, hessians, bin_words, children, split_feature, split_bin):
    plan = Plan(lax.axis_size("rows"), lax.axis_size("feat"), gradients, bin_words, children)
    params = pltpu.CompilerParams(vmem_limit_bytes=VMEM_BYTES)

    inputs = (gradients, hessians, bin_words, children, split_feature, split_bin)
    inputs = tuple(pltpu.with_memory_space_constraint(a, pltpu.HBM) for a in inputs)
    send = pl.pallas_call(
        functools.partial(prep_kernel, plan),
        out_shape=jax.ShapeDtypeStruct((plan.devices, plan.sent_rows, plan.slots), bf16),
        in_specs=[pl.BlockSpec(memory_space=pltpu.HBM)] * len(inputs),
        out_specs=whole(),
        scratch_shapes=[
            *(pltpu.VMEM(a.shape, a.dtype) for a in inputs[:4]),
            *(pltpu.SMEM(a.shape, a.dtype) for a in inputs[4:]),
            pltpu.VMEM((2 * plan.leaves * 8, plan.row_dev), f32),
            pltpu.VMEM((plan.outs + plan.feats + TILE, plan.row_dev), bf16),
            pltpu.VMEM((2, plan.outs + plan.feats + TILE, plan.slots), f32),
            pltpu.SemaphoreType.DMA((len(inputs),)),
        ],
        compiler_params=params,
        name="prep",
    )(*inputs)

    got = lax.all_to_all(send, "rows", 0, 0)
    arrays = [got] + ([flipped(got, 1)] if plan.pair > 1 else [])
    scores = pl.pallas_call(
        functools.partial(score_kernel, plan),
        out_shape=jax.ShapeDtypeStruct((8, plan.outs), f32),
        in_specs=[whole()],
        out_specs=whole(),
        compiler_params=params,
        name="scores",
    )(got)
    score_parts = [scores] + [flipped(scores, away) for away in range(1, lax.axis_size("feat"))]

    chunk = max(1, min(plan.devices, 4096 // plan.slots))
    while plan.devices % chunk:
        chunk -= 1
    sums_rows = plan.leaves * plan.outs_dev + TILE
    message = pl.pallas_call(
        functools.partial(main_kernel, plan, chunk),
        out_shape=jax.ShapeDtypeStruct((plan.half, plan.message, LANES), f32),
        in_specs=[whole()] * len(arrays),
        out_specs=whole(),
        scratch_shapes=[
            pltpu.VMEM((sums_rows, chunk * plan.slots), bf16),
            pltpu.VMEM((sums_rows, plan.share * BINS), f32),
        ],
        cost_estimate=pl.CostEstimate(
            flops=2 * sums_rows * plan.devices * plan.slots * plan.share * BINS,
            bytes_accessed=4 * plan.devices * plan.sent_rows * plan.slots,
            transcendentals=0,
        ),
        compiler_params=params,
        name="gains",
    )(*arrays)

    message, *score_parts = lax.optimization_barrier((message, *score_parts))
    halves = [list(range(plan.half)), list(range(plan.half, plan.devices))]
    answer = lax.all_to_all(message, "rows", 0, 0, axis_index_groups=halves)
    shapes = [
        jax.ShapeDtypeStruct((count, BINS), f32) for count in plan.returned
    ]
    shapes.append(jax.ShapeDtypeStruct((plan.levels, 1, 2, plan.outs), f32))
    return pl.pallas_call(
        functools.partial(final_kernel, plan),
        out_shape=tuple(shapes),
        in_specs=[whole()] * (1 + len(score_parts)),
        out_specs=tuple(whole() for _ in shapes),
        compiler_params=params,
        name="finish",
    )(answer, *score_parts)


def solution(mesh):
    placed = (P("rows", None), P("rows"), P("feat", "rows"), P(None, "rows"), P(), P())
    return jax.shard_map(
        on_device,
        mesh=mesh,
        in_specs=placed,
        out_specs=(
            P("rows", "feat"),
            P("rows", "feat"),
            P("rows", "feat"),
            P(None, "rows", None, None),
        ),
        check_vma=False,
    )
```

```python
import functools

import jax
import jax.numpy as jnp
from jax import lax
from jax.experimental import pallas as pl
from jax.experimental.pallas import tpu as pltpu
from jax.sharding import PartitionSpec as P

BINS = 64
LANES = 128
TILE = 16
OUT_SPLIT = 2
PIECES = 2
penalty = 1.0
VMEM_BYTES = 32 * 2**20

bf16 = jnp.bfloat16
f32 = jnp.float32
NT = (((1,), (1,)), ((), ()))
PERMUTED = 8


def div(value, by):
    return value // by if isinstance(value, int) else lax.div(value, jnp.int32(by))


def rem(value, by):
    return value % by if isinstance(value, int) else lax.rem(value, jnp.int32(by))


def round_up(value, unit):
    return -(-value // unit) * unit


def whole(*_):
    return pl.BlockSpec(memory_space=pltpu.VMEM)


class Plan:
    def __init__(self, rows_axis, feat_axis, gradients, bin_words, children):
        self.devices = rows_axis
        self.half = rows_axis // 2
        self.row_dev, self.outs = gradients.shape
        self.words = bin_words.shape[0]
        self.feats = 2 * self.words
        self.levels = children.shape[0]
        self.leaves = 2 ** (self.levels - 1)
        self.slots = round_up(self.row_dev * 3 // 4, LANES)
        self.shares = self.half // OUT_SPLIT
        self.share = self.feats // self.shares
        self.outs_dev = self.outs // OUT_SPLIT
        self.pair = 2 if feat_axis % 2 == 0 else 1
        self.outs_sent = self.outs_dev // self.pair
        self.grad_at = self.share
        self.misc_at = self.share + self.outs_sent
        self.score_rows = 2 * self.levels + 1
        self.spans = self.slots // LANES
        self.misc_rows = 2 + -(-self.score_rows * PIECES // self.spans)
        self.sent_rows = round_up(self.misc_at + self.misc_rows, 8)
        self.sizes = [self.devices >> (level + 1) for level in range(self.levels)]
        self.returned = [self.feats // size for size in self.sizes]
        self.needed = [min(self.share, count) for count in self.returned]
        self.block = min(self.needed)
        self.step = min(8, self.share)
        self.tiles = [
            (start + k, start + k + self.block // 2)
            for start in range(0, self.share, self.block)
            for k in range(self.block // 2)
        ]
        self.level_at = [sum(self.needed[:level]) // 2 for level in range(self.levels)]
        self.gain_rows = sum(self.needed) // 2
        self.message = round_up(self.gain_rows, 8)
        self.ends = [(level, n) for level in reversed(range(self.levels)) for n in range(2**level)]
        self.permuted = self.half <= PERMUTED
        self.messages = self.half if self.permuted else 1

    def code_row(self, feature):
        return feature // 2 + (feature % 2) * (self.share // 2)


def prep_kernel(plan, *refs):
    inputs, send_ref, refs = refs[:6], refs[6], refs[7:]
    fetched, (masks, table, packed, sems) = refs[:6], refs[6:]
    copies = [
        pltpu.make_async_copy(source, target, sems.at[i])
        for i, (source, target) in enumerate(zip(inputs, fetched, strict=True))
    ]
    for copy in copies:
        copy.start()
    rows = plan.row_dev
    panel = lax.axis_index("feat")
    sent = OUT_SPLIT * plan.outs_sent
    low_at, high_at, own_at = sent, sent + plan.words, sent + plan.feats
    at = lax.broadcasted_iota(jnp.int32, (sent, plan.outs), 0)
    wanted = at + (at // plan.outs_sent) * (plan.outs_dev - plan.outs_sent) + lax.rem(panel, plan.pair) * plan.outs_sent
    turn = jnp.where(wanted == lax.broadcasted_iota(jnp.int32, (sent, plan.outs), 1), 1.0, 0.0).astype(bf16)
    ahead = jnp.where(
        lax.broadcasted_iota(jnp.int32, (rows, rows), 0) <= lax.broadcasted_iota(jnp.int32, (rows, rows), 1), 1.0, 0.0
    ).astype(bf16)
    for copy in copies:
        copy.wait()
    grad_ref, hess_ref, word_ref, child_ref, feature_ref, bin_ref = fetched
    grads = grad_ref[...]
    hess = hess_ref[...].astype(f32).reshape(1, rows)
    words = word_ref[...]
    low = jnp.bitwise_and(words, 63)
    high = jnp.bitwise_and(jnp.right_shift(words, 6), 63)
    codes = (low.astype(f32), high.astype(f32))
    nodes = [child_ref[0:1, :]]
    for level in range(1, plan.levels):
        nodes.append(nodes[-1] * 2 + child_ref[level : level + 1, :])

    table[0:low_at] = lax.dot_general(turn, grads, NT, preferred_element_type=f32).astype(bf16)
    table[low_at:high_at] = low.astype(f32).astype(bf16)
    table[high_at:own_at] = high.astype(f32).astype(bf16)
    at = lax.broadcasted_iota(jnp.int32, (TILE, rows), 0)
    leaf = jnp.bitwise_and(nodes[-1], plan.leaves - 1).astype(f32)
    table[own_at:] = jnp.where(at == 0, hess, jnp.where(at == 1, leaf, 0.0)).astype(bf16)
    side = jnp.where(at == nodes[0], 1.0, 0.0)
    rank = jnp.dot(side.astype(bf16), ahead, preferred_element_type=f32)
    slot = jnp.where(side > 0.0, rank - 1.0, -1.0)
    slot_ids = lax.broadcasted_iota(jnp.int32, (plan.slots, rows), 0).astype(f32)
    for half in range(2):
        chosen = jnp.where(slot_ids == slot[half : half + 1], 1.0, 0.0).astype(bf16)
        packed[half] = lax.dot_general(table[...], chosen, NT, preferred_element_type=f32)

    masks[...] = jnp.zeros_like(masks)
    leaf_count = 2 * plan.leaves
    for level in range(plan.levels):
        for node in range(2 ** (level + 1)):
            slot = 2 ** (level + 1) - 2 + node
            feature = feature_ref[slot]
            inner = feature - panel * plan.feats
            owned = jnp.logical_and(inner >= 0, inner < plan.feats)
            inner = jnp.clip(inner, 0, plan.feats - 1)
            word = word_ref[pl.ds(inner // 2, 1), :]
            code = jnp.bitwise_and(jnp.right_shift(word, 6 * lax.rem(inner, 2)), 63)
            here = jnp.where(nodes[level] == node, jnp.where(owned, 1.0, 0.0), 0.0)
            left = jnp.where(code <= bin_ref[slot], here, 0.0)
            right = here - left
            under = 2 ** (plan.levels - level - 1)
            for leaf in range(node * under, (node + 1) * under):
                masks[leaf * 8 + level : leaf * 8 + level + 1, :] = left
                at_right = leaf * 8 + plan.levels + level
                masks[at_right : at_right + 1, :] = right
    mask = masks[...]
    sums = jnp.dot(mask.astype(bf16), grads, preferred_element_type=f32)
    curv = jnp.sum(mask * hess, axis=1, keepdims=True)
    shape = (leaf_count * 8, plan.outs)
    line = jnp.bitwise_and(lax.broadcasted_iota(jnp.int32, shape, 0), 7)
    lane = lax.broadcasted_iota(jnp.int32, shape, 1)
    spread = jnp.where(lane == line, curv, 0.0).reshape(leaf_count, 8, plan.outs)
    spread = jnp.broadcast_to(jnp.sum(spread, axis=1, keepdims=True), spread.shape)
    sums = jnp.where(line == 2 * plan.levels, spread.reshape(shape), sums)
    pieces = []
    for _ in range(PIECES):
        pieces.append(sums.astype(bf16).astype(f32))
        sums = sums - pieces[-1]

    word_share = plan.share // 2
    blank = jnp.zeros((1, LANES), f32)
    filler = jnp.zeros((plan.sent_rows - plan.misc_at - plan.misc_rows, plan.slots), f32)
    lines = []
    for leaf in range(leaf_count):
        parts = [piece[leaf * 8 + i : leaf * 8 + i + 1] for i in range(plan.score_rows) for piece in pieces]
        parts += [blank] * (-len(parts) % plan.spans)
        parts = [jnp.concatenate(parts[i : i + plan.spans], axis=1) for i in range(0, len(parts), plan.spans)]
        lines.append(jnp.concatenate(parts + ([filler] if filler.shape[0] else []), axis=0))
    for device in range(plan.devices):
        half, place = divmod(device, plan.half)
        share, split = divmod(place, OUT_SPLIT)
        grads_from = split * plan.outs_sent
        low_from, high_from = low_at + share * word_share, high_at + share * word_share
        send_ref[device] = jnp.concatenate(
            [
                packed[half, low_from : low_from + word_share, :],
                packed[half, high_from : high_from + word_share, :],
                packed[half, grads_from : grads_from + plan.outs_sent, :],
                packed[half, own_at : own_at + 2, :],
                lines[device * leaf_count // plan.devices],
            ],
            axis=0,
        ).astype(bf16)


def main_kernel(plan, chunk, got_ref, *refs):
    others, refs = refs[: plan.pair - 1], refs[plan.pair - 1 :]
    out_refs, (weighted, gain_table, left_sums) = refs[: plan.messages], refs[plan.messages :]
    rows = plan.slots
    leaves, outs_dev, step = plan.leaves, plan.outs_dev, plan.step
    hess_at = leaves * outs_dev
    order = [feature for tile in plan.tiles for feature in tile]
    level_bins = lax.broadcasted_iota(jnp.int32, (BINS, rows), 0).astype(f32).astype(bf16)
    leaf_ids = lax.broadcasted_iota(jnp.int32, (TILE, rows), 0).astype(f32)
    zero = jnp.zeros((), bf16)
    one = jnp.ones((), bf16)

    def marked(source, feature):
        row = plan.code_row(feature)
        code = jnp.broadcast_to(got_ref[source, row : row + 1, :], (BINS, rows))
        return jnp.where(code <= level_bins, one, zero)

    def add_chunk(first, fresh):
        for k in range(chunk):
            source = first + k
            columns = slice(k * rows, (k + 1) * rows)
            misc = got_ref[source, plan.misc_at : plan.misc_at + 2, :].astype(f32)
            hess, node = misc[0:1], misc[1:2]
            weighted[hess_at : hess_at + TILE, columns] = jnp.where(leaf_ids == node, hess, 0.0).astype(bf16)
            node_wide = jnp.broadcast_to(node, (plan.outs_sent, rows)).astype(bf16)
            for place, ref in enumerate((got_ref, *others)):
                grads_from = plan.grad_at if place == 0 else 0
                grads = ref[source, grads_from : grads_from + plan.outs_sent, :]
                for leaf in range(leaves):
                    at = leaf * outs_dev + place * plan.outs_sent
                    weighted[at : at + plan.outs_sent, columns] = jnp.where(
                        node_wide == jnp.asarray(leaf, bf16), grads, zero
                    )
        for group in range(plan.share // step):
            features = order[group * step : (group + 1) * step]
            marks = jnp.concatenate(
                [
                    jnp.concatenate([marked(first + k, feature) for feature in features], axis=0)
                    for k in range(chunk)
                ],
                axis=1,
            )
            part = lax.dot_general(weighted[...], marks, NT, preferred_element_type=f32)
            span = slice(group * step * BINS, (group + 1) * step * BINS)
            if count == 1:
                add_gains(group, part)
            elif fresh:
                left_sums[:, span] = part
            else:
                left_sums[:, span] += part

    known = []

    def add_gains(group, sums):
        left = [sums[leaf * outs_dev : (leaf + 1) * outs_dev] for leaf in range(leaves)]
        hess = [sums[hess_at + leaf : hess_at + leaf + 1] for leaf in range(leaves)]
        for level in reversed(range(plan.levels - 1)):
            past = len(left) - 2 ** (level + 1)
            for n in range(past, len(left), 2):
                left.append(left[n] + left[n + 1])
                hess.append(hess[n] + hess[n + 1])
        hess = jnp.concatenate(hess, axis=0) + penalty
        if not known:
            totals = [part[:, BINS - 1 : BINS] for part in left]
            squares = jnp.concatenate([jnp.sum(t * t, axis=0, keepdims=True) for t in totals], axis=0)
            hess_total = hess[:, BINS - 1 : BINS] + penalty
            known.extend([totals, hess_total, squares / (hess_total - penalty)])
        totals, hess_total, whole_part = known
        on_left = jnp.concatenate([jnp.sum(part * part, axis=0, keepdims=True) for part in left], axis=0)
        rights = [t - part for t, part in zip(totals, left, strict=True)]
        on_right = jnp.concatenate([jnp.sum(part * part, axis=0, keepdims=True) for part in rights], axis=0)
        gains = (on_left / hess + on_right / (hess_total - hess) - whole_part) / plan.outs
        for end in range(len(plan.ends)):
            for tile in range(step // 2):
                at = group * (step // 2) + tile
                gain_table[end, at : at + 1, :] = gains[end : end + 1, tile * LANES : (tile + 1) * LANES]

    count = plan.devices // chunk
    add_chunk(0, True)
    if count > 1:
        lax.fori_loop(1, count, lambda c, _: (add_chunk(c * chunk, False), 0)[1], 0)
        for group in range(plan.share // step):
            add_gains(group, left_sums[:, group * step * BINS : (group + 1) * step * BINS])
    me = rem(lax.axis_index("rows"), plan.half)
    for slot in range(plan.half):
        place = jnp.bitwise_xor(me, slot) if plan.permuted else slot
        out_ref = out_refs[slot] if plan.permuted else out_refs[0].at[slot]
        for level in range(plan.levels):
            count = plan.needed[level] // 2
            end = plan.ends.index((level, 0)) + div(place, plan.sizes[level])
            first = rem(rem(place, plan.sizes[level]) * plan.returned[level], plan.share) // 2
            if not isinstance(first, int) and count % 8 == 0:
                first = pl.multiple_of(first, 8)
            at = plan.level_at[level]
            out_ref[at : at + count, :] = gain_table[end, pl.ds(first, count), :]
        if plan.message > plan.gain_rows:
            out_ref[plan.gain_rows :, :] = jnp.zeros((plan.message - plan.gain_rows, LANES), f32)


def score_kernel(plan, got_ref, score_ref, grads_ref):
    grads_ref[...] = got_ref[:, plan.grad_at : plan.grad_at + plan.outs_sent, :]

    def add(source, total):
        return total + got_ref[source, plan.misc_at + 2 : plan.misc_at + plan.misc_rows, :].astype(f32)

    total = lax.fori_loop(0, plan.devices, add, jnp.zeros((plan.misc_rows - 2, plan.slots), f32))
    score_ref[...] = jnp.zeros_like(score_ref)
    for i in range(plan.score_rows):
        value = 0.0
        for piece in reversed(range(PIECES)):
            line, span = divmod(i * PIECES + piece, plan.spans)
            value = value + total[line : line + 1, span * LANES : (span + 1) * LANES]
        score_ref[i : i + 1, :] = value


def final_kernel(plan, *refs):
    got_refs, refs = refs[: plan.messages], refs[plan.messages :]
    score_refs, refs = refs[: -plan.levels - 1], refs[-plan.levels - 1 :]
    *gain_refs, child_ref = refs
    me = rem(lax.axis_index("rows"), plan.half)
    side = plan.block // 2
    totals = []
    for other in range(plan.shares):
        share = jnp.bitwise_xor(div(me, OUT_SPLIT), other)
        total = 0.0
        for split in range(OUT_SPLIT):
            slot = other * OUT_SPLIT + split
            total = total + (got_refs[slot][...] if plan.permuted else got_refs[0][jnp.bitwise_xor(me, slot)])
        totals.append((share, total))
    for level, gain_ref in enumerate(gain_refs):
        rows = slice(plan.level_at[level], plan.level_at[level] + plan.needed[level] // 2)
        first = div(rem(me, plan.sizes[level]) * plan.returned[level], plan.share)
        for turn in range(plan.returned[level] // plan.needed[level]):
            value = totals[0][1][rows]
            for share, total in totals[1:]:
                value = jnp.where(share == first + turn, total[rows], value)
            for start in range(0, plan.needed[level], plan.block):
                part = value[start // 2 : start // 2 + side]
                at = turn * plan.share + start
                gain_ref[at : at + side, :] = part[:, :BINS]
                gain_ref[at + side : at + 2 * side, :] = part[:, BINS:]
    sums = score_refs[0][...]
    for score_ref in score_refs[1:]:
        sums = sums + score_ref[...]
    curv = sums[2 * plan.levels : 2 * plan.levels + 1, :]
    for level in range(plan.levels):
        for side in range(2):
            line = side * plan.levels + level
            scale = jnp.sqrt(curv[:, line : line + 1] + penalty)
            child_ref[level, 0, side : side + 1, :] = -sums[line : line + 1, :] / scale


def flipped(block, bits, axis="feat"):
    count = lax.axis_size(axis)
    return lax.ppermute(block, axis, [(p, p ^ bits) for p in range(count)])


def on_device(gradients, hessians, bin_words, children, split_feature, split_bin):
    plan = Plan(lax.axis_size("rows"), lax.axis_size("feat"), gradients, bin_words, children)
    params = pltpu.CompilerParams(vmem_limit_bytes=VMEM_BYTES)

    table_rows = OUT_SPLIT * plan.outs_sent + plan.feats + TILE
    inputs = (gradients, hessians, bin_words, children, split_feature, split_bin)
    inputs = tuple(pltpu.with_memory_space_constraint(a, pltpu.HBM) for a in inputs)
    send = pl.pallas_call(
        functools.partial(prep_kernel, plan),
        out_shape=jax.ShapeDtypeStruct((plan.devices, plan.sent_rows, plan.slots), bf16),
        in_specs=[pl.BlockSpec(memory_space=pltpu.HBM)] * len(inputs),
        out_specs=whole(),
        scratch_shapes=[
            *(pltpu.VMEM(a.shape, a.dtype) for a in inputs[:4]),
            *(pltpu.SMEM(a.shape, a.dtype) for a in inputs[4:]),
            pltpu.VMEM((2 * plan.leaves * 8, plan.row_dev), f32),
            pltpu.VMEM((table_rows, plan.row_dev), bf16),
            pltpu.VMEM((2, table_rows, plan.slots), f32),
            pltpu.SemaphoreType.DMA((len(inputs),)),
        ],
        compiler_params=params,
        name="prep",
    )(*inputs)

    got = lax.all_to_all(send, "rows", 0, 0)
    scores, grads_part = pl.pallas_call(
        functools.partial(score_kernel, plan),
        out_shape=(
            jax.ShapeDtypeStruct((8, plan.outs), f32),
            jax.ShapeDtypeStruct((plan.devices, plan.outs_sent, plan.slots), bf16),
        ),
        in_specs=[whole()],
        out_specs=(whole(), whole()),
        compiler_params=params,
        name="scores",
    )(got)
    arrays = [got] + ([flipped(grads_part, 1)] if plan.pair > 1 else [])
    score_parts = [scores] + [flipped(scores, away) for away in range(1, lax.axis_size("feat"))]

    chunk = max(1, min(plan.devices, 4096 // plan.slots))
    while plan.devices % chunk:
        chunk -= 1
    sums_rows = plan.leaves * plan.outs_dev + TILE
    block = (plan.message, LANES) if plan.permuted else (plan.half, plan.message, LANES)
    messages = pl.pallas_call(
        functools.partial(main_kernel, plan, chunk),
        out_shape=[jax.ShapeDtypeStruct(block, f32)] * plan.messages,
        in_specs=[whole()] * len(arrays),
        out_specs=[whole()] * plan.messages,
        scratch_shapes=[
            pltpu.VMEM((sums_rows, chunk * plan.slots), bf16),
            pltpu.VMEM((len(plan.ends), plan.share // 2, LANES), f32),
            pltpu.VMEM((sums_rows, plan.share * BINS), f32),
        ],
        cost_estimate=pl.CostEstimate(
            flops=2 * sums_rows * plan.devices * plan.slots * plan.share * BINS,
            bytes_accessed=4 * plan.devices * plan.sent_rows * plan.slots,
            transcendentals=0,
        ),
        compiler_params=params,
        name="gains",
    )(*arrays)

    messages, score_parts = lax.optimization_barrier((list(messages), score_parts))
    if plan.permuted:
        messages = [flipped(block, slot, "rows") if slot else block for slot, block in enumerate(messages)]
    else:
        halves = [list(range(plan.half)), list(range(plan.half, plan.devices))]
        messages = [lax.all_to_all(messages[0], "rows", 0, 0, axis_index_groups=halves)]
    shapes = [
        jax.ShapeDtypeStruct((count, BINS), f32) for count in plan.returned
    ]
    shapes.append(jax.ShapeDtypeStruct((plan.levels, 1, 2, plan.outs), f32))
    return pl.pallas_call(
        functools.partial(final_kernel, plan),
        out_shape=tuple(shapes),
        in_specs=[whole()] * (plan.messages + len(score_parts)),
        out_specs=tuple(whole() for _ in shapes),
        compiler_params=params,
        name="finish",
    )(*messages, *score_parts)


def solution(mesh):
    placed = (P("rows", None), P("rows"), P("feat", "rows"), P(None, "rows"), P(), P())
    return jax.shard_map(
        on_device,
        mesh=mesh,
        in_specs=placed,
        out_specs=(
            P("rows", "feat"),
            P("rows", "feat"),
            P("rows", "feat"),
            P(None, "rows", None, None),
        ),
        check_vma=False,
    )
```

```python
import functools

import jax
import jax.numpy as jnp
from jax import lax
from jax.experimental import pallas as pl
from jax.experimental.pallas import tpu as pltpu
from jax.sharding import PartitionSpec as P

BINS = 64
LANES = 128
TILE = 16
OUT_SPLIT = 2
PIECES = 2
penalty = 1.0
VMEM_BYTES = 32 * 2**20

bf16 = jnp.bfloat16
f32 = jnp.float32
NT = (((1,), (1,)), ((), ()))
PERMUTED = 8


def div(value, by):
    return value // by if isinstance(value, int) else lax.div(value, jnp.int32(by))


def rem(value, by):
    return value % by if isinstance(value, int) else lax.rem(value, jnp.int32(by))


def round_up(value, unit):
    return -(-value // unit) * unit


def whole(*_):
    return pl.BlockSpec(memory_space=pltpu.VMEM)


def aligned(value, unit):
    return value if isinstance(value, int) or unit % 8 else pl.multiple_of(value, 8)


def target(me, slot, count):
    return rem(me + slot, count)


def source_of(me, slot, count):
    return rem(me + (count - slot), count)


def exchanged(blocks, group, count):
    moved = [blocks[0]]
    for slot in range(1, group):
        route = [(p, p - p % group + (p + slot) % group) for p in range(count)]
        moved.append(lax.ppermute(blocks[slot], "rows", route))
    return moved


class Plan:
    def __init__(self, rows_axis, feat_axis, gradients, bin_words, children):
        self.devices = rows_axis
        self.half = rows_axis // 2
        self.row_dev, self.outs = gradients.shape
        self.words = bin_words.shape[0]
        self.feats = 2 * self.words
        self.levels = children.shape[0]
        self.leaves = 2 ** (self.levels - 1)
        self.slots = round_up(self.row_dev * 3 // 4, LANES)
        self.shares = self.half // OUT_SPLIT
        self.share = self.feats // self.shares
        self.outs_dev = self.outs // OUT_SPLIT
        self.pair = 2 if feat_axis % 2 == 0 else 1
        self.outs_sent = self.outs_dev // self.pair
        self.grad_at = self.share
        self.misc_at = self.share + self.outs_sent
        self.score_rows = 2 * self.levels + 1
        self.spans = self.slots // LANES
        self.misc_rows = 2 + -(-self.score_rows * PIECES // self.spans)
        self.sent_rows = round_up(self.misc_at + self.misc_rows, 8)
        self.sizes = [self.devices >> (level + 1) for level in range(self.levels)]
        self.returned = [self.feats // size for size in self.sizes]
        self.needed = [min(self.share, count) for count in self.returned]
        self.block = min(self.needed)
        self.step = min(8, self.share)
        self.tiles = [
            (start + k, start + k + self.block // 2)
            for start in range(0, self.share, self.block)
            for k in range(self.block // 2)
        ]
        self.level_at = [sum(self.needed[:level]) // 2 for level in range(self.levels)]
        self.gain_rows = sum(self.needed) // 2
        self.message = round_up(self.gain_rows, 8)
        self.ends = [(level, n) for level in reversed(range(self.levels)) for n in range(2**level)]
        self.permuted = self.devices <= PERMUTED
        self.messages = self.half if self.permuted else 1
        self.parcels = self.devices if self.permuted else 1

    def code_row(self, feature):
        return feature // 2 + (feature % 2) * (self.share // 2)


def prep_kernel(plan, *refs):
    inputs, send_refs, refs = refs[:6], refs[6 : 6 + plan.parcels], refs[6 + plan.parcels :]
    fetched, (masks, table, packed, lines, sems) = refs[:6], refs[6:]
    copies = [
        pltpu.make_async_copy(source, target, sems.at[i])
        for i, (source, target) in enumerate(zip(inputs, fetched, strict=True))
    ]
    for copy in copies:
        copy.start()
    rows = plan.row_dev
    panel = lax.axis_index("feat")
    sent = OUT_SPLIT * plan.outs_sent
    low_at, high_at, own_at = sent, sent + plan.words, sent + plan.feats
    at = lax.broadcasted_iota(jnp.int32, (sent, plan.outs), 0)
    wanted = at + (at // plan.outs_sent) * (plan.outs_dev - plan.outs_sent) + lax.rem(panel, plan.pair) * plan.outs_sent
    turn = jnp.where(wanted == lax.broadcasted_iota(jnp.int32, (sent, plan.outs), 1), 1.0, 0.0).astype(bf16)
    ahead = jnp.where(
        lax.broadcasted_iota(jnp.int32, (rows, rows), 0) <= lax.broadcasted_iota(jnp.int32, (rows, rows), 1), 1.0, 0.0
    ).astype(bf16)
    for copy in copies:
        copy.wait()
    grad_ref, hess_ref, word_ref, child_ref, feature_ref, bin_ref = fetched
    grads = grad_ref[...]
    hess = hess_ref[...].astype(f32).reshape(1, rows)
    words = word_ref[...]
    low = jnp.bitwise_and(words, 63)
    high = jnp.bitwise_and(jnp.right_shift(words, 6), 63)
    codes = (low.astype(f32), high.astype(f32))
    nodes = [child_ref[0:1, :]]
    for level in range(1, plan.levels):
        nodes.append(nodes[-1] * 2 + child_ref[level : level + 1, :])

    table[0:low_at] = lax.dot_general(turn, grads, NT, preferred_element_type=f32).astype(bf16)
    table[low_at:high_at] = low.astype(f32).astype(bf16)
    table[high_at:own_at] = high.astype(f32).astype(bf16)
    at = lax.broadcasted_iota(jnp.int32, (TILE, rows), 0)
    leaf = jnp.bitwise_and(nodes[-1], plan.leaves - 1).astype(f32)
    table[own_at:] = jnp.where(at == 0, hess, jnp.where(at == 1, leaf, 0.0)).astype(bf16)
    side = jnp.where(at == nodes[0], 1.0, 0.0)
    rank = jnp.dot(side.astype(bf16), ahead, preferred_element_type=f32)
    slot = jnp.where(side > 0.0, rank - 1.0, -1.0)
    slot_ids = lax.broadcasted_iota(jnp.int32, (plan.slots, rows), 0).astype(f32)
    for half in range(2):
        chosen = jnp.where(slot_ids == slot[half : half + 1], 1.0, 0.0).astype(bf16)
        packed[half] = lax.dot_general(table[...], chosen, NT, preferred_element_type=f32)

    masks[...] = jnp.zeros_like(masks)
    leaf_count = 2 * plan.leaves
    for level in range(plan.levels):
        for node in range(2 ** (level + 1)):
            slot = 2 ** (level + 1) - 2 + node
            feature = feature_ref[slot]
            inner = feature - panel * plan.feats
            owned = jnp.logical_and(inner >= 0, inner < plan.feats)
            inner = jnp.clip(inner, 0, plan.feats - 1)
            word = word_ref[pl.ds(inner // 2, 1), :]
            code = jnp.bitwise_and(jnp.right_shift(word, 6 * lax.rem(inner, 2)), 63)
            here = jnp.where(nodes[level] == node, jnp.where(owned, 1.0, 0.0), 0.0)
            left = jnp.where(code <= bin_ref[slot], here, 0.0)
            right = here - left
            under = 2 ** (plan.levels - level - 1)
            for leaf in range(node * under, (node + 1) * under):
                masks[leaf * 8 + level : leaf * 8 + level + 1, :] = left
                at_right = leaf * 8 + plan.levels + level
                masks[at_right : at_right + 1, :] = right
    mask = masks[...]
    sums = jnp.dot(mask.astype(bf16), grads, preferred_element_type=f32)
    curv = jnp.sum(mask * hess, axis=1, keepdims=True)
    shape = (leaf_count * 8, plan.outs)
    line = jnp.bitwise_and(lax.broadcasted_iota(jnp.int32, shape, 0), 7)
    lane = lax.broadcasted_iota(jnp.int32, shape, 1)
    spread = jnp.where(lane == line, curv, 0.0).reshape(leaf_count, 8, plan.outs)
    spread = jnp.broadcast_to(jnp.sum(spread, axis=1, keepdims=True), spread.shape)
    sums = jnp.where(line == 2 * plan.levels, spread.reshape(shape), sums)
    pieces = []
    for _ in range(PIECES):
        pieces.append(sums.astype(bf16).astype(f32))
        sums = sums - pieces[-1]

    word_share = plan.share // 2
    blank = jnp.zeros((1, LANES), f32)
    filler = jnp.zeros((plan.sent_rows - plan.misc_at - plan.misc_rows, plan.slots), f32)
    for leaf in range(leaf_count):
        parts = [piece[leaf * 8 + i : leaf * 8 + i + 1] for i in range(plan.score_rows) for piece in pieces]
        parts += [blank] * (-len(parts) % plan.spans)
        parts = [jnp.concatenate(parts[i : i + plan.spans], axis=1) for i in range(0, len(parts), plan.spans)]
        lines[leaf] = jnp.concatenate(parts + ([filler] if filler.shape[0] else []), axis=0)
    for slot in range(plan.devices):
        device = target(lax.axis_index("rows"), slot, plan.devices) if plan.permuted else slot
        half, place = div(device, plan.half), rem(device, plan.half)
        share, split = div(place, OUT_SPLIT), rem(place, OUT_SPLIT)
        from_low = aligned(low_at + share * word_share, word_share)
        from_high = aligned(high_at + share * word_share, word_share)
        message = jnp.concatenate(
            [
                packed[half, pl.ds(from_low, word_share), :],
                packed[half, pl.ds(from_high, word_share), :],
                packed[half, pl.ds(aligned(split * plan.outs_sent, plan.outs_sent), plan.outs_sent), :],
                packed[half, own_at : own_at + 2, :],
                lines[div(device, plan.devices // leaf_count)],
            ],
            axis=0,
        ).astype(bf16)
        if plan.permuted:
            send_refs[slot][...] = message
        else:
            send_refs[0][slot] = message


def main_kernel(plan, chunk, *refs):
    got_refs, refs = refs[: plan.parcels], refs[plan.parcels :]
    others, refs = refs[: plan.pair - 1], refs[plan.pair - 1 :]
    out_refs, (weighted, gain_table, left_sums) = refs[: plan.messages], refs[plan.messages :]
    rows = plan.slots
    leaves, outs_dev, step = plan.leaves, plan.outs_dev, plan.step
    hess_at = leaves * outs_dev
    order = [feature for tile in plan.tiles for feature in tile]
    level_bins = lax.broadcasted_iota(jnp.int32, (BINS, rows), 0).astype(f32).astype(bf16)
    leaf_ids = lax.broadcasted_iota(jnp.int32, (TILE, rows), 0).astype(f32)
    zero = jnp.zeros((), bf16)
    one = jnp.ones((), bf16)

    def parcel(source):
        return got_refs[source] if plan.permuted else got_refs[0].at[source]

    def marked(source, feature):
        row = plan.code_row(feature)
        code = jnp.broadcast_to(parcel(source)[row : row + 1, :], (BINS, rows))
        return jnp.where(code <= level_bins, one, zero)

    def add_chunk(first, fresh):
        for k in range(chunk):
            source = first + k
            columns = slice(k * rows, (k + 1) * rows)
            misc = parcel(source)[plan.misc_at : plan.misc_at + 2, :].astype(f32)
            hess, node = misc[0:1], misc[1:2]
            weighted[hess_at : hess_at + TILE, columns] = jnp.where(leaf_ids == node, hess, 0.0).astype(bf16)
            node_wide = jnp.broadcast_to(node, (plan.outs_sent, rows)).astype(bf16)
            grads_parts = [parcel(source)[plan.grad_at : plan.grad_at + plan.outs_sent, :]]
            grads_parts += [ref[source] for ref in others]
            for place, grads in enumerate(grads_parts):
                for leaf in range(leaves):
                    at = leaf * outs_dev + place * plan.outs_sent
                    weighted[at : at + plan.outs_sent, columns] = jnp.where(
                        node_wide == jnp.asarray(leaf, bf16), grads, zero
                    )
        for group in range(plan.share // step):
            features = order[group * step : (group + 1) * step]
            marks = jnp.concatenate(
                [
                    jnp.concatenate([marked(first + k, feature) for feature in features], axis=0)
                    for k in range(chunk)
                ],
                axis=1,
            )
            part = lax.dot_general(weighted[...], marks, NT, preferred_element_type=f32)
            span = slice(group * step * BINS, (group + 1) * step * BINS)
            if count == 1:
                add_gains(group, part)
            elif fresh:
                left_sums[:, span] = part
            else:
                left_sums[:, span] += part

    known = []

    def add_gains(group, sums):
        left = [sums[leaf * outs_dev : (leaf + 1) * outs_dev] for leaf in range(leaves)]
        hess = [sums[hess_at + leaf : hess_at + leaf + 1] for leaf in range(leaves)]
        for level in reversed(range(plan.levels - 1)):
            past = len(left) - 2 ** (level + 1)
            for n in range(past, len(left), 2):
                left.append(left[n] + left[n + 1])
                hess.append(hess[n] + hess[n + 1])
        hess = jnp.concatenate(hess, axis=0) + penalty
        if not known:
            totals = [part[:, BINS - 1 : BINS] for part in left]
            squares = jnp.concatenate([jnp.sum(t * t, axis=0, keepdims=True) for t in totals], axis=0)
            hess_total = hess[:, BINS - 1 : BINS] + penalty
            known.extend([totals, hess_total, squares / (hess_total - penalty)])
        totals, hess_total, whole_part = known
        on_left = jnp.concatenate([jnp.sum(part * part, axis=0, keepdims=True) for part in left], axis=0)
        rights = [t - part for t, part in zip(totals, left, strict=True)]
        on_right = jnp.concatenate([jnp.sum(part * part, axis=0, keepdims=True) for part in rights], axis=0)
        gains = (on_left / hess + on_right / (hess_total - hess) - whole_part) / plan.outs
        for end in range(len(plan.ends)):
            for tile in range(step // 2):
                at = group * (step // 2) + tile
                gain_table[end, at : at + 1, :] = gains[end : end + 1, tile * LANES : (tile + 1) * LANES]

    count = plan.devices // chunk
    add_chunk(0, True)
    if count > 1:
        lax.fori_loop(1, count, lambda c, _: (add_chunk(c * chunk, False), 0)[1], 0)
        for group in range(plan.share // step):
            add_gains(group, left_sums[:, group * step * BINS : (group + 1) * step * BINS])
    me = rem(lax.axis_index("rows"), plan.half)
    for slot in range(plan.half):
        place = target(me, slot, plan.half) if plan.permuted else slot
        out_ref = out_refs[slot] if plan.permuted else out_refs[0].at[slot]
        for level in range(plan.levels):
            count = plan.needed[level] // 2
            end = plan.ends.index((level, 0)) + div(place, plan.sizes[level])
            first = rem(rem(place, plan.sizes[level]) * plan.returned[level], plan.share) // 2
            if not isinstance(first, int) and count % 8 == 0:
                first = pl.multiple_of(first, 8)
            at = plan.level_at[level]
            out_ref[at : at + count, :] = gain_table[end, pl.ds(first, count), :]
        if plan.message > plan.gain_rows:
            out_ref[plan.gain_rows :, :] = jnp.zeros((plan.message - plan.gain_rows, LANES), f32)


def score_kernel(plan, *refs):
    got_refs, (score_ref, grads_ref) = refs[: plan.parcels], refs[plan.parcels :]
    tail = slice(plan.misc_at + 2, plan.misc_at + plan.misc_rows)
    wanted = slice(plan.grad_at, plan.grad_at + plan.outs_sent)
    total = jnp.zeros((plan.misc_rows - 2, plan.slots), f32)
    if plan.permuted:
        for source, ref in enumerate(got_refs):
            grads_ref[source] = ref[wanted, :]
            total = total + ref[tail, :].astype(f32)
    else:
        grads_ref[...] = got_refs[0][:, wanted, :]
        total = lax.fori_loop(0, plan.devices, lambda k, sums: sums + got_refs[0][k, tail, :].astype(f32), total)
    score_ref[...] = jnp.zeros_like(score_ref)
    for i in range(plan.score_rows):
        value = 0.0
        for piece in reversed(range(PIECES)):
            line, span = divmod(i * PIECES + piece, plan.spans)
            value = value + total[line : line + 1, span * LANES : (span + 1) * LANES]
        score_ref[i : i + 1, :] = value


def final_kernel(plan, *refs):
    got_refs, refs = refs[: plan.messages], refs[plan.messages :]
    score_refs, refs = refs[: -plan.levels - 1], refs[-plan.levels - 1 :]
    *gain_refs, child_ref = refs
    me = rem(lax.axis_index("rows"), plan.half)
    side = plan.block // 2
    arrived = []
    for slot in range(plan.half):
        place = source_of(me, slot, plan.half) if plan.permuted else slot
        arrived.append((div(place, OUT_SPLIT), got_refs[slot] if plan.permuted else got_refs[0].at[slot]))
    for level, gain_ref in enumerate(gain_refs):
        rows = slice(plan.level_at[level], plan.level_at[level] + plan.needed[level] // 2)
        first = div(rem(me, plan.sizes[level]) * plan.returned[level], plan.share)
        for turn in range(plan.returned[level] // plan.needed[level]):
            value = 0.0
            for share, ref in arrived:
                value = value + jnp.where(share == first + turn, ref[rows, :], 0.0)
            for start in range(0, plan.needed[level], plan.block):
                part = value[start // 2 : start // 2 + side]
                at = turn * plan.share + start
                gain_ref[at : at + side, :] = part[:, :BINS]
                gain_ref[at + side : at + 2 * side, :] = part[:, BINS:]
    sums = score_refs[0][...]
    for score_ref in score_refs[1:]:
        sums = sums + score_ref[...]
    curv = sums[2 * plan.levels : 2 * plan.levels + 1, :]
    for level in range(plan.levels):
        for side in range(2):
            line = side * plan.levels + level
            scale = jnp.sqrt(curv[:, line : line + 1] + penalty)
            child_ref[level, 0, side : side + 1, :] = -sums[line : line + 1, :] / scale


def flipped(block, bits):
    count = lax.axis_size("feat")
    return lax.ppermute(block, "feat", [(p, p ^ bits) for p in range(count)])


def on_device(gradients, hessians, bin_words, children, split_feature, split_bin):
    plan = Plan(lax.axis_size("rows"), lax.axis_size("feat"), gradients, bin_words, children)
    params = pltpu.CompilerParams(vmem_limit_bytes=VMEM_BYTES)

    table_rows = OUT_SPLIT * plan.outs_sent + plan.feats + TILE
    inputs = (gradients, hessians, bin_words, children, split_feature, split_bin)
    inputs = tuple(pltpu.with_memory_space_constraint(a, pltpu.HBM) for a in inputs)
    parcel = (plan.sent_rows, plan.slots) if plan.permuted else (plan.devices, plan.sent_rows, plan.slots)
    parcels = pl.pallas_call(
        functools.partial(prep_kernel, plan),
        out_shape=[jax.ShapeDtypeStruct(parcel, bf16)] * plan.parcels,
        in_specs=[pl.BlockSpec(memory_space=pltpu.HBM)] * len(inputs),
        out_specs=[whole()] * plan.parcels,
        scratch_shapes=[
            *(pltpu.VMEM(a.shape, a.dtype) for a in inputs[:4]),
            *(pltpu.SMEM(a.shape, a.dtype) for a in inputs[4:]),
            pltpu.VMEM((2 * plan.leaves * 8, plan.row_dev), f32),
            pltpu.VMEM((table_rows, plan.row_dev), bf16),
            pltpu.VMEM((2, table_rows, plan.slots), f32),
            pltpu.VMEM((2 * plan.leaves, plan.sent_rows - plan.misc_at - 2, plan.slots), f32),
            pltpu.SemaphoreType.DMA((len(inputs),)),
        ],
        compiler_params=params,
        name="prep",
    )(*inputs)

    if plan.permuted:
        got = exchanged(parcels, plan.devices, plan.devices)
    else:
        got = [lax.all_to_all(parcels[0], "rows", 0, 0)]
    scores, grads_part = pl.pallas_call(
        functools.partial(score_kernel, plan),
        out_shape=(
            jax.ShapeDtypeStruct((8, plan.outs), f32),
            jax.ShapeDtypeStruct((plan.devices, plan.outs_sent, plan.slots), bf16),
        ),
        in_specs=[whole()] * plan.parcels,
        out_specs=(whole(), whole()),
        compiler_params=params,
        name="scores",
    )(*got)
    arrays = got + ([flipped(grads_part, 1)] if plan.pair > 1 else [])
    score_parts = [scores] + [flipped(scores, away) for away in range(1, lax.axis_size("feat"))]

    chunk = max(1, min(plan.devices, 4096 // plan.slots))
    while plan.devices % chunk:
        chunk -= 1
    sums_rows = plan.leaves * plan.outs_dev + TILE
    block = (plan.message, LANES) if plan.permuted else (plan.half, plan.message, LANES)
    messages = pl.pallas_call(
        functools.partial(main_kernel, plan, chunk),
        out_shape=[jax.ShapeDtypeStruct(block, f32)] * plan.messages,
        in_specs=[whole()] * len(arrays),
        out_specs=[whole()] * plan.messages,
        scratch_shapes=[
            pltpu.VMEM((sums_rows, chunk * plan.slots), bf16),
            pltpu.VMEM((len(plan.ends), plan.share // 2, LANES), f32),
            pltpu.VMEM((sums_rows, plan.share * BINS), f32),
        ],
        cost_estimate=pl.CostEstimate(
            flops=2 * sums_rows * plan.devices * plan.slots * plan.share * BINS,
            bytes_accessed=4 * plan.devices * plan.sent_rows * plan.slots,
            transcendentals=0,
        ),
        compiler_params=params,
        name="gains",
    )(*arrays)

    messages, score_parts = lax.optimization_barrier((list(messages), score_parts))
    if plan.permuted:
        messages = exchanged(messages, plan.half, plan.devices)
    else:
        halves = [list(range(plan.half)), list(range(plan.half, plan.devices))]
        messages = [lax.all_to_all(messages[0], "rows", 0, 0, axis_index_groups=halves)]
    shapes = [
        jax.ShapeDtypeStruct((count, BINS), f32) for count in plan.returned
    ]
    shapes.append(jax.ShapeDtypeStruct((plan.levels, 1, 2, plan.outs), f32))
    return pl.pallas_call(
        functools.partial(final_kernel, plan),
        out_shape=tuple(shapes),
        in_specs=[whole()] * (plan.messages + len(score_parts)),
        out_specs=tuple(whole() for _ in shapes),
        compiler_params=params,
        name="finish",
    )(*messages, *score_parts)


def solution(mesh):
    placed = (P("rows", None), P("rows"), P("feat", "rows"), P(None, "rows"), P(), P())
    return jax.shard_map(
        on_device,
        mesh=mesh,
        in_specs=placed,
        out_specs=(
            P("rows", "feat"),
            P("rows", "feat"),
            P("rows", "feat"),
            P(None, "rows", None, None),
        ),
        check_vma=False,
    )
```

```python
import functools

import jax
import jax.numpy as jnp
from jax import lax
from jax.experimental import pallas as pl
from jax.experimental.pallas import tpu as pltpu
from jax.sharding import PartitionSpec as P

BINS = 64
LANES = 128
TILE = 16
OUT_SPLIT = 2
PIECES = 2
penalty = 1.0
VMEM_BYTES = 32 * 2**20

bf16 = jnp.bfloat16
f32 = jnp.float32
NT = (((1,), (1,)), ((), ()))
PERMUTED = 8


def div(value, by):
    return value // by if isinstance(value, int) else lax.div(value, jnp.int32(by))


def rem(value, by):
    return value % by if isinstance(value, int) else lax.rem(value, jnp.int32(by))


def round_up(value, unit):
    return -(-value // unit) * unit


def whole(*_):
    return pl.BlockSpec(memory_space=pltpu.VMEM)


def aligned(value, unit):
    return value if isinstance(value, int) or unit % 8 else pl.multiple_of(value, 8)


def target(me, slot, count):
    return rem(me + slot, count)


def source_of(me, slot, count):
    return rem(me + (count - slot), count)


def exchanged(blocks, group, count):
    moved = [blocks[0]]
    for slot in range(1, group):
        route = [(p, p - p % group + (p + slot) % group) for p in range(count)]
        moved.append(lax.ppermute(blocks[slot], "rows", route))
    return moved


def spread(parcels, plan):
    feat_axis = lax.axis_size("feat")
    moved = []
    for slot, block in enumerate(parcels):
        route = []
        for p in range(plan.devices * feat_axis):
            row, panel = divmod(p, feat_axis)
            row = (row + 2 * slot + 2 - panel % 2) % plan.devices
            route.append((p, row * feat_axis + panel))
        moved.append(lax.ppermute(block, ("rows", "feat"), route))
    return moved


class Plan:
    def __init__(self, rows_axis, feat_axis, gradients, bin_words, children):
        self.devices = rows_axis
        self.half = rows_axis // 2
        self.row_dev, self.outs = gradients.shape
        self.words = bin_words.shape[0]
        self.feats = 2 * self.words
        self.levels = children.shape[0]
        self.leaves = 2 ** (self.levels - 1)
        self.slots = round_up(self.row_dev * 3 // 4, LANES)
        self.shares = self.half // OUT_SPLIT
        self.share = self.feats // self.shares
        self.outs_dev = self.outs // OUT_SPLIT
        self.permuted = rows_axis <= PERMUTED and feat_axis % 2 == 0
        self.panels = 2 if self.permuted else 1
        self.parcels = rows_axis // 2 if self.permuted else 1
        self.codes = self.panels * self.feats
        self.splits = 2 ** (self.levels + 1) - 2
        self.split_rows = round_up(self.splits, TILE)
        self.grad_at = self.share
        self.misc_at = self.share + self.outs_dev
        self.score_rows = 2 * self.levels + 1
        self.spans = self.slots // LANES
        self.misc_rows = 2 + -(-self.score_rows * PIECES // self.spans)
        self.base_rows = round_up(self.misc_at + self.misc_rows, 8)
        self.sent_rows = self.base_rows + (self.panels - 1) * self.share
        self.sizes = [self.devices >> (level + 1) for level in range(self.levels)]
        self.returned = [self.feats // size for size in self.sizes]
        self.needed = [min(self.share, count) for count in self.returned]
        self.block = min(self.needed)
        self.step = min(8, self.share)
        self.tiles = [
            (start + k, start + k + self.block // 2)
            for start in range(0, self.share, self.block)
            for k in range(self.block // 2)
        ]
        self.level_at = [sum(self.needed[:level]) // 2 for level in range(self.levels)]
        self.gain_rows = sum(self.needed) // 2
        self.message = round_up(self.gain_rows, 8)
        self.ends = [(level, n) for level in reversed(range(self.levels)) for n in range(2**level)]
        self.messages = self.half if self.permuted else 1

    def code_row(self, feature):
        return feature // 2 + (feature % 2) * (self.share // 2)


def fetch_kernel(plan, *refs):
    inputs, refs = refs[:6], refs[6:]
    (grad_ref, word_ref, row_ref, pick_ref, chosen_ref), (hess_ref, child_ref, feature_ref, bin_ref, sems) = refs[:5], refs[5:]
    targets = (grad_ref, hess_ref, child_ref, feature_ref, bin_ref, word_ref)
    copies = [
        pltpu.make_async_copy(source, into, sems.at[i])
        for i, (source, into) in enumerate(zip(inputs, targets, strict=True))
    ]
    for copy in copies:
        copy.start()
    rows = plan.row_dev
    ahead = jnp.where(
        lax.broadcasted_iota(jnp.int32, (rows, rows), 0) <= lax.broadcasted_iota(jnp.int32, (rows, rows), 1), 1.0, 0.0
    ).astype(bf16)
    for copy in copies:
        copy.wait()

    nodes = [child_ref[0:1, :]]
    for level in range(1, plan.levels):
        nodes.append(nodes[-1] * 2 + child_ref[level : level + 1, :])
    row_ref[...] = jnp.zeros_like(row_ref)
    row_ref[0:1, :] = hess_ref[...].astype(f32).reshape(1, rows)
    for level, node in enumerate(nodes):
        row_ref[level + 1 : level + 2, :] = node.astype(f32)

    at = lax.broadcasted_iota(jnp.int32, (TILE, rows), 0)
    side = jnp.where(at == nodes[0], 1.0, 0.0)
    rank = jnp.dot(side.astype(bf16), ahead, preferred_element_type=f32)
    slot = jnp.where(side > 0.0, rank - 1.0, -1.0)
    slot_ids = lax.broadcasted_iota(jnp.int32, (plan.slots, rows), 0).astype(f32)
    for half in range(2):
        chosen_ref[half] = jnp.where(slot_ids == slot[half : half + 1], 1.0, 0.0).astype(bf16)

    panel = lax.axis_index("feat")
    lane = lax.broadcasted_iota(jnp.int32, (1, plan.codes), 1)
    pick_ref[...] = jnp.zeros_like(pick_ref)
    for slot in range(plan.splits):
        feature = feature_ref[slot]
        owner = lax.div(feature, jnp.int32(plan.feats))
        inner = feature - owner * plan.feats
        held = jnp.bitwise_xor(owner, panel)
        place = held * plan.words + inner // 2 + lax.rem(inner, 2) * (plan.panels * plan.words)
        place = jnp.where(held < plan.panels, place, plan.codes)
        pick_ref[0, slot : slot + 1, :] = jnp.where(lane == place, 1.0, 0.0)
        pick_ref[1, slot : slot + 1, :] = jnp.full((1, plan.codes), bin_ref[slot].astype(f32))
        pick_ref[2, slot : slot + 1, :] = jnp.full((1, plan.codes), jnp.where(held < plan.panels, 1.0, 0.0))


def prep_kernel(plan, *refs):
    (grad_ref, row_ref, pick_ref, chosen_ref), refs = refs[:4], refs[4:]
    word_refs, send_refs = refs[: plan.panels], refs[plan.panels : plan.panels + plan.parcels]
    table, packed, lines, marked = refs[plan.panels + plan.parcels :]
    rows = plan.row_dev
    low_at, high_at = plan.outs, plan.outs + plan.panels * plan.words
    own_at = plan.outs + plan.codes
    grads = grad_ref[...]
    hess = row_ref[0:1, :]
    nodes = [row_ref[level + 1 : level + 2, :] for level in range(plan.levels)]

    turn = jnp.where(
        lax.broadcasted_iota(jnp.int32, (plan.outs, plan.outs), 0)
        == lax.broadcasted_iota(jnp.int32, (plan.outs, plan.outs), 1),
        1.0,
        0.0,
    ).astype(bf16)
    table[0:low_at] = lax.dot_general(turn, grads, NT, preferred_element_type=f32).astype(bf16)
    for which, word_ref in enumerate(word_refs):
        words = word_ref[...]
        low = jnp.bitwise_and(words, 63)
        high = jnp.bitwise_and(jnp.right_shift(words, 6), 63)
        for first, codes in ((low_at, low), (high_at, high)):
            at = first + which * plan.words
            table[at : at + plan.words] = codes.astype(f32).astype(bf16)
    at = lax.broadcasted_iota(jnp.int32, (TILE, rows), 0)
    leaf = nodes[-1] - nodes[0] * plan.leaves
    table[own_at:] = jnp.where(at == 0, hess, jnp.where(at == 1, leaf, 0.0)).astype(bf16)
    for half in range(2):
        packed[half] = lax.dot_general(table[...], chosen_ref[half], NT, preferred_element_type=f32)

    ends = [(level, node) for level in range(plan.levels) for node in range(2 ** (level + 1))]
    code = jnp.dot(pick_ref[0].astype(bf16), table[low_at:own_at], preferred_element_type=f32)
    marked[...] = jnp.zeros_like(marked)
    for slot, (level, node) in enumerate(ends):
        here = jnp.where(nodes[level] == node, pick_ref[2, slot : slot + 1, 0:1], 0.0)
        left = jnp.where(code[slot : slot + 1] <= pick_ref[1, slot : slot + 1, 0:1], here, 0.0)
        marked[slot : slot + 1, :] = left
        marked[plan.split_rows + slot : plan.split_rows + slot + 1, :] = here - left
    mark = marked[...]
    sums = jnp.dot(mark.astype(bf16), grads, preferred_element_type=f32)
    curv = jnp.sum(mark * hess, axis=1, keepdims=True)
    shape = (2 * plan.split_rows, plan.outs)
    curv = jnp.broadcast_to(curv, shape)
    lane = lax.broadcasted_iota(jnp.int32, (1, plan.outs), 1)
    blank = jnp.zeros((1, LANES), f32)
    filler = jnp.zeros((plan.base_rows - plan.misc_at - plan.misc_rows, plan.slots), f32)
    for leaf in range(2 * plan.leaves):
        places = [
            side * plan.split_rows + 2 ** (level + 1) - 2 + (leaf >> (plan.levels - 1 - level))
            for side in range(2)
            for level in range(plan.levels)
        ]
        spread_curv = jnp.zeros((1, plan.outs), f32)
        for i, at in enumerate(places):
            spread_curv = jnp.where(lane == i, curv[at : at + 1], spread_curv)
        parts = []
        for value in [*(sums[at : at + 1] for at in places), spread_curv]:
            for _ in range(PIECES):
                parts.append(value.astype(bf16).astype(f32))
                value = value - parts[-1]
        parts += [blank] * (-len(parts) % plan.spans)
        parts = [jnp.concatenate(parts[i : i + plan.spans], axis=1) for i in range(0, len(parts), plan.spans)]
        lines[leaf] = jnp.concatenate(parts + ([filler] if filler.shape[0] else []), axis=0)

    word_share = plan.share // 2
    parity = rem(lax.axis_index("feat"), plan.panels)
    for slot in range(plan.parcels if plan.permuted else plan.devices):
        device = slot
        if plan.permuted:
            device = rem(lax.axis_index("rows") + 2 * slot + 2 - parity, plan.devices)
        half, place = div(device, plan.half), rem(device, plan.half)
        share, split = div(place, OUT_SPLIT), rem(place, OUT_SPLIT)

        def codes(which):
            at = [first + which * plan.words + share * word_share for first in (low_at, high_at)]
            return [packed[half, pl.ds(aligned(first, word_share), word_share), :] for first in at]

        message = [
            *codes(0),
            packed[half, pl.ds(aligned(split * plan.outs_dev, plan.outs_dev), plan.outs_dev), :],
            packed[half, own_at : own_at + 2, :],
            lines[div(device, plan.devices // (2 * plan.leaves))],
        ]
        if plan.permuted:
            send_refs[slot][...] = jnp.concatenate(message + codes(1), axis=0).astype(bf16)
        else:
            send_refs[0][slot] = jnp.concatenate(message, axis=0).astype(bf16)


def main_kernel(plan, chunk, *refs):
    got_refs, refs = refs[: plan.parcels], refs[plan.parcels :]
    others, refs = refs[: plan.panels - 1], refs[plan.panels - 1 :]
    out_refs, (weighted, gain_table, left_sums) = refs[: plan.messages], refs[plan.messages :]
    rows = plan.slots
    leaves, outs_dev, step = plan.leaves, plan.outs_dev, plan.step
    hess_at = leaves * outs_dev
    order = [feature for tile in plan.tiles for feature in tile]
    level_bins = lax.broadcasted_iota(jnp.int32, (BINS, rows), 0).astype(f32).astype(bf16)
    leaf_ids = lax.broadcasted_iota(jnp.int32, (TILE, rows), 0).astype(f32)
    zero = jnp.zeros((), bf16)
    one = jnp.ones((), bf16)

    def parcel(source):
        if not plan.permuted:
            return got_refs[0].at[source]
        return got_refs[source] if source < plan.parcels else others[0].at[source - plan.parcels]

    def marked(source, feature):
        row = plan.code_row(feature)
        code = jnp.broadcast_to(parcel(source)[row : row + 1, :], (BINS, rows))
        return jnp.where(code <= level_bins, one, zero)

    def add_chunk(first, fresh):
        for k in range(chunk):
            source = first + k
            columns = slice(k * rows, (k + 1) * rows)
            misc = parcel(source)[plan.misc_at : plan.misc_at + 2, :].astype(f32)
            hess, node = misc[0:1], misc[1:2]
            weighted[hess_at : hess_at + TILE, columns] = jnp.where(leaf_ids == node, hess, 0.0).astype(bf16)
            node_wide = jnp.broadcast_to(node, (outs_dev, rows)).astype(bf16)
            grads = parcel(source)[plan.grad_at : plan.grad_at + outs_dev, :]
            for leaf in range(leaves):
                weighted[leaf * outs_dev : (leaf + 1) * outs_dev, columns] = jnp.where(
                    node_wide == jnp.asarray(leaf, bf16), grads, zero
                )
        for group in range(plan.share // step):
            features = order[group * step : (group + 1) * step]
            marks = jnp.concatenate(
                [
                    jnp.concatenate([marked(first + k, feature) for feature in features], axis=0)
                    for k in range(chunk)
                ],
                axis=1,
            )
            part = lax.dot_general(weighted[...], marks, NT, preferred_element_type=f32)
            span = slice(group * step * BINS, (group + 1) * step * BINS)
            if count == 1:
                add_gains(group, part)
            elif fresh:
                left_sums[:, span] = part
            else:
                left_sums[:, span] += part

    known = []

    def add_gains(group, sums):
        left = [sums[leaf * outs_dev : (leaf + 1) * outs_dev] for leaf in range(leaves)]
        hess = [sums[hess_at + leaf : hess_at + leaf + 1] for leaf in range(leaves)]
        for level in reversed(range(plan.levels - 1)):
            past = len(left) - 2 ** (level + 1)
            for n in range(past, len(left), 2):
                left.append(left[n] + left[n + 1])
                hess.append(hess[n] + hess[n + 1])
        hess = jnp.concatenate(hess, axis=0) + penalty
        if not known:
            totals = [part[:, BINS - 1 : BINS] for part in left]
            squares = jnp.concatenate([jnp.sum(t * t, axis=0, keepdims=True) for t in totals], axis=0)
            hess_total = hess[:, BINS - 1 : BINS] + penalty
            known.extend([totals, hess_total, squares / (hess_total - penalty)])
        totals, hess_total, whole_part = known
        on_left = jnp.concatenate([jnp.sum(part * part, axis=0, keepdims=True) for part in left], axis=0)
        rights = [t - part for t, part in zip(totals, left, strict=True)]
        on_right = jnp.concatenate([jnp.sum(part * part, axis=0, keepdims=True) for part in rights], axis=0)
        gains = (on_left / hess + on_right / (hess_total - hess) - whole_part) / plan.outs
        for end in range(len(plan.ends)):
            for tile in range(step // 2):
                at = group * (step // 2) + tile
                gain_table[end, at : at + 1, :] = gains[end : end + 1, tile * LANES : (tile + 1) * LANES]

    count = plan.devices // chunk
    add_chunk(0, True)
    if count > 1:
        lax.fori_loop(1, count, lambda c, _: (add_chunk(c * chunk, False), 0)[1], 0)
        for group in range(plan.share // step):
            add_gains(group, left_sums[:, group * step * BINS : (group + 1) * step * BINS])
    me = rem(lax.axis_index("rows"), plan.half)
    for slot in range(plan.half):
        place = target(me, slot, plan.half) if plan.permuted else slot
        out_ref = out_refs[slot] if plan.permuted else out_refs[0].at[slot]
        for level in range(plan.levels):
            count = plan.needed[level] // 2
            end = plan.ends.index((level, 0)) + div(place, plan.sizes[level])
            first = rem(rem(place, plan.sizes[level]) * plan.returned[level], plan.share) // 2
            if not isinstance(first, int) and count % 8 == 0:
                first = pl.multiple_of(first, 8)
            at = plan.level_at[level]
            out_ref[at : at + count, :] = gain_table[end, pl.ds(first, count), :]
        if plan.message > plan.gain_rows:
            out_ref[plan.gain_rows :, :] = jnp.zeros((plan.message - plan.gain_rows, LANES), f32)


def score_kernel(plan, *refs):
    got_refs, (score_ref, *passed) = refs[: plan.parcels], refs[plan.parcels :]
    tail = slice(plan.misc_at + 2, plan.misc_at + plan.misc_rows)
    total = jnp.zeros((plan.misc_rows - 2, plan.slots), f32)
    if plan.permuted:
        for source, ref in enumerate(got_refs):
            passed[0][source, : plan.share] = ref[plan.base_rows :, :]
            passed[0][source, plan.share :] = ref[plan.share : plan.base_rows, :]
            total = total + ref[tail, :].astype(f32)
    else:
        total = lax.fori_loop(0, plan.devices, lambda k, sums: sums + got_refs[0][k, tail, :].astype(f32), total)
    score_ref[...] = jnp.zeros_like(score_ref)
    for i in range(plan.score_rows):
        value = 0.0
        for piece in reversed(range(PIECES)):
            line, span = divmod(i * PIECES + piece, plan.spans)
            value = value + total[line : line + 1, span * LANES : (span + 1) * LANES]
        score_ref[i : i + 1, :] = value


def final_kernel(plan, *refs):
    got_refs, refs = refs[: plan.messages], refs[plan.messages :]
    score_refs, refs = refs[: -plan.levels - 1], refs[-plan.levels - 1 :]
    *gain_refs, child_ref = refs
    me = rem(lax.axis_index("rows"), plan.half)
    side = plan.block // 2
    arrived = []
    for slot in range(plan.half):
        place = source_of(me, slot, plan.half) if plan.permuted else slot
        arrived.append((div(place, OUT_SPLIT), got_refs[slot] if plan.permuted else got_refs[0].at[slot]))
    for level, gain_ref in enumerate(gain_refs):
        rows = slice(plan.level_at[level], plan.level_at[level] + plan.needed[level] // 2)
        first = div(rem(me, plan.sizes[level]) * plan.returned[level], plan.share)
        for turn in range(plan.returned[level] // plan.needed[level]):
            value = 0.0
            for share, ref in arrived:
                value = value + jnp.where(share == first + turn, ref[rows, :], 0.0)
            for start in range(0, plan.needed[level], plan.block):
                part = value[start // 2 : start // 2 + side]
                at = turn * plan.share + start
                gain_ref[at : at + side, :] = part[:, :BINS]
                gain_ref[at + side : at + 2 * side, :] = part[:, BINS:]
    sums = score_refs[0][...]
    for score_ref in score_refs[1:]:
        sums = sums + score_ref[...]
    curv = sums[2 * plan.levels : 2 * plan.levels + 1, :]
    for level in range(plan.levels):
        for side in range(2):
            line = side * plan.levels + level
            scale = jnp.sqrt(curv[:, line : line + 1] + penalty)
            child_ref[level, 0, side : side + 1, :] = -sums[line : line + 1, :] / scale


def flipped(block, bits):
    count = lax.axis_size("feat")
    return lax.ppermute(block, "feat", [(p, p ^ bits) for p in range(count)])


def on_device(gradients, hessians, bin_words, children, split_feature, split_bin):
    plan = Plan(lax.axis_size("rows"), lax.axis_size("feat"), gradients, bin_words, children)
    params = pltpu.CompilerParams(vmem_limit_bytes=VMEM_BYTES)

    inputs = (gradients, hessians, children, split_feature, split_bin, bin_words)
    crossed = [flipped(bin_words, 1)] if plan.permuted else []
    row_dev, table_rows = plan.row_dev, plan.outs + plan.codes + TILE
    grads, words, row_values, picks, chosen = pl.pallas_call(
        functools.partial(fetch_kernel, plan),
        out_shape=(
            jax.ShapeDtypeStruct(gradients.shape, bf16),
            jax.ShapeDtypeStruct(bin_words.shape, jnp.int32),
            jax.ShapeDtypeStruct((8, row_dev), f32),
            jax.ShapeDtypeStruct((3, plan.split_rows, plan.codes), f32),
            jax.ShapeDtypeStruct((2, plan.slots, row_dev), bf16),
        ),
        in_specs=[pl.BlockSpec(memory_space=pltpu.HBM)] * len(inputs),
        out_specs=[whole()] * 5,
        scratch_shapes=[
            pltpu.VMEM(hessians.shape, bf16),
            pltpu.VMEM(children.shape, jnp.int32),
            pltpu.SMEM(split_feature.shape, jnp.int32),
            pltpu.SMEM(split_bin.shape, jnp.int32),
            pltpu.SemaphoreType.DMA((len(inputs),)),
        ],
        cost_estimate=pl.CostEstimate(flops=10**9, bytes_accessed=10**6, transcendentals=0),
        compiler_params=params,
        name="fetch",
    )(*(pltpu.with_memory_space_constraint(a, pltpu.HBM) for a in inputs))
    parcel = (plan.sent_rows, plan.slots) if plan.permuted else (plan.devices, plan.sent_rows, plan.slots)
    parcels = pl.pallas_call(
        functools.partial(prep_kernel, plan),
        out_shape=[jax.ShapeDtypeStruct(parcel, bf16)] * plan.parcels,
        in_specs=[whole()] * (4 + plan.panels),
        out_specs=[whole()] * plan.parcels,
        scratch_shapes=[
            pltpu.VMEM((table_rows, row_dev), bf16),
            pltpu.VMEM((2, table_rows, plan.slots), f32),
            pltpu.VMEM((2 * plan.leaves, plan.base_rows - plan.misc_at - 2, plan.slots), f32),
            pltpu.VMEM((2 * plan.split_rows, row_dev), f32),
        ],
        compiler_params=params,
        name="prep",
    )(grads, row_values, picks, chosen, words, *crossed)

    shapes = [jax.ShapeDtypeStruct((8, plan.outs), f32)]
    if plan.permuted:
        got = spread(parcels, plan)
        shapes.append(jax.ShapeDtypeStruct((plan.parcels, plan.base_rows, plan.slots), bf16))
    else:
        got = [lax.all_to_all(parcels[0], "rows", 0, 0)]
    scores, *passed = pl.pallas_call(
        functools.partial(score_kernel, plan),
        out_shape=shapes,
        in_specs=[whole()] * plan.parcels,
        out_specs=[whole()] * len(shapes),
        compiler_params=params,
        name="scores",
    )(*got)
    arrays = got + [flipped(block, 1) for block in passed]
    score_parts = [scores] + [flipped(scores, away) for away in range(1, lax.axis_size("feat"))]

    chunk = max(1, min(plan.devices, 4096 // plan.slots))
    while plan.devices % chunk:
        chunk -= 1
    sums_rows = plan.leaves * plan.outs_dev + TILE
    block = (plan.message, LANES) if plan.permuted else (plan.half, plan.message, LANES)
    messages = pl.pallas_call(
        functools.partial(main_kernel, plan, chunk),
        out_shape=[jax.ShapeDtypeStruct(block, f32)] * plan.messages,
        in_specs=[whole()] * len(arrays),
        out_specs=[whole()] * plan.messages,
        scratch_shapes=[
            pltpu.VMEM((sums_rows, chunk * plan.slots), bf16),
            pltpu.VMEM((len(plan.ends), plan.share // 2, LANES), f32),
            pltpu.VMEM((sums_rows, plan.share * BINS), f32),
        ],
        cost_estimate=pl.CostEstimate(
            flops=2 * sums_rows * plan.devices * plan.slots * plan.share * BINS,
            bytes_accessed=4 * plan.devices * plan.sent_rows * plan.slots,
            transcendentals=0,
        ),
        compiler_params=params,
        name="gains",
    )(*arrays)

    messages, score_parts = lax.optimization_barrier((list(messages), score_parts))
    if plan.permuted:
        messages = exchanged(messages, plan.half, plan.devices)
    else:
        halves = [list(range(plan.half)), list(range(plan.half, plan.devices))]
        messages = [lax.all_to_all(messages[0], "rows", 0, 0, axis_index_groups=halves)]
    shapes = [
        jax.ShapeDtypeStruct((count, BINS), f32) for count in plan.returned
    ]
    shapes.append(jax.ShapeDtypeStruct((plan.levels, 1, 2, plan.outs), f32))
    return pl.pallas_call(
        functools.partial(final_kernel, plan),
        out_shape=tuple(shapes),
        in_specs=[whole()] * (plan.messages + len(score_parts)),
        out_specs=tuple(whole() for _ in shapes),
        compiler_params=params,
        name="finish",
    )(*messages, *score_parts)


def solution(mesh):
    placed = (P("rows", None), P("rows"), P("feat", "rows"), P(None, "rows"), P(), P())
    return jax.shard_map(
        on_device,
        mesh=mesh,
        in_specs=placed,
        out_specs=(
            P("rows", "feat"),
            P("rows", "feat"),
            P("rows", "feat"),
            P(None, "rows", None, None),
        ),
        check_vma=False,
    )
```

```python
import functools

import jax
import jax.numpy as jnp
from jax import lax
from jax.experimental import pallas as pl
from jax.experimental.pallas import tpu as pltpu
from jax.sharding import PartitionSpec as P

BINS = 64
LANES = 128
TILE = 16
OUT_SPLIT = 2
PIECES = 2
penalty = 1.0
VMEM_BYTES = 32 * 2**20

bf16 = jnp.bfloat16
f32 = jnp.float32
NT = (((1,), (1,)), ((), ()))
PERMUTED = 8


def div(value, by):
    return value // by if isinstance(value, int) else lax.div(value, jnp.int32(by))


def rem(value, by):
    return value % by if isinstance(value, int) else lax.rem(value, jnp.int32(by))


def round_up(value, unit):
    return -(-value // unit) * unit


def whole(*_):
    return pl.BlockSpec(memory_space=pltpu.VMEM)


def aligned(value, unit):
    return value if isinstance(value, int) or unit % 8 else pl.multiple_of(value, 8)


def target(me, slot, count):
    return rem(me + slot, count)


def source_of(me, slot, count):
    return rem(me + (count - slot), count)


def exchanged(blocks, group, count):
    moved = [blocks[0]]
    for slot in range(1, group):
        route = [(p, p - p % group + (p + slot) % group) for p in range(count)]
        moved.append(lax.ppermute(blocks[slot], "rows", route))
    return moved


def spread(parcels, plan):
    feat_axis = lax.axis_size("feat")
    moved = []
    for slot, block in enumerate(parcels):
        route = []
        for p in range(plan.devices * feat_axis):
            row, panel = divmod(p, feat_axis)
            row = (row + 2 * slot + 2 - panel % 2) % plan.devices
            route.append((p, row * feat_axis + panel))
        moved.append(lax.ppermute(block, ("rows", "feat"), route))
    return moved


class Plan:
    def __init__(self, rows_axis, feat_axis, gradients, bin_words, children):
        self.devices = rows_axis
        self.half = rows_axis // 2
        self.row_dev, self.outs = gradients.shape
        self.words = bin_words.shape[0]
        self.feats = 2 * self.words
        self.levels = children.shape[0]
        self.leaves = 2 ** (self.levels - 1)
        self.slots = round_up(self.row_dev * 3 // 4, LANES)
        self.shares = self.half // OUT_SPLIT
        self.share = self.feats // self.shares
        self.outs_dev = self.outs // OUT_SPLIT
        self.permuted = rows_axis <= PERMUTED and feat_axis % 2 == 0
        self.panels = 2 if self.permuted else 1
        self.parcels = rows_axis // 2 if self.permuted else 1
        self.codes = self.panels * self.feats
        self.splits = 2 ** (self.levels + 1) - 2
        self.split_rows = round_up(self.splits, TILE)
        self.grad_at = self.share
        self.misc_at = self.share + self.outs_dev
        self.score_rows = 2 * self.levels + 1
        self.spans = self.slots // LANES
        self.misc_rows = 2 + -(-self.score_rows * PIECES // self.spans)
        self.base_rows = round_up(self.misc_at + self.misc_rows, 8)
        self.sent_rows = self.base_rows + (self.panels - 1) * self.share
        self.sizes = [self.devices >> (level + 1) for level in range(self.levels)]
        self.returned = [self.feats // size for size in self.sizes]
        self.needed = [min(self.share, count) for count in self.returned]
        self.block = min(self.needed)
        self.step = min(8, self.share)
        self.tiles = [
            (start + k, start + k + self.block // 2)
            for start in range(0, self.share, self.block)
            for k in range(self.block // 2)
        ]
        self.level_at = [sum(self.needed[:level]) // 2 for level in range(self.levels)]
        self.gain_rows = sum(self.needed) // 2
        self.message = round_up(self.gain_rows, 8)
        self.ends = [(level, n) for level in reversed(range(self.levels)) for n in range(2**level)]
        self.messages = self.half if self.permuted else 1

    def code_row(self, feature):
        return feature // 2 + (feature % 2) * (self.share // 2)


def fetch_kernel(plan, *refs):
    inputs, refs = refs[:6], refs[6:]
    (grad_ref, word_ref, row_ref, pick_ref, chosen_ref), (hess_ref, child_ref, feature_ref, bin_ref, sems) = refs[:5], refs[5:]
    targets = (grad_ref, hess_ref, child_ref, feature_ref, bin_ref, word_ref)
    copies = [
        pltpu.make_async_copy(source, into, sems.at[i])
        for i, (source, into) in enumerate(zip(inputs, targets, strict=True))
    ]
    for copy in copies:
        copy.start()
    rows = plan.row_dev
    ahead = jnp.where(
        lax.broadcasted_iota(jnp.int32, (rows, rows), 0) <= lax.broadcasted_iota(jnp.int32, (rows, rows), 1), 1.0, 0.0
    ).astype(bf16)
    for copy in copies:
        copy.wait()

    nodes = [child_ref[0:1, :]]
    for level in range(1, plan.levels):
        nodes.append(nodes[-1] * 2 + child_ref[level : level + 1, :])
    row_ref[...] = jnp.zeros_like(row_ref)
    row_ref[0:1, :] = hess_ref[...].astype(f32).reshape(1, rows)
    for level, node in enumerate(nodes):
        row_ref[level + 1 : level + 2, :] = node.astype(f32)

    at = lax.broadcasted_iota(jnp.int32, (TILE, rows), 0)
    side = jnp.where(at == nodes[0], 1.0, 0.0)
    rank = jnp.dot(side.astype(bf16), ahead, preferred_element_type=f32)
    slot = jnp.where(side > 0.0, rank - 1.0, -1.0)
    slot_ids = lax.broadcasted_iota(jnp.int32, (plan.slots, rows), 0).astype(f32)
    for half in range(2):
        chosen_ref[half] = jnp.where(slot_ids == slot[half : half + 1], 1.0, 0.0).astype(bf16)

    panel = lax.axis_index("feat")
    lane = lax.broadcasted_iota(jnp.int32, (1, plan.codes), 1)
    pick_ref[...] = jnp.zeros_like(pick_ref)
    for slot in range(plan.splits):
        feature = feature_ref[slot]
        owner = lax.div(feature, jnp.int32(plan.feats))
        inner = feature - owner * plan.feats
        held = jnp.bitwise_xor(owner, panel)
        place = held * plan.words + inner // 2 + lax.rem(inner, 2) * (plan.panels * plan.words)
        place = jnp.where(held < plan.panels, place, plan.codes)
        pick_ref[0, slot : slot + 1, :] = jnp.where(lane == place, 1.0, 0.0)
        pick_ref[1, slot : slot + 1, :] = jnp.full((1, plan.codes), bin_ref[slot].astype(f32))
        pick_ref[2, slot : slot + 1, :] = jnp.full((1, plan.codes), jnp.where(held < plan.panels, 1.0, 0.0))


def prep_kernel(plan, *refs):
    (grad_ref, row_ref, pick_ref, chosen_ref), refs = refs[:4], refs[4:]
    word_refs, send_refs = refs[: plan.panels], refs[plan.panels : plan.panels + plan.parcels]
    table, packed, lines, marked = refs[plan.panels + plan.parcels :]
    rows = plan.row_dev
    low_at, high_at = plan.outs, plan.outs + plan.panels * plan.words
    own_at = plan.outs + plan.codes
    grads = grad_ref[...]
    hess = row_ref[0:1, :]
    nodes = [row_ref[level + 1 : level + 2, :] for level in range(plan.levels)]

    turn = jnp.where(
        lax.broadcasted_iota(jnp.int32, (plan.outs, plan.outs), 0)
        == lax.broadcasted_iota(jnp.int32, (plan.outs, plan.outs), 1),
        1.0,
        0.0,
    ).astype(bf16)
    table[0:low_at] = lax.dot_general(turn, grads, NT, preferred_element_type=f32).astype(bf16)
    for which, word_ref in enumerate(word_refs):
        words = word_ref[...]
        low = jnp.bitwise_and(words, 63)
        high = jnp.bitwise_and(jnp.right_shift(words, 6), 63)
        for first, codes in ((low_at, low), (high_at, high)):
            at = first + which * plan.words
            table[at : at + plan.words] = codes.astype(f32).astype(bf16)
    at = lax.broadcasted_iota(jnp.int32, (TILE, rows), 0)
    leaf = nodes[-1] - nodes[0] * plan.leaves
    table[own_at:] = jnp.where(at == 0, hess, jnp.where(at == 1, leaf, 0.0)).astype(bf16)
    for half in range(2):
        packed[half] = lax.dot_general(table[...], chosen_ref[half], NT, preferred_element_type=f32)

    ends = [(level, node) for level in range(plan.levels) for node in range(2 ** (level + 1))]
    code = jnp.dot(pick_ref[0].astype(bf16), table[low_at:own_at], preferred_element_type=f32)
    marked[...] = jnp.zeros_like(marked)
    for slot, (level, node) in enumerate(ends):
        here = jnp.where(nodes[level] == node, pick_ref[2, slot : slot + 1, 0:1], 0.0)
        left = jnp.where(code[slot : slot + 1] <= pick_ref[1, slot : slot + 1, 0:1], here, 0.0)
        marked[slot : slot + 1, :] = left
        marked[plan.split_rows + slot : plan.split_rows + slot + 1, :] = here - left
    mark = marked[...]
    sums = jnp.dot(mark.astype(bf16), grads, preferred_element_type=f32)
    curv = jnp.sum(mark * hess, axis=1, keepdims=True)
    shape = (2 * plan.split_rows, plan.outs)
    curv = jnp.broadcast_to(curv, shape)
    lane = lax.broadcasted_iota(jnp.int32, (1, plan.outs), 1)
    blank = jnp.zeros((1, LANES), f32)
    filler = jnp.zeros((plan.base_rows - plan.misc_at - plan.misc_rows, plan.slots), f32)
    for leaf in range(2 * plan.leaves):
        places = [
            side * plan.split_rows + 2 ** (level + 1) - 2 + (leaf >> (plan.levels - 1 - level))
            for side in range(2)
            for level in range(plan.levels)
        ]
        spread_curv = jnp.zeros((1, plan.outs), f32)
        for i, at in enumerate(places):
            spread_curv = jnp.where(lane == i, curv[at : at + 1], spread_curv)
        parts = []
        for value in [*(sums[at : at + 1] for at in places), spread_curv]:
            for _ in range(PIECES):
                parts.append(value.astype(bf16).astype(f32))
                value = value - parts[-1]
        parts += [blank] * (-len(parts) % plan.spans)
        parts = [jnp.concatenate(parts[i : i + plan.spans], axis=1) for i in range(0, len(parts), plan.spans)]
        lines[leaf] = jnp.concatenate(parts + ([filler] if filler.shape[0] else []), axis=0)

    word_share = plan.share // 2
    parity = rem(lax.axis_index("feat"), plan.panels)
    for slot in range(plan.parcels if plan.permuted else plan.devices):
        device = slot
        if plan.permuted:
            device = rem(lax.axis_index("rows") + 2 * slot + 2 - parity, plan.devices)
        half, place = div(device, plan.half), rem(device, plan.half)
        share, split = div(place, OUT_SPLIT), rem(place, OUT_SPLIT)

        def codes(which):
            at = [first + which * plan.words + share * word_share for first in (low_at, high_at)]
            return [packed[half, pl.ds(aligned(first, word_share), word_share), :] for first in at]

        message = [
            *codes(0),
            packed[half, pl.ds(aligned(split * plan.outs_dev, plan.outs_dev), plan.outs_dev), :],
            packed[half, own_at : own_at + 2, :],
            lines[div(device, plan.devices // (2 * plan.leaves))],
        ]
        if plan.permuted:
            send_refs[slot][...] = jnp.concatenate(message + codes(1), axis=0).astype(bf16)
        else:
            send_refs[0][slot] = jnp.concatenate(message, axis=0).astype(bf16)


def main_kernel(plan, chunk, *refs):
    got_refs, refs = refs[: plan.parcels], refs[plan.parcels :]
    if plan.permuted:
        got_refs, refs = got_refs + tuple(refs[0].at[k] for k in range(plan.parcels)), refs[1:]
    out_refs, (weighted, gain_table, left_sums) = refs[: plan.messages], refs[plan.messages :]
    rows = plan.slots
    leaves, outs_dev, step = plan.leaves, plan.outs_dev, plan.step
    hess_at = leaves * outs_dev
    order = [feature for tile in plan.tiles for feature in tile]
    level_bins = lax.broadcasted_iota(jnp.int32, (BINS, rows), 0).astype(f32).astype(bf16)
    leaf_ids = lax.broadcasted_iota(jnp.int32, (TILE, rows), 0).astype(f32)
    zero = jnp.zeros((), bf16)
    one = jnp.ones((), bf16)

    def parcel(source):
        return got_refs[source] if plan.permuted else got_refs[0].at[source]

    def marked(source, feature):
        row = plan.code_row(feature)
        code = jnp.broadcast_to(parcel(source)[row : row + 1, :], (BINS, rows))
        return jnp.where(code <= level_bins, one, zero)

    def add_chunk(first, fresh):
        for k in range(chunk):
            source = first + k
            columns = slice(k * rows, (k + 1) * rows)
            misc = parcel(source)[plan.misc_at : plan.misc_at + 2, :].astype(f32)
            hess, node = misc[0:1], misc[1:2]
            weighted[hess_at : hess_at + TILE, columns] = jnp.where(leaf_ids == node, hess, 0.0).astype(bf16)
            node_wide = jnp.broadcast_to(node, (outs_dev, rows)).astype(bf16)
            grads = parcel(source)[plan.grad_at : plan.grad_at + outs_dev, :]
            for leaf in range(leaves):
                weighted[leaf * outs_dev : (leaf + 1) * outs_dev, columns] = jnp.where(
                    node_wide == jnp.asarray(leaf, bf16), grads, zero
                )
        for group in range(plan.share // step):
            features = order[group * step : (group + 1) * step]
            marks = jnp.concatenate(
                [
                    jnp.concatenate([marked(first + k, feature) for feature in features], axis=0)
                    for k in range(chunk)
                ],
                axis=1,
            )
            part = lax.dot_general(weighted[...], marks, NT, preferred_element_type=f32)
            span = slice(group * step * BINS, (group + 1) * step * BINS)
            if count == 1:
                add_gains(group, part)
            elif fresh:
                left_sums[:, span] = part
            else:
                left_sums[:, span] += part

    known = []

    def add_gains(group, sums):
        left = [sums[leaf * outs_dev : (leaf + 1) * outs_dev] for leaf in range(leaves)]
        hess = [sums[hess_at + leaf : hess_at + leaf + 1] for leaf in range(leaves)]
        for level in reversed(range(plan.levels - 1)):
            past = len(left) - 2 ** (level + 1)
            for n in range(past, len(left), 2):
                left.append(left[n] + left[n + 1])
                hess.append(hess[n] + hess[n + 1])
        hess = jnp.concatenate(hess, axis=0) + penalty
        if not known:
            totals = [part[:, BINS - 1 : BINS] for part in left]
            squares = jnp.concatenate([jnp.sum(t * t, axis=0, keepdims=True) for t in totals], axis=0)
            hess_total = hess[:, BINS - 1 : BINS] + penalty
            known.extend([totals, hess_total, squares / (hess_total - penalty)])
        totals, hess_total, whole_part = known
        on_left = jnp.concatenate([jnp.sum(part * part, axis=0, keepdims=True) for part in left], axis=0)
        rights = [t - part for t, part in zip(totals, left, strict=True)]
        on_right = jnp.concatenate([jnp.sum(part * part, axis=0, keepdims=True) for part in rights], axis=0)
        gains = (on_left / hess + on_right / (hess_total - hess) - whole_part) / plan.outs
        for end in range(len(plan.ends)):
            for tile in range(step // 2):
                at = group * (step // 2) + tile
                gain_table[end, at : at + 1, :] = gains[end : end + 1, tile * LANES : (tile + 1) * LANES]

    count = plan.devices // chunk
    add_chunk(0, True)
    if count > 1:
        lax.fori_loop(1, count, lambda c, _: (add_chunk(c * chunk, False), 0)[1], 0)
        for group in range(plan.share // step):
            add_gains(group, left_sums[:, group * step * BINS : (group + 1) * step * BINS])
    me = rem(lax.axis_index("rows"), plan.half)
    for slot in range(plan.half):
        place = target(me, slot, plan.half) if plan.permuted else slot
        out_ref = out_refs[slot] if plan.permuted else out_refs[0].at[slot]
        for level in range(plan.levels):
            count = plan.needed[level] // 2
            end = plan.ends.index((level, 0)) + div(place, plan.sizes[level])
            first = rem(rem(place, plan.sizes[level]) * plan.returned[level], plan.share) // 2
            if not isinstance(first, int) and count % 8 == 0:
                first = pl.multiple_of(first, 8)
            at = plan.level_at[level]
            out_ref[at : at + count, :] = gain_table[end, pl.ds(first, count), :]
        if plan.message > plan.gain_rows:
            out_ref[plan.gain_rows :, :] = jnp.zeros((plan.message - plan.gain_rows, LANES), f32)


def score_kernel(plan, *refs):
    got_refs, (score_ref, *passed) = refs[: plan.parcels], refs[plan.parcels :]
    tail = slice(plan.misc_at + 2, plan.misc_at + plan.misc_rows)
    total = jnp.zeros((plan.misc_rows - 2, plan.slots), f32)
    if plan.permuted:
        for source, ref in enumerate(got_refs):
            passed[0][source, : plan.share] = ref[plan.base_rows :, :]
            passed[0][source, plan.share :] = ref[plan.share : plan.base_rows, :]
            total = total + ref[tail, :].astype(f32)
    else:
        total = lax.fori_loop(0, plan.devices, lambda k, sums: sums + got_refs[0][k, tail, :].astype(f32), total)
    score_ref[...] = jnp.zeros_like(score_ref)
    for i in range(plan.score_rows):
        value = 0.0
        for piece in reversed(range(PIECES)):
            line, span = divmod(i * PIECES + piece, plan.spans)
            value = value + total[line : line + 1, span * LANES : (span + 1) * LANES]
        score_ref[i : i + 1, :] = value


def final_kernel(plan, *refs):
    got_refs, refs = refs[: plan.messages], refs[plan.messages :]
    score_refs, refs = refs[: -plan.levels - 1], refs[-plan.levels - 1 :]
    *gain_refs, child_ref = refs
    me = rem(lax.axis_index("rows"), plan.half)
    side = plan.block // 2
    arrived = []
    for slot in range(plan.half):
        place = source_of(me, slot, plan.half) if plan.permuted else slot
        arrived.append((div(place, OUT_SPLIT), got_refs[slot] if plan.permuted else got_refs[0].at[slot]))
    for level, gain_ref in enumerate(gain_refs):
        rows = slice(plan.level_at[level], plan.level_at[level] + plan.needed[level] // 2)
        first = div(rem(me, plan.sizes[level]) * plan.returned[level], plan.share)
        for turn in range(plan.returned[level] // plan.needed[level]):
            value = 0.0
            for share, ref in arrived:
                value = value + jnp.where(share == first + turn, ref[rows, :], 0.0)
            for start in range(0, plan.needed[level], plan.block):
                part = value[start // 2 : start // 2 + side]
                at = turn * plan.share + start
                gain_ref[at : at + side, :] = part[:, :BINS]
                gain_ref[at + side : at + 2 * side, :] = part[:, BINS:]
    sums = score_refs[0][...]
    for score_ref in score_refs[1:]:
        sums = sums + score_ref[...]
    curv = sums[2 * plan.levels : 2 * plan.levels + 1, :]
    for level in range(plan.levels):
        for side in range(2):
            line = side * plan.levels + level
            scale = jnp.sqrt(curv[:, line : line + 1] + penalty)
            child_ref[level, 0, side : side + 1, :] = -sums[line : line + 1, :] / scale


def flipped(block, bits):
    count = lax.axis_size("feat")
    return lax.ppermute(block, "feat", [(p, p ^ bits) for p in range(count)])


def on_device(gradients, hessians, bin_words, children, split_feature, split_bin):
    plan = Plan(lax.axis_size("rows"), lax.axis_size("feat"), gradients, bin_words, children)
    params = pltpu.CompilerParams(vmem_limit_bytes=VMEM_BYTES)

    inputs = (gradients, hessians, children, split_feature, split_bin, bin_words)
    crossed = [flipped(bin_words, 1)] if plan.permuted else []
    row_dev, table_rows = plan.row_dev, plan.outs + plan.codes + TILE
    grads, words, row_values, picks, chosen = pl.pallas_call(
        functools.partial(fetch_kernel, plan),
        out_shape=(
            jax.ShapeDtypeStruct(gradients.shape, bf16),
            jax.ShapeDtypeStruct(bin_words.shape, jnp.int32),
            jax.ShapeDtypeStruct((8, row_dev), f32),
            jax.ShapeDtypeStruct((3, plan.split_rows, plan.codes), f32),
            jax.ShapeDtypeStruct((2, plan.slots, row_dev), bf16),
        ),
        in_specs=[pl.BlockSpec(memory_space=pltpu.HBM)] * len(inputs),
        out_specs=[whole()] * 5,
        scratch_shapes=[
            pltpu.VMEM(hessians.shape, bf16),
            pltpu.VMEM(children.shape, jnp.int32),
            pltpu.SMEM(split_feature.shape, jnp.int32),
            pltpu.SMEM(split_bin.shape, jnp.int32),
            pltpu.SemaphoreType.DMA((len(inputs),)),
        ],
        cost_estimate=pl.CostEstimate(flops=10**9, bytes_accessed=10**6, transcendentals=0),
        compiler_params=params,
        name="fetch",
    )(*(pltpu.with_memory_space_constraint(a, pltpu.HBM) for a in inputs))
    parcel = (plan.sent_rows, plan.slots) if plan.permuted else (plan.devices, plan.sent_rows, plan.slots)
    parcels = pl.pallas_call(
        functools.partial(prep_kernel, plan),
        out_shape=[jax.ShapeDtypeStruct(parcel, bf16)] * plan.parcels,
        in_specs=[whole()] * (4 + plan.panels),
        out_specs=[whole()] * plan.parcels,
        scratch_shapes=[
            pltpu.VMEM((table_rows, row_dev), bf16),
            pltpu.VMEM((2, table_rows, plan.slots), f32),
            pltpu.VMEM((2 * plan.leaves, plan.base_rows - plan.misc_at - 2, plan.slots), f32),
            pltpu.VMEM((2 * plan.split_rows, row_dev), f32),
        ],
        compiler_params=params,
        name="prep",
    )(grads, row_values, picks, chosen, words, *crossed)

    if plan.permuted:
        got = spread(parcels, plan)
    else:
        got = [lax.all_to_all(parcels[0], "rows", 0, 0)]
    shapes = [jax.ShapeDtypeStruct((8, plan.outs), f32)]
    if plan.permuted:
        shapes.append(jax.ShapeDtypeStruct((plan.parcels, plan.base_rows, plan.slots), bf16))
    scores, *passed = pl.pallas_call(
        functools.partial(score_kernel, plan),
        out_shape=shapes,
        in_specs=[whole()] * plan.parcels,
        out_specs=[whole()] * len(shapes),
        compiler_params=params,
        name="scores",
    )(*got)
    arrays = got + [flipped(block, 1) for block in passed]
    far = [flipped(scores, away) for away in range(plan.panels, lax.axis_size("feat"), plan.panels)]

    chunk = max(1, min(plan.devices, 4096 // plan.slots))
    while plan.devices % chunk:
        chunk -= 1
    sums_rows = plan.leaves * plan.outs_dev + TILE
    block = (plan.message, LANES) if plan.permuted else (plan.half, plan.message, LANES)
    messages = pl.pallas_call(
        functools.partial(main_kernel, plan, chunk),
        out_shape=[jax.ShapeDtypeStruct(block, f32)] * plan.messages,
        in_specs=[whole()] * len(arrays),
        out_specs=[whole()] * plan.messages,
        scratch_shapes=[
            pltpu.VMEM((sums_rows, chunk * plan.slots), bf16),
            pltpu.VMEM((len(plan.ends), plan.share // 2, LANES), f32),
            pltpu.VMEM((sums_rows, plan.share * BINS), f32),
        ],
        cost_estimate=pl.CostEstimate(
            flops=2 * sums_rows * plan.devices * plan.slots * plan.share * BINS,
            bytes_accessed=4 * plan.devices * plan.sent_rows * plan.slots,
            transcendentals=0,
        ),
        compiler_params=params,
        name="gains",
    )(*arrays)

    messages, far = lax.optimization_barrier((list(messages), far))
    scores = sum(far, scores)
    score_parts = [scores] + ([flipped(scores, 1)] if plan.permuted else [])
    if plan.permuted:
        messages = exchanged(messages, plan.half, plan.devices)
    else:
        halves = [list(range(plan.half)), list(range(plan.half, plan.devices))]
        messages = [lax.all_to_all(messages[0], "rows", 0, 0, axis_index_groups=halves)]
    shapes = [
        jax.ShapeDtypeStruct((count, BINS), f32) for count in plan.returned
    ]
    shapes.append(jax.ShapeDtypeStruct((plan.levels, 1, 2, plan.outs), f32))
    return pl.pallas_call(
        functools.partial(final_kernel, plan),
        out_shape=tuple(shapes),
        in_specs=[whole()] * (plan.messages + len(score_parts)),
        out_specs=tuple(whole() for _ in shapes),
        compiler_params=params,
        name="finish",
    )(*messages, *score_parts)


def solution(mesh):
    placed = (P("rows", None), P("rows"), P("feat", "rows"), P(None, "rows"), P(), P())
    return jax.shard_map(
        on_device,
        mesh=mesh,
        in_specs=placed,
        out_specs=(
            P("rows", "feat"),
            P("rows", "feat"),
            P("rows", "feat"),
            P(None, "rows", None, None),
        ),
        check_vma=False,
    )
```

```python
import functools

import jax
import jax.numpy as jnp
from jax import lax
from jax.experimental import pallas as pl
from jax.experimental.pallas import tpu as pltpu
from jax.sharding import PartitionSpec as P

BINS = 64
LANES = 128
TILE = 16
OUT_SPLIT = 2
PIECES = 2
penalty = 1.0
VMEM_BYTES = 32 * 2**20

bf16 = jnp.bfloat16
f32 = jnp.float32
NT = (((1,), (1,)), ((), ()))
PERMUTED = 8


def div(value, by):
    return value // by if isinstance(value, int) else lax.div(value, jnp.int32(by))


def rem(value, by):
    return value % by if isinstance(value, int) else lax.rem(value, jnp.int32(by))


def round_up(value, unit):
    return -(-value // unit) * unit


def whole(*_):
    return pl.BlockSpec(memory_space=pltpu.VMEM)


def aligned(value, unit):
    return value if isinstance(value, int) or unit % 8 else pl.multiple_of(value, 8)


def target(me, slot, count):
    return rem(me + slot, count)


def source_of(me, slot, count):
    return rem(me + (count - slot), count)


def exchanged(blocks, group, count):
    moved = [blocks[0]]
    for slot in range(1, group):
        route = [(p, p - p % group + (p + slot) % group) for p in range(count)]
        moved.append(lax.ppermute(blocks[slot], "rows", route))
    return moved


def spread(parcels, plan):
    feat_axis = lax.axis_size("feat")
    moved = []
    for slot, block in enumerate(parcels):
        route = []
        for p in range(plan.devices * feat_axis):
            row, panel = divmod(p, feat_axis)
            row = (row + plan.offsets[panel % 2][slot]) % plan.devices
            route.append((p, row * feat_axis + panel))
        moved.append(lax.ppermute(block, ("rows", "feat"), route))
    return moved


class Plan:
    def __init__(self, rows_axis, feat_axis, gradients, bin_words, children):
        self.devices = rows_axis
        self.half = rows_axis // 2
        self.row_dev, self.outs = gradients.shape
        self.words = bin_words.shape[0]
        self.feats = 2 * self.words
        self.levels = children.shape[0]
        self.leaves = 2 ** (self.levels - 1)
        self.slots = round_up(self.row_dev * 3 // 4, LANES)
        self.shares = self.half // OUT_SPLIT
        self.share = self.feats // self.shares
        self.outs_dev = self.outs // OUT_SPLIT
        self.permuted = rows_axis <= PERMUTED and feat_axis % 2 == 0
        self.panels = 2 if self.permuted else 1
        self.parcels = rows_axis // 2 if self.permuted else 1
        self.offsets = [
            sorted(range(first, rows_axis, 2), key=lambda k: (abs(k - rows_axis // 2), k)) for first in range(2)
        ]
        self.codes = self.panels * self.feats
        self.splits = 2 ** (self.levels + 1) - 2
        self.split_rows = round_up(self.splits, TILE)
        self.grad_at = self.share
        self.misc_at = self.share + self.outs_dev
        self.score_rows = 2 * self.levels + 1
        self.spans = self.slots // LANES
        self.misc_rows = 2 + -(-self.score_rows * PIECES // self.spans)
        self.base_rows = round_up(self.misc_at + self.misc_rows, 8)
        self.sent_rows = self.base_rows + (self.panels - 1) * self.share
        self.sizes = [self.devices >> (level + 1) for level in range(self.levels)]
        self.returned = [self.feats // size for size in self.sizes]
        self.needed = [min(self.share, count) for count in self.returned]
        self.block = min(self.needed)
        self.step = min(8, self.share)
        self.tiles = [
            (start + k, start + k + self.block // 2)
            for start in range(0, self.share, self.block)
            for k in range(self.block // 2)
        ]
        self.level_at = [sum(self.needed[:level]) // 2 for level in range(self.levels)]
        self.gain_rows = sum(self.needed) // 2
        self.message = round_up(self.gain_rows, 8)
        self.ends = [(level, n) for level in reversed(range(self.levels)) for n in range(2**level)]
        self.messages = self.half if self.permuted else 1

    def code_row(self, feature):
        return feature // 2 + (feature % 2) * (self.share // 2)


def fetch_kernel(plan, *refs):
    inputs, refs = refs[:6], refs[6:]
    (grad_ref, word_ref, row_ref, pick_ref, chosen_ref), (hess_ref, child_ref, feature_ref, bin_ref, sems) = refs[:5], refs[5:]
    targets = (grad_ref, hess_ref, child_ref, feature_ref, bin_ref, word_ref)
    copies = [
        pltpu.make_async_copy(source, into, sems.at[i])
        for i, (source, into) in enumerate(zip(inputs, targets, strict=True))
    ]
    for copy in copies:
        copy.start()
    rows = plan.row_dev
    ahead = jnp.where(
        lax.broadcasted_iota(jnp.int32, (rows, rows), 0) <= lax.broadcasted_iota(jnp.int32, (rows, rows), 1), 1.0, 0.0
    ).astype(bf16)
    for copy in copies:
        copy.wait()

    nodes = [child_ref[0:1, :]]
    for level in range(1, plan.levels):
        nodes.append(nodes[-1] * 2 + child_ref[level : level + 1, :])
    row_ref[...] = jnp.zeros_like(row_ref)
    row_ref[0:1, :] = hess_ref[...].astype(f32).reshape(1, rows)
    for level, node in enumerate(nodes):
        row_ref[level + 1 : level + 2, :] = node.astype(f32)

    at = lax.broadcasted_iota(jnp.int32, (TILE, rows), 0)
    side = jnp.where(at == nodes[0], 1.0, 0.0)
    rank = jnp.dot(side.astype(bf16), ahead, preferred_element_type=f32)
    slot = jnp.where(side > 0.0, rank - 1.0, -1.0)
    slot_ids = lax.broadcasted_iota(jnp.int32, (plan.slots, rows), 0).astype(f32)
    for half in range(2):
        chosen_ref[half] = jnp.where(slot_ids == slot[half : half + 1], 1.0, 0.0).astype(bf16)

    panel = lax.axis_index("feat")
    lane = lax.broadcasted_iota(jnp.int32, (1, plan.codes), 1)
    pick_ref[...] = jnp.zeros_like(pick_ref)
    for slot in range(plan.splits):
        feature = feature_ref[slot]
        owner = lax.div(feature, jnp.int32(plan.feats))
        inner = feature - owner * plan.feats
        held = jnp.bitwise_xor(owner, panel)
        place = held * plan.words + inner // 2 + lax.rem(inner, 2) * (plan.panels * plan.words)
        place = jnp.where(held < plan.panels, place, plan.codes)
        pick_ref[0, slot : slot + 1, :] = jnp.where(lane == place, 1.0, 0.0)
        pick_ref[1, slot : slot + 1, :] = jnp.full((1, plan.codes), bin_ref[slot].astype(f32))
        pick_ref[2, slot : slot + 1, :] = jnp.full((1, plan.codes), jnp.where(held < plan.panels, 1.0, 0.0))


def prep_kernel(plan, *refs):
    (grad_ref, row_ref, pick_ref, chosen_ref), refs = refs[:4], refs[4:]
    word_refs, send_refs = refs[: plan.panels], refs[plan.panels : plan.panels + plan.parcels]
    table, packed, lines, marked = refs[plan.panels + plan.parcels :]
    rows = plan.row_dev
    low_at, high_at = plan.outs, plan.outs + plan.panels * plan.words
    own_at = plan.outs + plan.codes
    grads = grad_ref[...]
    hess = row_ref[0:1, :]
    nodes = [row_ref[level + 1 : level + 2, :] for level in range(plan.levels)]

    turn = jnp.where(
        lax.broadcasted_iota(jnp.int32, (plan.outs, plan.outs), 0)
        == lax.broadcasted_iota(jnp.int32, (plan.outs, plan.outs), 1),
        1.0,
        0.0,
    ).astype(bf16)
    table[0:low_at] = lax.dot_general(turn, grads, NT, preferred_element_type=f32).astype(bf16)
    for which, word_ref in enumerate(word_refs):
        words = word_ref[...]
        low = jnp.bitwise_and(words, 63)
        high = jnp.bitwise_and(jnp.right_shift(words, 6), 63)
        for first, codes in ((low_at, low), (high_at, high)):
            at = first + which * plan.words
            table[at : at + plan.words] = codes.astype(f32).astype(bf16)
    at = lax.broadcasted_iota(jnp.int32, (TILE, rows), 0)
    leaf = nodes[-1] - nodes[0] * plan.leaves
    table[own_at:] = jnp.where(at == 0, hess, jnp.where(at == 1, leaf, 0.0)).astype(bf16)
    for half in range(2):
        packed[half] = lax.dot_general(table[...], chosen_ref[half], NT, preferred_element_type=f32)

    ends = [(level, node) for level in range(plan.levels) for node in range(2 ** (level + 1))]
    code = jnp.dot(pick_ref[0].astype(bf16), table[low_at:own_at], preferred_element_type=f32)
    marked[...] = jnp.zeros_like(marked)
    for slot, (level, node) in enumerate(ends):
        here = jnp.where(nodes[level] == node, pick_ref[2, slot : slot + 1, 0:1], 0.0)
        left = jnp.where(code[slot : slot + 1] <= pick_ref[1, slot : slot + 1, 0:1], here, 0.0)
        marked[slot : slot + 1, :] = left
        marked[plan.split_rows + slot : plan.split_rows + slot + 1, :] = here - left
    mark = marked[...]
    sums = jnp.dot(mark.astype(bf16), grads, preferred_element_type=f32)
    curv = jnp.sum(mark * hess, axis=1, keepdims=True)
    shape = (2 * plan.split_rows, plan.outs)
    curv = jnp.broadcast_to(curv, shape)
    lane = lax.broadcasted_iota(jnp.int32, (1, plan.outs), 1)
    blank = jnp.zeros((1, LANES), f32)
    filler = jnp.zeros((plan.base_rows - plan.misc_at - plan.misc_rows, plan.slots), f32)
    for leaf in range(2 * plan.leaves):
        places = [
            side * plan.split_rows + 2 ** (level + 1) - 2 + (leaf >> (plan.levels - 1 - level))
            for side in range(2)
            for level in range(plan.levels)
        ]
        spread_curv = jnp.zeros((1, plan.outs), f32)
        for i, at in enumerate(places):
            spread_curv = jnp.where(lane == i, curv[at : at + 1], spread_curv)
        parts = []
        for value in [*(sums[at : at + 1] for at in places), spread_curv]:
            for _ in range(PIECES):
                parts.append(value.astype(bf16).astype(f32))
                value = value - parts[-1]
        parts += [blank] * (-len(parts) % plan.spans)
        parts = [jnp.concatenate(parts[i : i + plan.spans], axis=1) for i in range(0, len(parts), plan.spans)]
        lines[leaf] = jnp.concatenate(parts + ([filler] if filler.shape[0] else []), axis=0)

    word_share = plan.share // 2
    parity = rem(lax.axis_index("feat"), plan.panels)
    for slot in range(plan.parcels if plan.permuted else plan.devices):
        device = slot
        if plan.permuted:
            offset = jnp.where(parity == 0, plan.offsets[0][slot], plan.offsets[1][slot])
            device = rem(lax.axis_index("rows") + offset, plan.devices)
        half, place = div(device, plan.half), rem(device, plan.half)
        share, split = div(place, OUT_SPLIT), rem(place, OUT_SPLIT)

        def codes(which):
            at = [first + which * plan.words + share * word_share for first in (low_at, high_at)]
            return [packed[half, pl.ds(aligned(first, word_share), word_share), :] for first in at]

        message = [
            *codes(0),
            packed[half, pl.ds(aligned(split * plan.outs_dev, plan.outs_dev), plan.outs_dev), :],
            packed[half, own_at : own_at + 2, :],
            lines[div(device, plan.devices // (2 * plan.leaves))],
        ]
        if plan.permuted:
            send_refs[slot][...] = jnp.concatenate(message + codes(1), axis=0).astype(bf16)
        else:
            send_refs[0][slot] = jnp.concatenate(message, axis=0).astype(bf16)


def main_kernel(plan, chunk, *refs):
    got_refs, refs = refs[: plan.parcels], refs[plan.parcels :]
    if plan.permuted:
        got_refs, refs = got_refs + tuple(refs[0].at[k] for k in range(plan.parcels)), refs[1:]
    out_refs, (weighted, gain_table, left_sums) = refs[: plan.messages], refs[plan.messages :]
    rows = plan.slots
    leaves, outs_dev, step = plan.leaves, plan.outs_dev, plan.step
    hess_at = leaves * outs_dev
    order = [feature for tile in plan.tiles for feature in tile]
    level_bins = lax.broadcasted_iota(jnp.int32, (BINS, rows), 0).astype(f32).astype(bf16)
    leaf_ids = lax.broadcasted_iota(jnp.int32, (TILE, rows), 0).astype(f32)
    zero = jnp.zeros((), bf16)
    one = jnp.ones((), bf16)

    def parcel(source):
        return got_refs[source] if plan.permuted else got_refs[0].at[source]

    def marked(source, feature):
        row = plan.code_row(feature)
        code = jnp.broadcast_to(parcel(source)[row : row + 1, :], (BINS, rows))
        return jnp.where(code <= level_bins, one, zero)

    def add_chunk(first, fresh):
        for k in range(chunk):
            source = first + k
            columns = slice(k * rows, (k + 1) * rows)
            misc = parcel(source)[plan.misc_at : plan.misc_at + 2, :].astype(f32)
            hess, node = misc[0:1], misc[1:2]
            weighted[hess_at : hess_at + TILE, columns] = jnp.where(leaf_ids == node, hess, 0.0).astype(bf16)
            node_wide = jnp.broadcast_to(node, (outs_dev, rows)).astype(bf16)
            grads = parcel(source)[plan.grad_at : plan.grad_at + outs_dev, :]
            for leaf in range(leaves):
                weighted[leaf * outs_dev : (leaf + 1) * outs_dev, columns] = jnp.where(
                    node_wide == jnp.asarray(leaf, bf16), grads, zero
                )
        for group in range(plan.share // step):
            features = order[group * step : (group + 1) * step]
            marks = jnp.concatenate(
                [
                    jnp.concatenate([marked(first + k, feature) for feature in features], axis=0)
                    for k in range(chunk)
                ],
                axis=1,
            )
            part = lax.dot_general(weighted[...], marks, NT, preferred_element_type=f32)
            span = slice(group * step * BINS, (group + 1) * step * BINS)
            if count == 1:
                add_gains(group, part)
            elif fresh:
                left_sums[:, span] = part
            else:
                left_sums[:, span] += part

    known = []

    def add_gains(group, sums):
        left = [sums[leaf * outs_dev : (leaf + 1) * outs_dev] for leaf in range(leaves)]
        hess = [sums[hess_at + leaf : hess_at + leaf + 1] for leaf in range(leaves)]
        for level in reversed(range(plan.levels - 1)):
            past = len(left) - 2 ** (level + 1)
            for n in range(past, len(left), 2):
                left.append(left[n] + left[n + 1])
                hess.append(hess[n] + hess[n + 1])
        hess = jnp.concatenate(hess, axis=0) + penalty
        if not known:
            totals = [part[:, BINS - 1 : BINS] for part in left]
            squares = jnp.concatenate([jnp.sum(t * t, axis=0, keepdims=True) for t in totals], axis=0)
            hess_total = hess[:, BINS - 1 : BINS] + penalty
            known.extend([totals, hess_total, squares / (hess_total - penalty)])
        totals, hess_total, whole_part = known
        on_left = jnp.concatenate([jnp.sum(part * part, axis=0, keepdims=True) for part in left], axis=0)
        rights = [t - part for t, part in zip(totals, left, strict=True)]
        on_right = jnp.concatenate([jnp.sum(part * part, axis=0, keepdims=True) for part in rights], axis=0)
        gains = (on_left / hess + on_right / (hess_total - hess) - whole_part) / plan.outs
        for end in range(len(plan.ends)):
            for tile in range(step // 2):
                at = group * (step // 2) + tile
                gain_table[end, at : at + 1, :] = gains[end : end + 1, tile * LANES : (tile + 1) * LANES]

    count = plan.devices // chunk
    add_chunk(0, True)
    if count > 1:
        lax.fori_loop(1, count, lambda c, _: (add_chunk(c * chunk, False), 0)[1], 0)
        for group in range(plan.share // step):
            add_gains(group, left_sums[:, group * step * BINS : (group + 1) * step * BINS])
    me = rem(lax.axis_index("rows"), plan.half)
    for slot in range(plan.half):
        place = target(me, slot, plan.half) if plan.permuted else slot
        out_ref = out_refs[slot] if plan.permuted else out_refs[0].at[slot]
        for level in range(plan.levels):
            count = plan.needed[level] // 2
            end = plan.ends.index((level, 0)) + div(place, plan.sizes[level])
            first = rem(rem(place, plan.sizes[level]) * plan.returned[level], plan.share) // 2
            if not isinstance(first, int) and count % 8 == 0:
                first = pl.multiple_of(first, 8)
            at = plan.level_at[level]
            out_ref[at : at + count, :] = gain_table[end, pl.ds(first, count), :]
        if plan.message > plan.gain_rows:
            out_ref[plan.gain_rows :, :] = jnp.zeros((plan.message - plan.gain_rows, LANES), f32)


def score_kernel(plan, *refs):
    got_refs, (score_ref, *passed) = refs[: plan.parcels], refs[plan.parcels :]
    tail = slice(plan.misc_at + 2, plan.misc_at + plan.misc_rows)
    total = jnp.zeros((plan.misc_rows - 2, plan.slots), f32)
    if plan.permuted:
        for source, ref in enumerate(got_refs):
            passed[0][source, : plan.share] = ref[plan.base_rows :, :]
            passed[0][source, plan.share :] = ref[plan.share : plan.base_rows, :]
            total = total + ref[tail, :].astype(f32)
    else:
        total = lax.fori_loop(0, plan.devices, lambda k, sums: sums + got_refs[0][k, tail, :].astype(f32), total)
    score_ref[...] = jnp.zeros_like(score_ref)
    for i in range(plan.score_rows):
        value = 0.0
        for piece in reversed(range(PIECES)):
            line, span = divmod(i * PIECES + piece, plan.spans)
            value = value + total[line : line + 1, span * LANES : (span + 1) * LANES]
        score_ref[i : i + 1, :] = value


def final_kernel(plan, *refs):
    got_refs, refs = refs[: plan.messages], refs[plan.messages :]
    score_refs, refs = refs[: -plan.levels - 1], refs[-plan.levels - 1 :]
    *gain_refs, child_ref = refs
    me = rem(lax.axis_index("rows"), plan.half)
    side = plan.block // 2
    arrived = []
    for slot in range(plan.half):
        place = source_of(me, slot, plan.half) if plan.permuted else slot
        arrived.append((div(place, OUT_SPLIT), got_refs[slot] if plan.permuted else got_refs[0].at[slot]))
    for level, gain_ref in enumerate(gain_refs):
        rows = slice(plan.level_at[level], plan.level_at[level] + plan.needed[level] // 2)
        first = div(rem(me, plan.sizes[level]) * plan.returned[level], plan.share)
        for turn in range(plan.returned[level] // plan.needed[level]):
            value = 0.0
            for share, ref in arrived:
                value = value + jnp.where(share == first + turn, ref[rows, :], 0.0)
            for start in range(0, plan.needed[level], plan.block):
                part = value[start // 2 : start // 2 + side]
                at = turn * plan.share + start
                gain_ref[at : at + side, :] = part[:, :BINS]
                gain_ref[at + side : at + 2 * side, :] = part[:, BINS:]
    sums = score_refs[0][...]
    for score_ref in score_refs[1:]:
        sums = sums + score_ref[...]
    curv = sums[2 * plan.levels : 2 * plan.levels + 1, :]
    for level in range(plan.levels):
        for side in range(2):
            line = side * plan.levels + level
            scale = jnp.sqrt(curv[:, line : line + 1] + penalty)
            child_ref[level, 0, side : side + 1, :] = -sums[line : line + 1, :] / scale


def flipped(block, bits):
    count = lax.axis_size("feat")
    return lax.ppermute(block, "feat", [(p, p ^ bits) for p in range(count)])


def on_device(gradients, hessians, bin_words, children, split_feature, split_bin):
    plan = Plan(lax.axis_size("rows"), lax.axis_size("feat"), gradients, bin_words, children)
    params = pltpu.CompilerParams(vmem_limit_bytes=VMEM_BYTES)

    inputs = (gradients, hessians, children, split_feature, split_bin, bin_words)
    crossed = [flipped(bin_words, 1)] if plan.permuted else []
    row_dev, table_rows = plan.row_dev, plan.outs + plan.codes + TILE
    grads, words, row_values, picks, chosen = pl.pallas_call(
        functools.partial(fetch_kernel, plan),
        out_shape=(
            jax.ShapeDtypeStruct(gradients.shape, bf16),
            jax.ShapeDtypeStruct(bin_words.shape, jnp.int32),
            jax.ShapeDtypeStruct((8, row_dev), f32),
            jax.ShapeDtypeStruct((3, plan.split_rows, plan.codes), f32),
            jax.ShapeDtypeStruct((2, plan.slots, row_dev), bf16),
        ),
        in_specs=[pl.BlockSpec(memory_space=pltpu.HBM)] * len(inputs),
        out_specs=[whole()] * 5,
        scratch_shapes=[
            pltpu.VMEM(hessians.shape, bf16),
            pltpu.VMEM(children.shape, jnp.int32),
            pltpu.SMEM(split_feature.shape, jnp.int32),
            pltpu.SMEM(split_bin.shape, jnp.int32),
            pltpu.SemaphoreType.DMA((len(inputs),)),
        ],
        cost_estimate=pl.CostEstimate(flops=10**9, bytes_accessed=10**6, transcendentals=0),
        compiler_params=params,
        name="fetch",
    )(*(pltpu.with_memory_space_constraint(a, pltpu.HBM) for a in inputs))
    parcel = (plan.sent_rows, plan.slots) if plan.permuted else (plan.devices, plan.sent_rows, plan.slots)
    parcels = pl.pallas_call(
        functools.partial(prep_kernel, plan),
        out_shape=[jax.ShapeDtypeStruct(parcel, bf16)] * plan.parcels,
        in_specs=[whole()] * (4 + plan.panels),
        out_specs=[whole()] * plan.parcels,
        scratch_shapes=[
            pltpu.VMEM((table_rows, row_dev), bf16),
            pltpu.VMEM((2, table_rows, plan.slots), f32),
            pltpu.VMEM((2 * plan.leaves, plan.base_rows - plan.misc_at - 2, plan.slots), f32),
            pltpu.VMEM((2 * plan.split_rows, row_dev), f32),
        ],
        compiler_params=params,
        name="prep",
    )(grads, row_values, picks, chosen, words, *crossed)

    if plan.permuted:
        got = spread(parcels, plan)
    else:
        got = [lax.all_to_all(parcels[0], "rows", 0, 0)]
    shapes = [jax.ShapeDtypeStruct((8, plan.outs), f32)]
    if plan.permuted:
        shapes.append(jax.ShapeDtypeStruct((plan.parcels, plan.base_rows, plan.slots), bf16))
    scores, *passed = pl.pallas_call(
        functools.partial(score_kernel, plan),
        out_shape=shapes,
        in_specs=[whole()] * plan.parcels,
        out_specs=[whole()] * len(shapes),
        compiler_params=params,
        name="scores",
    )(*got)
    arrays = got + [flipped(block, 1) for block in passed]
    far = [flipped(scores, away) for away in range(plan.panels, lax.axis_size("feat"), plan.panels)]

    chunk = max(1, min(plan.devices, 4096 // plan.slots))
    while plan.devices % chunk:
        chunk -= 1
    sums_rows = plan.leaves * plan.outs_dev + TILE
    block = (plan.message, LANES) if plan.permuted else (plan.half, plan.message, LANES)
    messages = pl.pallas_call(
        functools.partial(main_kernel, plan, chunk),
        out_shape=[jax.ShapeDtypeStruct(block, f32)] * plan.messages,
        in_specs=[whole()] * len(arrays),
        out_specs=[whole()] * plan.messages,
        scratch_shapes=[
            pltpu.VMEM((sums_rows, chunk * plan.slots), bf16),
            pltpu.VMEM((len(plan.ends), plan.share // 2, LANES), f32),
            pltpu.VMEM((sums_rows, plan.share * BINS), f32),
        ],
        cost_estimate=pl.CostEstimate(
            flops=2 * sums_rows * plan.devices * plan.slots * plan.share * BINS,
            bytes_accessed=4 * plan.devices * plan.sent_rows * plan.slots,
            transcendentals=0,
        ),
        compiler_params=params,
        name="gains",
    )(*arrays)

    messages, far = lax.optimization_barrier((list(messages), far))
    scores = sum(far, scores)
    score_parts = [scores] + ([flipped(scores, 1)] if plan.permuted else [])
    if plan.permuted:
        messages = exchanged(messages, plan.half, plan.devices)
    else:
        halves = [list(range(plan.half)), list(range(plan.half, plan.devices))]
        messages = [lax.all_to_all(messages[0], "rows", 0, 0, axis_index_groups=halves)]
    shapes = [
        jax.ShapeDtypeStruct((count, BINS), f32) for count in plan.returned
    ]
    shapes.append(jax.ShapeDtypeStruct((plan.levels, 1, 2, plan.outs), f32))
    return pl.pallas_call(
        functools.partial(final_kernel, plan),
        out_shape=tuple(shapes),
        in_specs=[whole()] * (plan.messages + len(score_parts)),
        out_specs=tuple(whole() for _ in shapes),
        compiler_params=params,
        name="finish",
    )(*messages, *score_parts)


def solution(mesh):
    placed = (P("rows", None), P("rows"), P("feat", "rows"), P(None, "rows"), P(), P())
    return jax.shard_map(
        on_device,
        mesh=mesh,
        in_specs=placed,
        out_specs=(
            P("rows", "feat"),
            P("rows", "feat"),
            P("rows", "feat"),
            P(None, "rows", None, None),
        ),
        check_vma=False,
    )
```

```python
import functools

import jax
import jax.numpy as jnp
from jax import lax
from jax.experimental import pallas as pl
from jax.experimental.pallas import tpu as pltpu
from jax.sharding import PartitionSpec as P

BINS = 64
LANES = 128
TILE = 16
OUT_SPLIT = 2
PIECES = 2
penalty = 1.0
VMEM_BYTES = 32 * 2**20

bf16 = jnp.bfloat16
f32 = jnp.float32
NT = (((1,), (1,)), ((), ()))
PERMUTED = 8


def div(value, by):
    return value // by if isinstance(value, int) else lax.div(value, jnp.int32(by))


def rem(value, by):
    return value % by if isinstance(value, int) else lax.rem(value, jnp.int32(by))


def round_up(value, unit):
    return -(-value // unit) * unit


def whole(*_):
    return pl.BlockSpec(memory_space=pltpu.VMEM)


def aligned(value, unit):
    return value if isinstance(value, int) or unit % 8 else pl.multiple_of(value, 8)


def target(me, slot, count):
    return rem(me + slot, count)


def source_of(me, slot, count):
    return rem(me + (count - slot), count)


def exchanged(blocks, group, count):
    moved = [blocks[0]]
    for slot in range(1, group):
        route = [(p, p - p % group + (p + slot) % group) for p in range(count)]
        moved.append(lax.ppermute(blocks[slot], "rows", route))
    return moved


def spread(parcels, plan):
    feat_axis = lax.axis_size("feat")
    moved = []
    for slot, block in enumerate(parcels):
        route = []
        for p in range(plan.devices * feat_axis):
            row, panel = divmod(p, feat_axis)
            row = (row + plan.offsets[panel % 2][slot]) % plan.devices
            route.append((p, row * feat_axis + panel))
        moved.append(lax.ppermute(block, ("rows", "feat"), route))
    return moved


class Plan:
    def __init__(self, rows_axis, feat_axis, gradients, bin_words, children):
        self.devices = rows_axis
        self.half = rows_axis // 2
        self.row_dev, self.outs = gradients.shape
        self.words = bin_words.shape[0]
        self.feats = 2 * self.words
        self.levels = children.shape[0]
        self.leaves = 2 ** (self.levels - 1)
        self.slots = round_up(self.row_dev * 3 // 4, LANES)
        self.shares = self.half // OUT_SPLIT
        self.share = self.feats // self.shares
        self.outs_dev = self.outs // OUT_SPLIT
        self.permuted = rows_axis <= PERMUTED and feat_axis % 2 == 0
        self.panels = 2 if self.permuted else 1
        self.parcels = rows_axis // 2 if self.permuted else 1
        self.offsets = [
            sorted(range(first, rows_axis, 2), key=lambda k: (abs(k - rows_axis // 2), k)) for first in range(2)
        ]
        self.codes = self.panels * self.feats
        self.splits = 2 ** (self.levels + 1) - 2
        self.split_rows = round_up(self.splits, TILE)
        self.grad_at = self.share
        self.misc_at = self.share + self.outs_dev
        self.score_rows = 2 * self.levels + 1
        self.spans = self.slots // LANES
        self.misc_rows = 2 + -(-self.score_rows * PIECES // self.spans)
        self.base_rows = round_up(self.misc_at + self.misc_rows, 8)
        self.sent_rows = self.base_rows + (self.panels - 1) * self.share
        self.sizes = [self.devices >> (level + 1) for level in range(self.levels)]
        self.returned = [self.feats // size for size in self.sizes]
        self.needed = [min(self.share, count) for count in self.returned]
        self.block = min(self.needed)
        self.step = min(8, self.share)
        self.tiles = [
            (start + k, start + k + self.block // 2)
            for start in range(0, self.share, self.block)
            for k in range(self.block // 2)
        ]
        self.level_at = [sum(self.needed[:level]) // 2 for level in range(self.levels)]
        self.gain_rows = sum(self.needed) // 2
        self.message = round_up(self.gain_rows, 8)
        self.ends = [(level, n) for level in reversed(range(self.levels)) for n in range(2**level)]
        self.messages = self.half if self.permuted else 1

    def code_row(self, feature):
        return feature // 2 + (feature % 2) * (self.share // 2)


def split_words(words):
    codes = (jnp.bitwise_and(words, 63), jnp.bitwise_and(jnp.right_shift(words, 6), 63))
    return jnp.concatenate(codes, axis=0).astype(f32).astype(bf16)


def fetch_kernel(plan, *refs):
    inputs, refs = refs[:6], refs[6:]
    (grad_ref, word_ref, row_ref, pick_ref, chosen_ref, packed_ref), refs = refs[:6], refs[6:]
    hess_ref, child_ref, feature_ref, bin_ref, table, sems = refs
    targets = (grad_ref, hess_ref, child_ref, feature_ref, bin_ref, word_ref)
    copies = [
        pltpu.make_async_copy(source, into, sems.at[i])
        for i, (source, into) in enumerate(zip(inputs, targets, strict=True))
    ]
    for copy in copies:
        copy.start()
    rows = plan.row_dev
    ahead = jnp.where(
        lax.broadcasted_iota(jnp.int32, (rows, rows), 0) <= lax.broadcasted_iota(jnp.int32, (rows, rows), 1), 1.0, 0.0
    ).astype(bf16)
    for copy in copies:
        copy.wait()

    nodes = [child_ref[0:1, :]]
    for level in range(1, plan.levels):
        nodes.append(nodes[-1] * 2 + child_ref[level : level + 1, :])
    row_ref[...] = jnp.zeros_like(row_ref)
    row_ref[0:1, :] = hess_ref[...].astype(f32).reshape(1, rows)
    for level, node in enumerate(nodes):
        row_ref[level + 1 : level + 2, :] = node.astype(f32)

    at = lax.broadcasted_iota(jnp.int32, (TILE, rows), 0)
    side = jnp.where(at == nodes[0], 1.0, 0.0)
    rank = jnp.dot(side.astype(bf16), ahead, preferred_element_type=f32)
    slot = jnp.where(side > 0.0, rank - 1.0, -1.0)
    slot_ids = lax.broadcasted_iota(jnp.int32, (plan.slots, rows), 0).astype(f32)
    for half in range(2):
        chosen_ref[half] = jnp.where(slot_ids == slot[half : half + 1], 1.0, 0.0).astype(bf16)

    turn = jnp.where(
        lax.broadcasted_iota(jnp.int32, (plan.outs, plan.outs), 0)
        == lax.broadcasted_iota(jnp.int32, (plan.outs, plan.outs), 1),
        1.0,
        0.0,
    ).astype(bf16)
    own_at = plan.outs + plan.feats
    table[: plan.outs] = lax.dot_general(turn, grad_ref[...], NT, preferred_element_type=f32).astype(bf16)
    table[plan.outs : own_at] = split_words(word_ref[...])
    leaf = jnp.bitwise_and(nodes[-1], plan.leaves - 1).astype(f32)
    table[own_at:] = jnp.where(at == 0, row_ref[0:1, :], jnp.where(at == 1, leaf, 0.0)).astype(bf16)
    for half in range(2):
        packed_ref[half] = lax.dot_general(table[...], chosen_ref[half], NT, preferred_element_type=f32)

    panel = lax.axis_index("feat")
    lane = lax.broadcasted_iota(jnp.int32, (1, plan.codes), 1)
    pick_ref[...] = jnp.zeros_like(pick_ref)
    for slot in range(plan.splits):
        feature = feature_ref[slot]
        owner = lax.div(feature, jnp.int32(plan.feats))
        inner = feature - owner * plan.feats
        held = jnp.bitwise_xor(owner, panel)
        place = held * plan.feats + inner // 2 + lax.rem(inner, 2) * plan.words
        place = jnp.where(held < plan.panels, place, plan.codes)
        pick_ref[0, slot : slot + 1, :] = jnp.where(lane == place, 1.0, 0.0)
        pick_ref[1, slot : slot + 1, :] = jnp.full((1, plan.codes), bin_ref[slot].astype(f32))
        pick_ref[2, slot : slot + 1, :] = jnp.full((1, plan.codes), jnp.where(held < plan.panels, 1.0, 0.0))


def prep_kernel(plan, *refs):
    (grad_ref, row_ref, pick_ref, chosen_ref, own_ref), refs = refs[:5], refs[5:]
    word_refs, send_refs = refs[: plan.panels], refs[plan.panels : plan.panels + plan.parcels]
    table, packed, lines, marked = refs[plan.panels + plan.parcels :]
    own_at = plan.outs + plan.feats
    grads = grad_ref[...]
    hess = row_ref[0:1, :]
    nodes = [row_ref[level + 1 : level + 2, :] for level in range(plan.levels)]

    for which, word_ref in enumerate(word_refs):
        table[which * plan.feats : (which + 1) * plan.feats] = split_words(word_ref[...])
    if plan.panels > 1:
        for half in range(2):
            packed[half] = lax.dot_general(table[plan.feats :], chosen_ref[half], NT, preferred_element_type=f32)

    ends = [(level, node) for level in range(plan.levels) for node in range(2 ** (level + 1))]
    code = jnp.dot(pick_ref[0].astype(bf16), table[...], preferred_element_type=f32)
    marked[...] = jnp.zeros_like(marked)
    for slot, (level, node) in enumerate(ends):
        here = jnp.where(nodes[level] == node, pick_ref[2, slot : slot + 1, 0:1], 0.0)
        left = jnp.where(code[slot : slot + 1] <= pick_ref[1, slot : slot + 1, 0:1], here, 0.0)
        marked[slot : slot + 1, :] = left
        marked[plan.split_rows + slot : plan.split_rows + slot + 1, :] = here - left
    mark = marked[...]
    sums = jnp.dot(mark.astype(bf16), grads, preferred_element_type=f32)
    curv = jnp.sum(mark * hess, axis=1, keepdims=True)
    shape = (2 * plan.split_rows, plan.outs)
    curv = jnp.broadcast_to(curv, shape)
    lane = lax.broadcasted_iota(jnp.int32, (1, plan.outs), 1)
    blank = jnp.zeros((1, LANES), f32)
    filler = jnp.zeros((plan.base_rows - plan.misc_at - plan.misc_rows, plan.slots), f32)
    for leaf in range(2 * plan.leaves):
        places = [
            side * plan.split_rows + 2 ** (level + 1) - 2 + (leaf >> (plan.levels - 1 - level))
            for side in range(2)
            for level in range(plan.levels)
        ]
        spread_curv = jnp.zeros((1, plan.outs), f32)
        for i, at in enumerate(places):
            spread_curv = jnp.where(lane == i, curv[at : at + 1], spread_curv)
        parts = []
        for value in [*(sums[at : at + 1] for at in places), spread_curv]:
            for _ in range(PIECES):
                parts.append(value.astype(bf16).astype(f32))
                value = value - parts[-1]
        parts += [blank] * (-len(parts) % plan.spans)
        parts = [jnp.concatenate(parts[i : i + plan.spans], axis=1) for i in range(0, len(parts), plan.spans)]
        lines[leaf] = jnp.concatenate(parts + ([filler] if filler.shape[0] else []), axis=0)

    word_share = plan.share // 2
    parity = rem(lax.axis_index("feat"), plan.panels)
    for slot in range(plan.parcels if plan.permuted else plan.devices):
        device = slot
        if plan.permuted:
            offset = jnp.where(parity == 0, plan.offsets[0][slot], plan.offsets[1][slot])
            device = rem(lax.axis_index("rows") + offset, plan.devices)
        half, place = div(device, plan.half), rem(device, plan.half)
        share, split = div(place, OUT_SPLIT), rem(place, OUT_SPLIT)

        def codes(ref, first):
            at = [first + odd * plan.words + share * word_share for odd in range(2)]
            return [ref[half, pl.ds(aligned(k, word_share), word_share), :] for k in at]

        message = [
            *codes(own_ref, plan.outs),
            own_ref[half, pl.ds(aligned(split * plan.outs_dev, plan.outs_dev), plan.outs_dev), :],
            own_ref[half, own_at : own_at + 2, :],
            lines[div(device, plan.devices // (2 * plan.leaves))],
        ]
        if plan.permuted:
            send_refs[slot][...] = jnp.concatenate(message + codes(packed, 0), axis=0).astype(bf16)
        else:
            send_refs[0][slot] = jnp.concatenate(message, axis=0).astype(bf16)


def main_kernel(plan, chunk, *refs):
    got_refs, refs = refs[: plan.parcels], refs[plan.parcels :]
    if plan.permuted:
        got_refs, refs = got_refs + tuple(refs[0].at[k] for k in range(plan.parcels)), refs[1:]
    out_refs, (weighted, gain_table, left_sums) = refs[: plan.messages], refs[plan.messages :]
    rows = plan.slots
    leaves, outs_dev, step = plan.leaves, plan.outs_dev, plan.step
    hess_at = leaves * outs_dev
    order = [feature for tile in plan.tiles for feature in tile]
    level_bins = lax.broadcasted_iota(jnp.int32, (BINS, rows), 0).astype(f32).astype(bf16)
    leaf_ids = lax.broadcasted_iota(jnp.int32, (TILE, rows), 0).astype(f32)
    zero = jnp.zeros((), bf16)
    one = jnp.ones((), bf16)

    def parcel(source):
        return got_refs[source] if plan.permuted else got_refs[0].at[source]

    def marked(source, feature):
        row = plan.code_row(feature)
        code = jnp.broadcast_to(parcel(source)[row : row + 1, :], (BINS, rows))
        return jnp.where(code <= level_bins, one, zero)

    def add_chunk(first, fresh):
        for k in range(chunk):
            source = first + k
            columns = slice(k * rows, (k + 1) * rows)
            misc = parcel(source)[plan.misc_at : plan.misc_at + 2, :].astype(f32)
            hess, node = misc[0:1], misc[1:2]
            weighted[hess_at : hess_at + TILE, columns] = jnp.where(leaf_ids == node, hess, 0.0).astype(bf16)
            node_wide = jnp.broadcast_to(node, (outs_dev, rows)).astype(bf16)
            grads = parcel(source)[plan.grad_at : plan.grad_at + outs_dev, :]
            for leaf in range(leaves):
                weighted[leaf * outs_dev : (leaf + 1) * outs_dev, columns] = jnp.where(
                    node_wide == jnp.asarray(leaf, bf16), grads, zero
                )
        for group in range(plan.share // step):
            features = order[group * step : (group + 1) * step]
            marks = jnp.concatenate(
                [
                    jnp.concatenate([marked(first + k, feature) for feature in features], axis=0)
                    for k in range(chunk)
                ],
                axis=1,
            )
            part = lax.dot_general(weighted[...], marks, NT, preferred_element_type=f32)
            span = slice(group * step * BINS, (group + 1) * step * BINS)
            if count == 1:
                add_gains(group, part)
            elif fresh:
                left_sums[:, span] = part
            else:
                left_sums[:, span] += part

    known = []

    def add_gains(group, sums):
        left = [sums[leaf * outs_dev : (leaf + 1) * outs_dev] for leaf in range(leaves)]
        hess = [sums[hess_at + leaf : hess_at + leaf + 1] for leaf in range(leaves)]
        for level in reversed(range(plan.levels - 1)):
            past = len(left) - 2 ** (level + 1)
            for n in range(past, len(left), 2):
                left.append(left[n] + left[n + 1])
                hess.append(hess[n] + hess[n + 1])
        hess = jnp.concatenate(hess, axis=0) + penalty
        if not known:
            totals = [part[:, BINS - 1 : BINS] for part in left]
            squares = jnp.concatenate([jnp.sum(t * t, axis=0, keepdims=True) for t in totals], axis=0)
            hess_total = hess[:, BINS - 1 : BINS] + penalty
            known.extend([totals, hess_total, squares / (hess_total - penalty)])
        totals, hess_total, whole_part = known
        on_left = jnp.concatenate([jnp.sum(part * part, axis=0, keepdims=True) for part in left], axis=0)
        rights = [t - part for t, part in zip(totals, left, strict=True)]
        on_right = jnp.concatenate([jnp.sum(part * part, axis=0, keepdims=True) for part in rights], axis=0)
        gains = (on_left / hess + on_right / (hess_total - hess) - whole_part) / plan.outs
        for end in range(len(plan.ends)):
            for tile in range(step // 2):
                at = group * (step // 2) + tile
                gain_table[end, at : at + 1, :] = gains[end : end + 1, tile * LANES : (tile + 1) * LANES]

    count = plan.devices // chunk
    add_chunk(0, True)
    if count > 1:
        lax.fori_loop(1, count, lambda c, _: (add_chunk(c * chunk, False), 0)[1], 0)
        for group in range(plan.share // step):
            add_gains(group, left_sums[:, group * step * BINS : (group + 1) * step * BINS])
    me = rem(lax.axis_index("rows"), plan.half)
    for slot in range(plan.half):
        place = target(me, slot, plan.half) if plan.permuted else slot
        out_ref = out_refs[slot] if plan.permuted else out_refs[0].at[slot]
        for level in range(plan.levels):
            count = plan.needed[level] // 2
            end = plan.ends.index((level, 0)) + div(place, plan.sizes[level])
            first = rem(rem(place, plan.sizes[level]) * plan.returned[level], plan.share) // 2
            if not isinstance(first, int) and count % 8 == 0:
                first = pl.multiple_of(first, 8)
            at = plan.level_at[level]
            out_ref[at : at + count, :] = gain_table[end, pl.ds(first, count), :]
        if plan.message > plan.gain_rows:
            out_ref[plan.gain_rows :, :] = jnp.zeros((plan.message - plan.gain_rows, LANES), f32)


def score_kernel(plan, *refs):
    got_refs, (score_ref, *passed) = refs[: plan.parcels], refs[plan.parcels :]
    tail = slice(plan.misc_at + 2, plan.misc_at + plan.misc_rows)
    total = jnp.zeros((plan.misc_rows - 2, plan.slots), f32)
    if plan.permuted:
        for source, ref in enumerate(got_refs):
            passed[0][source, : plan.share] = ref[plan.base_rows :, :]
            passed[0][source, plan.share :] = ref[plan.share : plan.base_rows, :]
            total = total + ref[tail, :].astype(f32)
    else:
        total = lax.fori_loop(0, plan.devices, lambda k, sums: sums + got_refs[0][k, tail, :].astype(f32), total)
    score_ref[...] = jnp.zeros_like(score_ref)
    for i in range(plan.score_rows):
        value = 0.0
        for piece in reversed(range(PIECES)):
            line, span = divmod(i * PIECES + piece, plan.spans)
            value = value + total[line : line + 1, span * LANES : (span + 1) * LANES]
        score_ref[i : i + 1, :] = value


def final_kernel(plan, *refs):
    got_refs, refs = refs[: plan.messages], refs[plan.messages :]
    score_refs, refs = refs[: -plan.levels - 1], refs[-plan.levels - 1 :]
    *gain_refs, child_ref = refs
    me = rem(lax.axis_index("rows"), plan.half)
    side = plan.block // 2
    arrived = []
    for slot in range(plan.half):
        place = source_of(me, slot, plan.half) if plan.permuted else slot
        arrived.append((div(place, OUT_SPLIT), got_refs[slot] if plan.permuted else got_refs[0].at[slot]))
    for level, gain_ref in enumerate(gain_refs):
        rows = slice(plan.level_at[level], plan.level_at[level] + plan.needed[level] // 2)
        first = div(rem(me, plan.sizes[level]) * plan.returned[level], plan.share)
        for turn in range(plan.returned[level] // plan.needed[level]):
            value = 0.0
            for share, ref in arrived:
                value = value + jnp.where(share == first + turn, ref[rows, :], 0.0)
            for start in range(0, plan.needed[level], plan.block):
                part = value[start // 2 : start // 2 + side]
                at = turn * plan.share + start
                gain_ref[at : at + side, :] = part[:, :BINS]
                gain_ref[at + side : at + 2 * side, :] = part[:, BINS:]
    sums = score_refs[0][...]
    for score_ref in score_refs[1:]:
        sums = sums + score_ref[...]
    curv = sums[2 * plan.levels : 2 * plan.levels + 1, :]
    for level in range(plan.levels):
        for side in range(2):
            line = side * plan.levels + level
            scale = jnp.sqrt(curv[:, line : line + 1] + penalty)
            child_ref[level, 0, side : side + 1, :] = -sums[line : line + 1, :] / scale


def flipped(block, bits):
    count = lax.axis_size("feat")
    return lax.ppermute(block, "feat", [(p, p ^ bits) for p in range(count)])


def on_device(gradients, hessians, bin_words, children, split_feature, split_bin):
    plan = Plan(lax.axis_size("rows"), lax.axis_size("feat"), gradients, bin_words, children)
    params = pltpu.CompilerParams(vmem_limit_bytes=VMEM_BYTES)

    inputs = (gradients, hessians, children, split_feature, split_bin, bin_words)
    crossed = [flipped(bin_words, 1)] if plan.permuted else []
    row_dev, table_rows = plan.row_dev, plan.outs + plan.feats + TILE
    grads, words, row_values, picks, chosen, own_part = pl.pallas_call(
        functools.partial(fetch_kernel, plan),
        out_shape=(
            jax.ShapeDtypeStruct(gradients.shape, bf16),
            jax.ShapeDtypeStruct(bin_words.shape, jnp.int32),
            jax.ShapeDtypeStruct((8, row_dev), f32),
            jax.ShapeDtypeStruct((3, plan.split_rows, plan.codes), f32),
            jax.ShapeDtypeStruct((2, plan.slots, row_dev), bf16),
            jax.ShapeDtypeStruct((2, table_rows, plan.slots), f32),
        ),
        in_specs=[pl.BlockSpec(memory_space=pltpu.HBM)] * len(inputs),
        out_specs=[whole()] * 6,
        scratch_shapes=[
            pltpu.VMEM(hessians.shape, bf16),
            pltpu.VMEM(children.shape, jnp.int32),
            pltpu.SMEM(split_feature.shape, jnp.int32),
            pltpu.SMEM(split_bin.shape, jnp.int32),
            pltpu.VMEM((table_rows, row_dev), bf16),
            pltpu.SemaphoreType.DMA((len(inputs),)),
        ],
        cost_estimate=pl.CostEstimate(flops=10**9, bytes_accessed=10**6, transcendentals=0),
        compiler_params=params,
        name="fetch",
    )(*(pltpu.with_memory_space_constraint(a, pltpu.HBM) for a in inputs))
    parcel = (plan.sent_rows, plan.slots) if plan.permuted else (plan.devices, plan.sent_rows, plan.slots)
    parcels = pl.pallas_call(
        functools.partial(prep_kernel, plan),
        out_shape=[jax.ShapeDtypeStruct(parcel, bf16)] * plan.parcels,
        in_specs=[whole()] * (5 + plan.panels),
        out_specs=[whole()] * plan.parcels,
        scratch_shapes=[
            pltpu.VMEM((plan.codes, row_dev), bf16),
            pltpu.VMEM((2, plan.feats, plan.slots), f32),
            pltpu.VMEM((2 * plan.leaves, plan.base_rows - plan.misc_at - 2, plan.slots), f32),
            pltpu.VMEM((2 * plan.split_rows, row_dev), f32),
        ],
        compiler_params=params,
        name="prep",
    )(grads, row_values, picks, chosen, own_part, words, *crossed)

    if plan.permuted:
        got = spread(parcels, plan)
    else:
        got = [lax.all_to_all(parcels[0], "rows", 0, 0)]
    shapes = [jax.ShapeDtypeStruct((8, plan.outs), f32)]
    if plan.permuted:
        shapes.append(jax.ShapeDtypeStruct((plan.parcels, plan.base_rows, plan.slots), bf16))
    scores, *passed = pl.pallas_call(
        functools.partial(score_kernel, plan),
        out_shape=shapes,
        in_specs=[whole()] * plan.parcels,
        out_specs=[whole()] * len(shapes),
        compiler_params=params,
        name="scores",
    )(*got)
    arrays = got + [flipped(block, 1) for block in passed]
    far = [flipped(scores, away) for away in range(plan.panels, lax.axis_size("feat"), plan.panels)]

    chunk = max(1, min(plan.devices, 4096 // plan.slots))
    while plan.devices % chunk:
        chunk -= 1
    sums_rows = plan.leaves * plan.outs_dev + TILE
    block = (plan.message, LANES) if plan.permuted else (plan.half, plan.message, LANES)
    messages = pl.pallas_call(
        functools.partial(main_kernel, plan, chunk),
        out_shape=[jax.ShapeDtypeStruct(block, f32)] * plan.messages,
        in_specs=[whole()] * len(arrays),
        out_specs=[whole()] * plan.messages,
        scratch_shapes=[
            pltpu.VMEM((sums_rows, chunk * plan.slots), bf16),
            pltpu.VMEM((len(plan.ends), plan.share // 2, LANES), f32),
            pltpu.VMEM((sums_rows, plan.share * BINS), f32),
        ],
        cost_estimate=pl.CostEstimate(
            flops=2 * sums_rows * plan.devices * plan.slots * plan.share * BINS,
            bytes_accessed=4 * plan.devices * plan.sent_rows * plan.slots,
            transcendentals=0,
        ),
        compiler_params=params,
        name="gains",
    )(*arrays)

    messages, far = lax.optimization_barrier((list(messages), far))
    scores = sum(far, scores)
    score_parts = [scores] + ([flipped(scores, 1)] if plan.permuted else [])
    if plan.permuted:
        messages = exchanged(messages, plan.half, plan.devices)
    else:
        halves = [list(range(plan.half)), list(range(plan.half, plan.devices))]
        messages = [lax.all_to_all(messages[0], "rows", 0, 0, axis_index_groups=halves)]
    shapes = [
        jax.ShapeDtypeStruct((count, BINS), f32) for count in plan.returned
    ]
    shapes.append(jax.ShapeDtypeStruct((plan.levels, 1, 2, plan.outs), f32))
    return pl.pallas_call(
        functools.partial(final_kernel, plan),
        out_shape=tuple(shapes),
        in_specs=[whole()] * (plan.messages + len(score_parts)),
        out_specs=tuple(whole() for _ in shapes),
        compiler_params=params,
        name="finish",
    )(*messages, *score_parts)


def solution(mesh):
    placed = (P("rows", None), P("rows"), P("feat", "rows"), P(None, "rows"), P(), P())
    return jax.shard_map(
        on_device,
        mesh=mesh,
        in_specs=placed,
        out_specs=(
            P("rows", "feat"),
            P("rows", "feat"),
            P("rows", "feat"),
            P(None, "rows", None, None),
        ),
        check_vma=False,
    )
```

```python
import functools

import jax
import jax.numpy as jnp
from jax import lax
from jax.experimental import pallas as pl
from jax.experimental.pallas import tpu as pltpu
from jax.sharding import PartitionSpec as P

BINS = 64
LANES = 128
TILE = 16
OUT_SPLIT = 2
PIECES = 2
penalty = 1.0
VMEM_BYTES = 32 * 2**20

bf16 = jnp.bfloat16
f32 = jnp.float32
NT = (((1,), (1,)), ((), ()))
PERMUTED = 8


def div(value, by):
    return value // by if isinstance(value, int) else lax.div(value, jnp.int32(by))


def rem(value, by):
    return value % by if isinstance(value, int) else lax.rem(value, jnp.int32(by))


def round_up(value, unit):
    return -(-value // unit) * unit


def whole(*_):
    return pl.BlockSpec(memory_space=pltpu.VMEM)


def aligned(value, unit):
    return value if isinstance(value, int) or unit % 8 else pl.multiple_of(value, 8)


def target(me, slot, count):
    return rem(me + slot, count)


def source_of(me, slot, count):
    return rem(me + (count - slot), count)


def exchanged(blocks, group, count):
    moved = [blocks[0]]
    for slot in range(1, group):
        route = [(p, p - p % group + (p + slot) % group) for p in range(count)]
        moved.append(lax.ppermute(blocks[slot], "rows", route))
    return moved


def spread(parcels, plan):
    feat_axis = lax.axis_size("feat")
    moved = []
    for slot, block in enumerate(parcels):
        route = []
        for p in range(plan.devices * feat_axis):
            row, panel = divmod(p, feat_axis)
            row = (row + plan.offsets[panel % 2][slot]) % plan.devices
            route.append((p, row * feat_axis + panel))
        moved.append(lax.ppermute(block, ("rows", "feat"), route))
    return moved


class Plan:
    def __init__(self, rows_axis, feat_axis, gradients, bin_words, children):
        self.devices = rows_axis
        self.half = rows_axis // 2
        self.row_dev, self.outs = gradients.shape
        self.words = bin_words.shape[0]
        self.feats = 2 * self.words
        self.levels = children.shape[0]
        self.leaves = 2 ** (self.levels - 1)
        self.slots = round_up(self.row_dev * 3 // 4, LANES)
        self.shares = self.half // OUT_SPLIT
        self.share = self.feats // self.shares
        self.outs_dev = self.outs // OUT_SPLIT
        self.permuted = rows_axis <= PERMUTED and feat_axis % 2 == 0
        self.panels = 2 if self.permuted else 1
        self.parcels = rows_axis // 2 if self.permuted else 1
        self.offsets = [
            sorted(range(first, rows_axis, 2), key=lambda k: (abs(k - rows_axis // 2), k)) for first in range(2)
        ]
        self.codes = self.panels * self.feats
        self.splits = 2 ** (self.levels + 1) - 2
        self.split_rows = round_up(self.splits, TILE)
        self.grad_at = self.share
        self.misc_at = self.share + self.outs_dev
        self.score_rows = 2 * self.levels + 1
        self.spans = self.slots // LANES
        self.misc_rows = 2 + -(-self.score_rows * PIECES // self.spans)
        self.base_rows = round_up(self.misc_at + self.misc_rows, 8)
        self.sent_rows = self.base_rows + (self.panels - 1) * self.share
        self.sizes = [self.devices >> (level + 1) for level in range(self.levels)]
        self.returned = [self.feats // size for size in self.sizes]
        self.needed = [min(self.share, count) for count in self.returned]
        self.block = min(self.needed)
        self.step = min(16, self.share)
        self.tiles = [
            (start + k, start + k + self.block // 2)
            for start in range(0, self.share, self.block)
            for k in range(self.block // 2)
        ]
        self.level_at = [sum(self.needed[:level]) // 2 for level in range(self.levels)]
        self.gain_rows = sum(self.needed) // 2
        self.message = round_up(self.gain_rows, 8)
        self.ends = [(level, n) for level in reversed(range(self.levels)) for n in range(2**level)]
        self.messages = self.half if self.permuted else 1

    def code_row(self, feature):
        return feature // 2 + (feature % 2) * (self.share // 2)


def fetch_kernel(plan, *refs):
    inputs, refs = refs[:6], refs[6:]
    (grad_ref, word_ref, row_ref, pick_ref, chosen_ref), (hess_ref, child_ref, feature_ref, bin_ref, sems) = refs[:5], refs[5:]
    targets = (grad_ref, hess_ref, child_ref, feature_ref, bin_ref, word_ref)
    copies = [
        pltpu.make_async_copy(source, into, sems.at[i])
        for i, (source, into) in enumerate(zip(inputs, targets, strict=True))
    ]
    for copy in copies:
        copy.start()
    rows = plan.row_dev
    ahead = jnp.where(
        lax.broadcasted_iota(jnp.int32, (rows, rows), 0) <= lax.broadcasted_iota(jnp.int32, (rows, rows), 1), 1.0, 0.0
    ).astype(bf16)
    for copy in copies:
        copy.wait()

    nodes = [child_ref[0:1, :]]
    for level in range(1, plan.levels):
        nodes.append(nodes[-1] * 2 + child_ref[level : level + 1, :])
    row_ref[...] = jnp.zeros_like(row_ref)
    row_ref[0:1, :] = hess_ref[...].astype(f32).reshape(1, rows)
    for level, node in enumerate(nodes):
        row_ref[level + 1 : level + 2, :] = node.astype(f32)

    at = lax.broadcasted_iota(jnp.int32, (TILE, rows), 0)
    side = jnp.where(at == nodes[0], 1.0, 0.0)
    rank = jnp.dot(side.astype(bf16), ahead, preferred_element_type=f32)
    slot = jnp.where(side > 0.0, rank - 1.0, -1.0)
    slot_ids = lax.broadcasted_iota(jnp.int32, (plan.slots, rows), 0).astype(f32)
    for half in range(2):
        chosen_ref[half] = jnp.where(slot_ids == slot[half : half + 1], 1.0, 0.0).astype(bf16)

    panel = lax.axis_index("feat")
    lane = lax.broadcasted_iota(jnp.int32, (1, plan.codes), 1)
    pick_ref[...] = jnp.zeros_like(pick_ref)
    for slot in range(plan.splits):
        feature = feature_ref[slot]
        owner = lax.div(feature, jnp.int32(plan.feats))
        inner = feature - owner * plan.feats
        held = jnp.bitwise_xor(owner, panel)
        place = held * plan.words + inner // 2 + lax.rem(inner, 2) * (plan.panels * plan.words)
        place = jnp.where(held < plan.panels, place, plan.codes)
        pick_ref[0, slot : slot + 1, :] = jnp.where(lane == place, 1.0, 0.0)
        pick_ref[1, slot : slot + 1, :] = jnp.full((1, plan.codes), bin_ref[slot].astype(f32))
        pick_ref[2, slot : slot + 1, :] = jnp.full((1, plan.codes), jnp.where(held < plan.panels, 1.0, 0.0))


def prep_kernel(plan, *refs):
    (grad_ref, row_ref, pick_ref, chosen_ref), refs = refs[:4], refs[4:]
    word_refs, send_refs = refs[: plan.panels], refs[plan.panels : plan.panels + plan.parcels]
    table, packed, lines, marked = refs[plan.panels + plan.parcels :]
    rows = plan.row_dev
    low_at, high_at = plan.outs, plan.outs + plan.panels * plan.words
    own_at = plan.outs + plan.codes
    grads = grad_ref[...]
    hess = row_ref[0:1, :]
    nodes = [row_ref[level + 1 : level + 2, :] for level in range(plan.levels)]

    turn = jnp.where(
        lax.broadcasted_iota(jnp.int32, (plan.outs, plan.outs), 0)
        == lax.broadcasted_iota(jnp.int32, (plan.outs, plan.outs), 1),
        1.0,
        0.0,
    ).astype(bf16)
    table[0:low_at] = lax.dot_general(turn, grads, NT, preferred_element_type=f32).astype(bf16)
    for which, word_ref in enumerate(word_refs):
        words = word_ref[...]
        low = jnp.bitwise_and(words, 63)
        high = jnp.bitwise_and(jnp.right_shift(words, 6), 63)
        for first, codes in ((low_at, low), (high_at, high)):
            at = first + which * plan.words
            table[at : at + plan.words] = codes.astype(f32).astype(bf16)
    at = lax.broadcasted_iota(jnp.int32, (TILE, rows), 0)
    leaf = nodes[-1] - nodes[0] * plan.leaves
    table[own_at:] = jnp.where(at == 0, hess, jnp.where(at == 1, leaf, 0.0)).astype(bf16)
    for half in range(2):
        packed[half] = lax.dot_general(table[...], chosen_ref[half], NT, preferred_element_type=f32)

    ends = [(level, node) for level in range(plan.levels) for node in range(2 ** (level + 1))]
    code = jnp.dot(pick_ref[0].astype(bf16), table[low_at:own_at], preferred_element_type=f32)
    marked[...] = jnp.zeros_like(marked)
    for slot, (level, node) in enumerate(ends):
        here = jnp.where(nodes[level] == node, pick_ref[2, slot : slot + 1, 0:1], 0.0)
        left = jnp.where(code[slot : slot + 1] <= pick_ref[1, slot : slot + 1, 0:1], here, 0.0)
        marked[slot : slot + 1, :] = left
        marked[plan.split_rows + slot : plan.split_rows + slot + 1, :] = here - left
    mark = marked[...]
    sums = jnp.dot(mark.astype(bf16), grads, preferred_element_type=f32)
    curv = jnp.sum(mark * hess, axis=1, keepdims=True)
    shape = (2 * plan.split_rows, plan.outs)
    curv = jnp.broadcast_to(curv, shape)
    lane = lax.broadcasted_iota(jnp.int32, (1, plan.outs), 1)
    blank = jnp.zeros((1, LANES), f32)
    filler = jnp.zeros((plan.base_rows - plan.misc_at - plan.misc_rows, plan.slots), f32)
    for leaf in range(2 * plan.leaves):
        places = [
            side * plan.split_rows + 2 ** (level + 1) - 2 + (leaf >> (plan.levels - 1 - level))
            for side in range(2)
            for level in range(plan.levels)
        ]
        spread_curv = jnp.zeros((1, plan.outs), f32)
        for i, at in enumerate(places):
            spread_curv = jnp.where(lane == i, curv[at : at + 1], spread_curv)
        parts = []
        for value in [*(sums[at : at + 1] for at in places), spread_curv]:
            for _ in range(PIECES):
                parts.append(value.astype(bf16).astype(f32))
                value = value - parts[-1]
        parts += [blank] * (-len(parts) % plan.spans)
        parts = [jnp.concatenate(parts[i : i + plan.spans], axis=1) for i in range(0, len(parts), plan.spans)]
        lines[leaf] = jnp.concatenate(parts + ([filler] if filler.shape[0] else []), axis=0)

    word_share = plan.share // 2
    parity = rem(lax.axis_index("feat"), plan.panels)
    for slot in range(plan.parcels if plan.permuted else plan.devices):
        device = slot
        if plan.permuted:
            offset = jnp.where(parity == 0, plan.offsets[0][slot], plan.offsets[1][slot])
            device = rem(lax.axis_index("rows") + offset, plan.devices)
        half, place = div(device, plan.half), rem(device, plan.half)
        share, split = div(place, OUT_SPLIT), rem(place, OUT_SPLIT)

        def codes(which):
            at = [first + which * plan.words + share * word_share for first in (low_at, high_at)]
            return [packed[half, pl.ds(aligned(first, word_share), word_share), :] for first in at]

        message = [
            *codes(0),
            packed[half, pl.ds(aligned(split * plan.outs_dev, plan.outs_dev), plan.outs_dev), :],
            packed[half, own_at : own_at + 2, :],
            lines[div(device, plan.devices // (2 * plan.leaves))],
        ]
        if plan.permuted:
            send_refs[slot][...] = jnp.concatenate(message + codes(1), axis=0).astype(bf16)
        else:
            send_refs[0][slot] = jnp.concatenate(message, axis=0).astype(bf16)


def main_kernel(plan, chunk, *refs):
    got_refs, refs = refs[: plan.parcels], refs[plan.parcels :]
    if plan.permuted:
        got_refs, refs = got_refs + tuple(refs[0].at[k] for k in range(plan.parcels)), refs[1:]
    out_refs, (weighted, gain_table, left_sums) = refs[: plan.messages], refs[plan.messages :]
    rows = plan.slots
    leaves, outs_dev, step = plan.leaves, plan.outs_dev, plan.step
    hess_at = leaves * outs_dev
    order = [feature for tile in plan.tiles for feature in tile]
    level_bins = lax.broadcasted_iota(jnp.int32, (BINS, rows), 0).astype(f32).astype(bf16)
    leaf_ids = lax.broadcasted_iota(jnp.int32, (TILE, rows), 0).astype(f32)
    zero = jnp.zeros((), bf16)
    one = jnp.ones((), bf16)

    def parcel(source):
        return got_refs[source] if plan.permuted else got_refs[0].at[source]

    def marked(source, feature):
        row = plan.code_row(feature)
        code = jnp.broadcast_to(parcel(source)[row : row + 1, :], (BINS, rows))
        return jnp.where(code <= level_bins, one, zero)

    def add_chunk(first, fresh):
        for k in range(chunk):
            source = first + k
            columns = slice(k * rows, (k + 1) * rows)
            misc = parcel(source)[plan.misc_at : plan.misc_at + 2, :].astype(f32)
            hess, node = misc[0:1], misc[1:2]
            weighted[hess_at : hess_at + TILE, columns] = jnp.where(leaf_ids == node, hess, 0.0).astype(bf16)
            node_wide = jnp.broadcast_to(node, (outs_dev, rows)).astype(bf16)
            grads = parcel(source)[plan.grad_at : plan.grad_at + outs_dev, :]
            for leaf in range(leaves):
                weighted[leaf * outs_dev : (leaf + 1) * outs_dev, columns] = jnp.where(
                    node_wide == jnp.asarray(leaf, bf16), grads, zero
                )
        for group in range(plan.share // step):
            features = order[group * step : (group + 1) * step]
            marks = jnp.concatenate(
                [
                    jnp.concatenate([marked(first + k, feature) for feature in features], axis=0)
                    for k in range(chunk)
                ],
                axis=1,
            )
            part = lax.dot_general(weighted[...], marks, NT, preferred_element_type=f32)
            span = slice(group * step * BINS, (group + 1) * step * BINS)
            if count == 1:
                add_gains(group, part)
            elif fresh:
                left_sums[:, span] = part
            else:
                left_sums[:, span] += part

    known = []

    def add_gains(group, sums):
        left = [sums[leaf * outs_dev : (leaf + 1) * outs_dev] for leaf in range(leaves)]
        hess = [sums[hess_at + leaf : hess_at + leaf + 1] for leaf in range(leaves)]
        for level in reversed(range(plan.levels - 1)):
            past = len(left) - 2 ** (level + 1)
            for n in range(past, len(left), 2):
                left.append(left[n] + left[n + 1])
                hess.append(hess[n] + hess[n + 1])
        hess = jnp.concatenate(hess, axis=0) + penalty
        if not known:
            totals = [part[:, BINS - 1 : BINS] for part in left]
            squares = jnp.concatenate([jnp.sum(t * t, axis=0, keepdims=True) for t in totals], axis=0)
            hess_total = hess[:, BINS - 1 : BINS] + penalty
            known.extend([totals, hess_total, squares / (hess_total - penalty)])
        totals, hess_total, whole_part = known
        on_left = jnp.concatenate([jnp.sum(part * part, axis=0, keepdims=True) for part in left], axis=0)
        rights = [t - part for t, part in zip(totals, left, strict=True)]
        on_right = jnp.concatenate([jnp.sum(part * part, axis=0, keepdims=True) for part in rights], axis=0)
        gains = (on_left / hess + on_right / (hess_total - hess) - whole_part) / plan.outs
        for end in range(len(plan.ends)):
            for tile in range(step // 2):
                at = group * (step // 2) + tile
                gain_table[end, at : at + 1, :] = gains[end : end + 1, tile * LANES : (tile + 1) * LANES]

    count = plan.devices // chunk
    add_chunk(0, True)
    if count > 1:
        lax.fori_loop(1, count, lambda c, _: (add_chunk(c * chunk, False), 0)[1], 0)
        for group in range(plan.share // step):
            add_gains(group, left_sums[:, group * step * BINS : (group + 1) * step * BINS])
    me = rem(lax.axis_index("rows"), plan.half)
    for slot in range(plan.half):
        place = target(me, slot, plan.half) if plan.permuted else slot
        out_ref = out_refs[slot] if plan.permuted else out_refs[0].at[slot]
        for level in range(plan.levels):
            count = plan.needed[level] // 2
            end = plan.ends.index((level, 0)) + div(place, plan.sizes[level])
            first = rem(rem(place, plan.sizes[level]) * plan.returned[level], plan.share) // 2
            if not isinstance(first, int) and count % 8 == 0:
                first = pl.multiple_of(first, 8)
            at = plan.level_at[level]
            out_ref[at : at + count, :] = gain_table[end, pl.ds(first, count), :]
        if plan.message > plan.gain_rows:
            out_ref[plan.gain_rows :, :] = jnp.zeros((plan.message - plan.gain_rows, LANES), f32)


def score_kernel(plan, *refs):
    got_refs, (score_ref, *passed) = refs[: plan.parcels], refs[plan.parcels :]
    tail = slice(plan.misc_at + 2, plan.misc_at + plan.misc_rows)
    total = jnp.zeros((plan.misc_rows - 2, plan.slots), f32)
    if plan.permuted:
        for source, ref in enumerate(got_refs):
            passed[0][source, : plan.share] = ref[plan.base_rows :, :]
            passed[0][source, plan.share :] = ref[plan.share : plan.base_rows, :]
            total = total + ref[tail, :].astype(f32)
    else:
        total = lax.fori_loop(0, plan.devices, lambda k, sums: sums + got_refs[0][k, tail, :].astype(f32), total)
    score_ref[...] = jnp.zeros_like(score_ref)
    for i in range(plan.score_rows):
        value = 0.0
        for piece in reversed(range(PIECES)):
            line, span = divmod(i * PIECES + piece, plan.spans)
            value = value + total[line : line + 1, span * LANES : (span + 1) * LANES]
        score_ref[i : i + 1, :] = value


def final_kernel(plan, *refs):
    got_refs, refs = refs[: plan.messages], refs[plan.messages :]
    score_refs, refs = refs[: -plan.levels - 1], refs[-plan.levels - 1 :]
    *gain_refs, child_ref = refs
    me = rem(lax.axis_index("rows"), plan.half)
    side = plan.block // 2
    arrived = []
    for slot in range(plan.half):
        place = source_of(me, slot, plan.half) if plan.permuted else slot
        arrived.append((div(place, OUT_SPLIT), got_refs[slot] if plan.permuted else got_refs[0].at[slot]))
    for level, gain_ref in enumerate(gain_refs):
        rows = slice(plan.level_at[level], plan.level_at[level] + plan.needed[level] // 2)
        first = div(rem(me, plan.sizes[level]) * plan.returned[level], plan.share)
        for turn in range(plan.returned[level] // plan.needed[level]):
            value = 0.0
            for share, ref in arrived:
                value = value + jnp.where(share == first + turn, ref[rows, :], 0.0)
            for start in range(0, plan.needed[level], plan.block):
                part = value[start // 2 : start // 2 + side]
                at = turn * plan.share + start
                gain_ref[at : at + side, :] = part[:, :BINS]
                gain_ref[at + side : at + 2 * side, :] = part[:, BINS:]
    sums = score_refs[0][...]
    for score_ref in score_refs[1:]:
        sums = sums + score_ref[...]
    curv = sums[2 * plan.levels : 2 * plan.levels + 1, :]
    for level in range(plan.levels):
        for side in range(2):
            line = side * plan.levels + level
            scale = jnp.sqrt(curv[:, line : line + 1] + penalty)
            child_ref[level, 0, side : side + 1, :] = -sums[line : line + 1, :] / scale


def flipped(block, bits):
    count = lax.axis_size("feat")
    return lax.ppermute(block, "feat", [(p, p ^ bits) for p in range(count)])


def on_device(gradients, hessians, bin_words, children, split_feature, split_bin):
    plan = Plan(lax.axis_size("rows"), lax.axis_size("feat"), gradients, bin_words, children)
    params = pltpu.CompilerParams(vmem_limit_bytes=VMEM_BYTES)

    inputs = (gradients, hessians, children, split_feature, split_bin, bin_words)
    crossed = [flipped(bin_words, 1)] if plan.permuted else []
    row_dev, table_rows = plan.row_dev, plan.outs + plan.codes + TILE
    grads, words, row_values, picks, chosen = pl.pallas_call(
        functools.partial(fetch_kernel, plan),
        out_shape=(
            jax.ShapeDtypeStruct(gradients.shape, bf16),
            jax.ShapeDtypeStruct(bin_words.shape, jnp.int32),
            jax.ShapeDtypeStruct((8, row_dev), f32),
            jax.ShapeDtypeStruct((3, plan.split_rows, plan.codes), f32),
            jax.ShapeDtypeStruct((2, plan.slots, row_dev), bf16),
        ),
        in_specs=[pl.BlockSpec(memory_space=pltpu.HBM)] * len(inputs),
        out_specs=[whole()] * 5,
        scratch_shapes=[
            pltpu.VMEM(hessians.shape, bf16),
            pltpu.VMEM(children.shape, jnp.int32),
            pltpu.SMEM(split_feature.shape, jnp.int32),
            pltpu.SMEM(split_bin.shape, jnp.int32),
            pltpu.SemaphoreType.DMA((len(inputs),)),
        ],
        cost_estimate=pl.CostEstimate(flops=10**9, bytes_accessed=10**6, transcendentals=0),
        compiler_params=params,
        name="fetch",
    )(*(pltpu.with_memory_space_constraint(a, pltpu.HBM) for a in inputs))
    parcel = (plan.sent_rows, plan.slots) if plan.permuted else (plan.devices, plan.sent_rows, plan.slots)
    parcels = pl.pallas_call(
        functools.partial(prep_kernel, plan),
        out_shape=[jax.ShapeDtypeStruct(parcel, bf16)] * plan.parcels,
        in_specs=[whole()] * (4 + plan.panels),
        out_specs=[whole()] * plan.parcels,
        scratch_shapes=[
            pltpu.VMEM((table_rows, row_dev), bf16),
            pltpu.VMEM((2, table_rows, plan.slots), f32),
            pltpu.VMEM((2 * plan.leaves, plan.base_rows - plan.misc_at - 2, plan.slots), f32),
            pltpu.VMEM((2 * plan.split_rows, row_dev), f32),
        ],
        compiler_params=params,
        name="prep",
    )(grads, row_values, picks, chosen, words, *crossed)

    if plan.permuted:
        got = spread(parcels, plan)
    else:
        got = [lax.all_to_all(parcels[0], "rows", 0, 0)]
    shapes = [jax.ShapeDtypeStruct((8, plan.outs), f32)]
    if plan.permuted:
        shapes.append(jax.ShapeDtypeStruct((plan.parcels, plan.base_rows, plan.slots), bf16))
    scores, *passed = pl.pallas_call(
        functools.partial(score_kernel, plan),
        out_shape=shapes,
        in_specs=[whole()] * plan.parcels,
        out_specs=[whole()] * len(shapes),
        compiler_params=params,
        name="scores",
    )(*got)
    arrays = got + [flipped(block, 1) for block in passed]
    far = [flipped(scores, away) for away in range(plan.panels, lax.axis_size("feat"), plan.panels)]

    chunk = max(1, min(plan.devices, 4096 // plan.slots))
    while plan.devices % chunk:
        chunk -= 1
    sums_rows = plan.leaves * plan.outs_dev + TILE
    block = (plan.message, LANES) if plan.permuted else (plan.half, plan.message, LANES)
    messages = pl.pallas_call(
        functools.partial(main_kernel, plan, chunk),
        out_shape=[jax.ShapeDtypeStruct(block, f32)] * plan.messages,
        in_specs=[whole()] * len(arrays),
        out_specs=[whole()] * plan.messages,
        scratch_shapes=[
            pltpu.VMEM((sums_rows, chunk * plan.slots), bf16),
            pltpu.VMEM((len(plan.ends), plan.share // 2, LANES), f32),
            pltpu.VMEM((sums_rows, plan.share * BINS), f32),
        ],
        cost_estimate=pl.CostEstimate(
            flops=2 * sums_rows * plan.devices * plan.slots * plan.share * BINS,
            bytes_accessed=4 * plan.devices * plan.sent_rows * plan.slots,
            transcendentals=0,
        ),
        compiler_params=params,
        name="gains",
    )(*arrays)

    messages, far = lax.optimization_barrier((list(messages), far))
    scores = sum(far, scores)
    score_parts = [scores] + ([flipped(scores, 1)] if plan.permuted else [])
    if plan.permuted:
        messages = exchanged(messages, plan.half, plan.devices)
    else:
        halves = [list(range(plan.half)), list(range(plan.half, plan.devices))]
        messages = [lax.all_to_all(messages[0], "rows", 0, 0, axis_index_groups=halves)]
    shapes = [
        jax.ShapeDtypeStruct((count, BINS), f32) for count in plan.returned
    ]
    shapes.append(jax.ShapeDtypeStruct((plan.levels, 1, 2, plan.outs), f32))
    return pl.pallas_call(
        functools.partial(final_kernel, plan),
        out_shape=tuple(shapes),
        in_specs=[whole()] * (plan.messages + len(score_parts)),
        out_specs=tuple(whole() for _ in shapes),
        compiler_params=params,
        name="finish",
    )(*messages, *score_parts)


def solution(mesh):
    placed = (P("rows", None), P("rows"), P("feat", "rows"), P(None, "rows"), P(), P())
    return jax.shard_map(
        on_device,
        mesh=mesh,
        in_specs=placed,
        out_specs=(
            P("rows", "feat"),
            P("rows", "feat"),
            P("rows", "feat"),
            P(None, "rows", None, None),
        ),
        check_vma=False,
    )
```

```python
import functools

import jax
import jax.numpy as jnp
from jax import lax
from jax.experimental import pallas as pl
from jax.experimental.pallas import tpu as pltpu
from jax.sharding import PartitionSpec as P

BINS = 64
LANES = 128
TILE = 16
OUT_SPLIT = 2
PIECES = 2
penalty = 1.0
VMEM_BYTES = 32 * 2**20

bf16 = jnp.bfloat16
f32 = jnp.float32
NT = (((1,), (1,)), ((), ()))
PERMUTED = 8


def div(value, by):
    return value // by if isinstance(value, int) else lax.div(value, jnp.int32(by))


def rem(value, by):
    return value % by if isinstance(value, int) else lax.rem(value, jnp.int32(by))


def round_up(value, unit):
    return -(-value // unit) * unit


def whole(*_):
    return pl.BlockSpec(memory_space=pltpu.VMEM)


def aligned(value, unit):
    return value if isinstance(value, int) or unit % 8 else pl.multiple_of(value, 8)


def target(me, slot, count):
    return rem(me + slot, count)


def source_of(me, slot, count):
    return rem(me + (count - slot), count)


def exchanged(blocks, group, count):
    moved = [blocks[0]]
    for slot in range(1, group):
        route = [(p, p - p % group + (p + slot) % group) for p in range(count)]
        moved.append(lax.ppermute(blocks[slot], "rows", route))
    return moved


def spread(parcels, plan):
    feat_axis = lax.axis_size("feat")
    moved = []
    for slot, block in enumerate(parcels):
        route = []
        for p in range(plan.devices * feat_axis):
            row, panel = divmod(p, feat_axis)
            row = (row + plan.offsets[panel % 2][slot]) % plan.devices
            route.append((p, row * feat_axis + panel))
        moved.append(lax.ppermute(block, ("rows", "feat"), route))
    return moved


class Plan:
    def __init__(self, rows_axis, feat_axis, gradients, bin_words, children):
        self.devices = rows_axis
        self.half = rows_axis // 2
        self.row_dev, self.outs = gradients.shape
        self.words = bin_words.shape[0]
        self.feats = 2 * self.words
        self.levels = children.shape[0]
        self.leaves = 2 ** (self.levels - 1)
        self.slots = round_up(self.row_dev * 3 // 4, LANES)
        self.shares = self.half // OUT_SPLIT
        self.share = self.feats // self.shares
        self.outs_dev = self.outs // OUT_SPLIT
        self.permuted = rows_axis <= PERMUTED and feat_axis % 2 == 0
        self.panels = 2 if self.permuted else 1
        self.parcels = rows_axis // 2 if self.permuted else 1
        self.offsets = [
            sorted(range(first, rows_axis, 2), key=lambda k: (abs(k - rows_axis // 2), k)) for first in range(2)
        ]
        self.codes = self.panels * self.feats
        self.splits = 2 ** (self.levels + 1) - 2
        self.split_rows = round_up(self.splits, TILE)
        self.grad_at = self.share
        self.misc_at = self.share + self.outs_dev
        self.score_rows = 2 * self.levels + 1
        self.spans = self.slots // LANES
        self.misc_rows = 2 + -(-self.score_rows * PIECES // self.spans)
        self.base_rows = round_up(self.misc_at + self.misc_rows, 8)
        self.sent_rows = self.base_rows + (self.panels - 1) * self.share
        self.sizes = [self.devices >> (level + 1) for level in range(self.levels)]
        self.returned = [self.feats // size for size in self.sizes]
        self.needed = [min(self.share, count) for count in self.returned]
        self.block = min(self.needed)
        self.step = min(16, self.share)
        self.tiles = [
            (start + k, start + k + self.block // 2)
            for start in range(0, self.share, self.block)
            for k in range(self.block // 2)
        ]
        self.level_at = [sum(self.needed[:level]) // 2 for level in range(self.levels)]
        self.gain_rows = sum(self.needed) // 2
        self.message = round_up(self.gain_rows, 8)
        self.ends = [(level, n) for level in reversed(range(self.levels)) for n in range(2**level)]
        self.messages = self.half if self.permuted else 1

    def code_row(self, feature):
        return feature // 2 + (feature % 2) * (self.share // 2)


def split_words(words):
    codes = (jnp.bitwise_and(words, 63), jnp.bitwise_and(jnp.right_shift(words, 6), 63))
    return jnp.concatenate(codes, axis=0).astype(f32).astype(bf16)


def fetch_kernel(plan, *refs):
    inputs, refs = refs[:6], refs[6:]
    (grad_ref, word_ref, row_ref, pick_ref, chosen_ref, packed_ref), refs = refs[:6], refs[6:]
    hess_ref, child_ref, feature_ref, bin_ref, table, sems = refs
    targets = (grad_ref, hess_ref, child_ref, feature_ref, bin_ref, word_ref)
    copies = [
        pltpu.make_async_copy(source, into, sems.at[i])
        for i, (source, into) in enumerate(zip(inputs, targets, strict=True))
    ]
    for copy in copies:
        copy.start()
    rows = plan.row_dev
    ahead = jnp.where(
        lax.broadcasted_iota(jnp.int32, (rows, rows), 0) <= lax.broadcasted_iota(jnp.int32, (rows, rows), 1), 1.0, 0.0
    ).astype(bf16)
    for copy in copies:
        copy.wait()

    nodes = [child_ref[0:1, :]]
    for level in range(1, plan.levels):
        nodes.append(nodes[-1] * 2 + child_ref[level : level + 1, :])
    row_ref[...] = jnp.zeros_like(row_ref)
    row_ref[0:1, :] = hess_ref[...].astype(f32).reshape(1, rows)
    for level, node in enumerate(nodes):
        row_ref[level + 1 : level + 2, :] = node.astype(f32)

    at = lax.broadcasted_iota(jnp.int32, (TILE, rows), 0)
    side = jnp.where(at == nodes[0], 1.0, 0.0)
    rank = jnp.dot(side.astype(bf16), ahead, preferred_element_type=f32)
    slot = jnp.where(side > 0.0, rank - 1.0, -1.0)
    slot_ids = lax.broadcasted_iota(jnp.int32, (plan.slots, rows), 0).astype(f32)
    for half in range(2):
        chosen_ref[half] = jnp.where(slot_ids == slot[half : half + 1], 1.0, 0.0).astype(bf16)

    turn = jnp.where(
        lax.broadcasted_iota(jnp.int32, (plan.outs, plan.outs), 0)
        == lax.broadcasted_iota(jnp.int32, (plan.outs, plan.outs), 1),
        1.0,
        0.0,
    ).astype(bf16)
    own_at = plan.outs + plan.feats
    table[: plan.outs] = lax.dot_general(turn, grad_ref[...], NT, preferred_element_type=f32).astype(bf16)
    table[plan.outs : own_at] = split_words(word_ref[...])
    leaf = jnp.bitwise_and(nodes[-1], plan.leaves - 1).astype(f32)
    table[own_at:] = jnp.where(at == 0, row_ref[0:1, :], jnp.where(at == 1, leaf, 0.0)).astype(bf16)
    for half in range(2):
        packed_ref[half] = lax.dot_general(table[...], chosen_ref[half], NT, preferred_element_type=f32)

    panel = lax.axis_index("feat")
    lane = lax.broadcasted_iota(jnp.int32, (1, plan.codes), 1)
    pick_ref[...] = jnp.zeros_like(pick_ref)
    for slot in range(plan.splits):
        feature = feature_ref[slot]
        owner = lax.div(feature, jnp.int32(plan.feats))
        inner = feature - owner * plan.feats
        held = jnp.bitwise_xor(owner, panel)
        place = held * plan.feats + inner // 2 + lax.rem(inner, 2) * plan.words
        place = jnp.where(held < plan.panels, place, plan.codes)
        pick_ref[0, slot : slot + 1, :] = jnp.where(lane == place, 1.0, 0.0)
        pick_ref[1, slot : slot + 1, :] = jnp.full((1, plan.codes), bin_ref[slot].astype(f32))
        pick_ref[2, slot : slot + 1, :] = jnp.full((1, plan.codes), jnp.where(held < plan.panels, 1.0, 0.0))


def prep_kernel(plan, *refs):
    (grad_ref, row_ref, pick_ref, chosen_ref, own_ref), refs = refs[:5], refs[5:]
    word_refs, send_refs = refs[: plan.panels], refs[plan.panels : plan.panels + plan.parcels]
    table, packed, lines, marked = refs[plan.panels + plan.parcels :]
    own_at = plan.outs + plan.feats
    grads = grad_ref[...]
    hess = row_ref[0:1, :]
    nodes = [row_ref[level + 1 : level + 2, :] for level in range(plan.levels)]

    for which, word_ref in enumerate(word_refs):
        table[which * plan.feats : (which + 1) * plan.feats] = split_words(word_ref[...])
    if plan.panels > 1:
        for half in range(2):
            packed[half] = lax.dot_general(table[plan.feats :], chosen_ref[half], NT, preferred_element_type=f32)

    ends = [(level, node) for level in range(plan.levels) for node in range(2 ** (level + 1))]
    code = jnp.dot(pick_ref[0].astype(bf16), table[...], preferred_element_type=f32)
    marked[...] = jnp.zeros_like(marked)
    for slot, (level, node) in enumerate(ends):
        here = jnp.where(nodes[level] == node, pick_ref[2, slot : slot + 1, 0:1], 0.0)
        left = jnp.where(code[slot : slot + 1] <= pick_ref[1, slot : slot + 1, 0:1], here, 0.0)
        marked[slot : slot + 1, :] = left
        marked[plan.split_rows + slot : plan.split_rows + slot + 1, :] = here - left
    mark = marked[...]
    sums = jnp.dot(mark.astype(bf16), grads, preferred_element_type=f32)
    curv = jnp.sum(mark * hess, axis=1, keepdims=True)
    shape = (2 * plan.split_rows, plan.outs)
    curv = jnp.broadcast_to(curv, shape)
    lane = lax.broadcasted_iota(jnp.int32, (1, plan.outs), 1)
    blank = jnp.zeros((1, LANES), f32)
    filler = jnp.zeros((plan.base_rows - plan.misc_at - plan.misc_rows, plan.slots), f32)
    for leaf in range(2 * plan.leaves):
        places = [
            side * plan.split_rows + 2 ** (level + 1) - 2 + (leaf >> (plan.levels - 1 - level))
            for side in range(2)
            for level in range(plan.levels)
        ]
        spread_curv = jnp.zeros((1, plan.outs), f32)
        for i, at in enumerate(places):
            spread_curv = jnp.where(lane == i, curv[at : at + 1], spread_curv)
        parts = []
        for value in [*(sums[at : at + 1] for at in places), spread_curv]:
            for _ in range(PIECES):
                parts.append(value.astype(bf16).astype(f32))
                value = value - parts[-1]
        parts += [blank] * (-len(parts) % plan.spans)
        parts = [jnp.concatenate(parts[i : i + plan.spans], axis=1) for i in range(0, len(parts), plan.spans)]
        lines[leaf] = jnp.concatenate(parts + ([filler] if filler.shape[0] else []), axis=0)

    word_share = plan.share // 2
    parity = rem(lax.axis_index("feat"), plan.panels)
    for slot in range(plan.parcels if plan.permuted else plan.devices):
        device = slot
        if plan.permuted:
            offset = jnp.where(parity == 0, plan.offsets[0][slot], plan.offsets[1][slot])
            device = rem(lax.axis_index("rows") + offset, plan.devices)
        half, place = div(device, plan.half), rem(device, plan.half)
        share, split = div(place, OUT_SPLIT), rem(place, OUT_SPLIT)

        def codes(ref, first):
            at = [first + odd * plan.words + share * word_share for odd in range(2)]
            return [ref[half, pl.ds(aligned(k, word_share), word_share), :] for k in at]

        message = [
            *codes(own_ref, plan.outs),
            own_ref[half, pl.ds(aligned(split * plan.outs_dev, plan.outs_dev), plan.outs_dev), :],
            own_ref[half, own_at : own_at + 2, :],
            lines[div(device, plan.devices // (2 * plan.leaves))],
        ]
        if plan.permuted:
            send_refs[slot][...] = jnp.concatenate(message + codes(packed, 0), axis=0).astype(bf16)
        else:
            send_refs[0][slot] = jnp.concatenate(message, axis=0).astype(bf16)


def main_kernel(plan, chunk, *refs):
    got_refs, refs = refs[: plan.parcels], refs[plan.parcels :]
    if plan.permuted:
        got_refs, refs = got_refs + tuple(refs[0].at[k] for k in range(plan.parcels)), refs[1:]
    out_refs, (weighted, gain_table, left_sums) = refs[: plan.messages], refs[plan.messages :]
    rows = plan.slots
    leaves, outs_dev, step = plan.leaves, plan.outs_dev, plan.step
    hess_at = leaves * outs_dev
    order = [feature for tile in plan.tiles for feature in tile]
    level_bins = lax.broadcasted_iota(jnp.int32, (BINS, rows), 0).astype(f32).astype(bf16)
    leaf_ids = lax.broadcasted_iota(jnp.int32, (TILE, rows), 0).astype(f32)
    zero = jnp.zeros((), bf16)
    one = jnp.ones((), bf16)

    def parcel(source):
        return got_refs[source] if plan.permuted else got_refs[0].at[source]

    def marked(source, feature):
        row = plan.code_row(feature)
        code = jnp.broadcast_to(parcel(source)[row : row + 1, :], (BINS, rows))
        return jnp.where(code <= level_bins, one, zero)

    def add_chunk(first, fresh):
        for k in range(chunk):
            source = first + k
            columns = slice(k * rows, (k + 1) * rows)
            misc = parcel(source)[plan.misc_at : plan.misc_at + 2, :].astype(f32)
            hess, node = misc[0:1], misc[1:2]
            weighted[hess_at : hess_at + TILE, columns] = jnp.where(leaf_ids == node, hess, 0.0).astype(bf16)
            node_wide = jnp.broadcast_to(node, (outs_dev, rows)).astype(bf16)
            grads = parcel(source)[plan.grad_at : plan.grad_at + outs_dev, :]
            for leaf in range(leaves):
                weighted[leaf * outs_dev : (leaf + 1) * outs_dev, columns] = jnp.where(
                    node_wide == jnp.asarray(leaf, bf16), grads, zero
                )
        for group in range(plan.share // step):
            features = order[group * step : (group + 1) * step]
            marks = jnp.concatenate(
                [
                    jnp.concatenate([marked(first + k, feature) for feature in features], axis=0)
                    for k in range(chunk)
                ],
                axis=1,
            )
            part = lax.dot_general(weighted[...], marks, NT, preferred_element_type=f32)
            span = slice(group * step * BINS, (group + 1) * step * BINS)
            if count == 1:
                add_gains(group, part)
            elif fresh:
                left_sums[:, span] = part
            else:
                left_sums[:, span] += part

    known = []

    def add_gains(group, sums):
        left = [sums[leaf * outs_dev : (leaf + 1) * outs_dev] for leaf in range(leaves)]
        hess = [sums[hess_at + leaf : hess_at + leaf + 1] for leaf in range(leaves)]
        for level in reversed(range(plan.levels - 1)):
            past = len(left) - 2 ** (level + 1)
            for n in range(past, len(left), 2):
                left.append(left[n] + left[n + 1])
                hess.append(hess[n] + hess[n + 1])
        hess = jnp.concatenate(hess, axis=0) + penalty
        if not known:
            totals = [part[:, BINS - 1 : BINS] for part in left]
            squares = jnp.concatenate([jnp.sum(t * t, axis=0, keepdims=True) for t in totals], axis=0)
            hess_total = hess[:, BINS - 1 : BINS] + penalty
            known.extend([totals, hess_total, squares / (hess_total - penalty)])
        totals, hess_total, whole_part = known
        on_left = jnp.concatenate([jnp.sum(part * part, axis=0, keepdims=True) for part in left], axis=0)
        rights = [t - part for t, part in zip(totals, left, strict=True)]
        on_right = jnp.concatenate([jnp.sum(part * part, axis=0, keepdims=True) for part in rights], axis=0)
        gains = (on_left / hess + on_right / (hess_total - hess) - whole_part) / plan.outs
        for end in range(len(plan.ends)):
            for tile in range(step // 2):
                at = group * (step // 2) + tile
                gain_table[end, at : at + 1, :] = gains[end : end + 1, tile * LANES : (tile + 1) * LANES]

    count = plan.devices // chunk
    add_chunk(0, True)
    if count > 1:
        lax.fori_loop(1, count, lambda c, _: (add_chunk(c * chunk, False), 0)[1], 0)
        for group in range(plan.share // step):
            add_gains(group, left_sums[:, group * step * BINS : (group + 1) * step * BINS])
    me = rem(lax.axis_index("rows"), plan.half)
    for slot in range(plan.half):
        place = target(me, slot, plan.half) if plan.permuted else slot
        out_ref = out_refs[slot] if plan.permuted else out_refs[0].at[slot]
        for level in range(plan.levels):
            count = plan.needed[level] // 2
            end = plan.ends.index((level, 0)) + div(place, plan.sizes[level])
            first = rem(rem(place, plan.sizes[level]) * plan.returned[level], plan.share) // 2
            if not isinstance(first, int) and count % 8 == 0:
                first = pl.multiple_of(first, 8)
            at = plan.level_at[level]
            out_ref[at : at + count, :] = gain_table[end, pl.ds(first, count), :]
        if plan.message > plan.gain_rows:
            out_ref[plan.gain_rows :, :] = jnp.zeros((plan.message - plan.gain_rows, LANES), f32)


def score_kernel(plan, *refs):
    got_refs, (score_ref, *passed) = refs[: plan.parcels], refs[plan.parcels :]
    tail = slice(plan.misc_at + 2, plan.misc_at + plan.misc_rows)
    total = jnp.zeros((plan.misc_rows - 2, plan.slots), f32)
    if plan.permuted:
        for source, ref in enumerate(got_refs):
            passed[0][source, : plan.share] = ref[plan.base_rows :, :]
            passed[0][source, plan.share :] = ref[plan.share : plan.base_rows, :]
            total = total + ref[tail, :].astype(f32)
    else:
        total = lax.fori_loop(0, plan.devices, lambda k, sums: sums + got_refs[0][k, tail, :].astype(f32), total)
    score_ref[...] = jnp.zeros_like(score_ref)
    for i in range(plan.score_rows):
        value = 0.0
        for piece in reversed(range(PIECES)):
            line, span = divmod(i * PIECES + piece, plan.spans)
            value = value + total[line : line + 1, span * LANES : (span + 1) * LANES]
        score_ref[i : i + 1, :] = value


def final_kernel(plan, *refs):
    got_refs, refs = refs[: plan.messages], refs[plan.messages :]
    score_refs, refs = refs[: -plan.levels - 1], refs[-plan.levels - 1 :]
    *gain_refs, child_ref = refs
    me = rem(lax.axis_index("rows"), plan.half)
    side = plan.block // 2
    arrived = []
    for slot in range(plan.half):
        place = source_of(me, slot, plan.half) if plan.permuted else slot
        arrived.append((div(place, OUT_SPLIT), got_refs[slot] if plan.permuted else got_refs[0].at[slot]))
    for level, gain_ref in enumerate(gain_refs):
        rows = slice(plan.level_at[level], plan.level_at[level] + plan.needed[level] // 2)
        first = div(rem(me, plan.sizes[level]) * plan.returned[level], plan.share)
        for turn in range(plan.returned[level] // plan.needed[level]):
            value = 0.0
            for share, ref in arrived:
                value = value + jnp.where(share == first + turn, ref[rows, :], 0.0)
            for start in range(0, plan.needed[level], plan.block):
                part = value[start // 2 : start // 2 + side]
                at = turn * plan.share + start
                gain_ref[at : at + side, :] = part[:, :BINS]
                gain_ref[at + side : at + 2 * side, :] = part[:, BINS:]
    sums = score_refs[0][...]
    for score_ref in score_refs[1:]:
        sums = sums + score_ref[...]
    curv = sums[2 * plan.levels : 2 * plan.levels + 1, :]
    for level in range(plan.levels):
        for side in range(2):
            line = side * plan.levels + level
            scale = jnp.sqrt(curv[:, line : line + 1] + penalty)
            child_ref[level, 0, side : side + 1, :] = -sums[line : line + 1, :] / scale


def flipped(block, bits):
    count = lax.axis_size("feat")
    return lax.ppermute(block, "feat", [(p, p ^ bits) for p in range(count)])


def on_device(gradients, hessians, bin_words, children, split_feature, split_bin):
    plan = Plan(lax.axis_size("rows"), lax.axis_size("feat"), gradients, bin_words, children)
    params = pltpu.CompilerParams(vmem_limit_bytes=VMEM_BYTES)

    inputs = (gradients, hessians, children, split_feature, split_bin, bin_words)
    crossed = [flipped(bin_words, 1)] if plan.permuted else []
    row_dev, table_rows = plan.row_dev, plan.outs + plan.feats + TILE
    grads, words, row_values, picks, chosen, own_part = pl.pallas_call(
        functools.partial(fetch_kernel, plan),
        out_shape=(
            jax.ShapeDtypeStruct(gradients.shape, bf16),
            jax.ShapeDtypeStruct(bin_words.shape, jnp.int32),
            jax.ShapeDtypeStruct((8, row_dev), f32),
            jax.ShapeDtypeStruct((3, plan.split_rows, plan.codes), f32),
            jax.ShapeDtypeStruct((2, plan.slots, row_dev), bf16),
            jax.ShapeDtypeStruct((2, table_rows, plan.slots), f32),
        ),
        in_specs=[pl.BlockSpec(memory_space=pltpu.HBM)] * len(inputs),
        out_specs=[whole()] * 6,
        scratch_shapes=[
            pltpu.VMEM(hessians.shape, bf16),
            pltpu.VMEM(children.shape, jnp.int32),
            pltpu.SMEM(split_feature.shape, jnp.int32),
            pltpu.SMEM(split_bin.shape, jnp.int32),
            pltpu.VMEM((table_rows, row_dev), bf16),
            pltpu.SemaphoreType.DMA((len(inputs),)),
        ],
        cost_estimate=pl.CostEstimate(flops=10**9, bytes_accessed=10**6, transcendentals=0),
        compiler_params=params,
        name="fetch",
    )(*(pltpu.with_memory_space_constraint(a, pltpu.HBM) for a in inputs))
    parcel = (plan.sent_rows, plan.slots) if plan.permuted else (plan.devices, plan.sent_rows, plan.slots)
    parcels = pl.pallas_call(
        functools.partial(prep_kernel, plan),
        out_shape=[jax.ShapeDtypeStruct(parcel, bf16)] * plan.parcels,
        in_specs=[whole()] * (5 + plan.panels),
        out_specs=[whole()] * plan.parcels,
        scratch_shapes=[
            pltpu.VMEM((plan.codes, row_dev), bf16),
            pltpu.VMEM((2, plan.feats, plan.slots), f32),
            pltpu.VMEM((2 * plan.leaves, plan.base_rows - plan.misc_at - 2, plan.slots), f32),
            pltpu.VMEM((2 * plan.split_rows, row_dev), f32),
        ],
        compiler_params=params,
        name="prep",
    )(grads, row_values, picks, chosen, own_part, words, *crossed)

    if plan.permuted:
        got = spread(parcels, plan)
    else:
        got = [lax.all_to_all(parcels[0], "rows", 0, 0)]
    shapes = [jax.ShapeDtypeStruct((8, plan.outs), f32)]
    if plan.permuted:
        shapes.append(jax.ShapeDtypeStruct((plan.parcels, plan.base_rows, plan.slots), bf16))
    scores, *passed = pl.pallas_call(
        functools.partial(score_kernel, plan),
        out_shape=shapes,
        in_specs=[whole()] * plan.parcels,
        out_specs=[whole()] * len(shapes),
        compiler_params=params,
        name="scores",
    )(*got)
    arrays = got + [flipped(block, 1) for block in passed]
    far = [flipped(scores, away) for away in range(plan.panels, lax.axis_size("feat"), plan.panels)]

    chunk = max(1, min(plan.devices, 4096 // plan.slots))
    while plan.devices % chunk:
        chunk -= 1
    sums_rows = plan.leaves * plan.outs_dev + TILE
    block = (plan.message, LANES) if plan.permuted else (plan.half, plan.message, LANES)
    messages = pl.pallas_call(
        functools.partial(main_kernel, plan, chunk),
        out_shape=[jax.ShapeDtypeStruct(block, f32)] * plan.messages,
        in_specs=[whole()] * len(arrays),
        out_specs=[whole()] * plan.messages,
        scratch_shapes=[
            pltpu.VMEM((sums_rows, chunk * plan.slots), bf16),
            pltpu.VMEM((len(plan.ends), plan.share // 2, LANES), f32),
            pltpu.VMEM((sums_rows, plan.share * BINS), f32),
        ],
        cost_estimate=pl.CostEstimate(
            flops=2 * sums_rows * plan.devices * plan.slots * plan.share * BINS,
            bytes_accessed=4 * plan.devices * plan.sent_rows * plan.slots,
            transcendentals=0,
        ),
        compiler_params=params,
        name="gains",
    )(*arrays)

    messages, far = lax.optimization_barrier((list(messages), far))
    scores = sum(far, scores)
    score_parts = [scores] + ([flipped(scores, 1)] if plan.permuted else [])
    if plan.permuted:
        messages = exchanged(messages, plan.half, plan.devices)
    else:
        halves = [list(range(plan.half)), list(range(plan.half, plan.devices))]
        messages = [lax.all_to_all(messages[0], "rows", 0, 0, axis_index_groups=halves)]
    shapes = [
        jax.ShapeDtypeStruct((count, BINS), f32) for count in plan.returned
    ]
    shapes.append(jax.ShapeDtypeStruct((plan.levels, 1, 2, plan.outs), f32))
    return pl.pallas_call(
        functools.partial(final_kernel, plan),
        out_shape=tuple(shapes),
        in_specs=[whole()] * (plan.messages + len(score_parts)),
        out_specs=tuple(whole() for _ in shapes),
        compiler_params=params,
        name="finish",
    )(*messages, *score_parts)


def solution(mesh):
    placed = (P("rows", None), P("rows"), P("feat", "rows"), P(None, "rows"), P(), P())
    return jax.shard_map(
        on_device,
        mesh=mesh,
        in_specs=placed,
        out_specs=(
            P("rows", "feat"),
            P("rows", "feat"),
            P("rows", "feat"),
            P(None, "rows", None, None),
        ),
        check_vma=False,
    )
```
